32 devices in a mesh: chan: 2 (over x), row: 16 (over z, y, core).
Axes of the slice: x: 2, y: 2, z: 4, core: 2. Of those that a mesh axis runs over, the one named last changes fastest.
Arguments:
- inputs: bfloat16 [1, 192, 448, 1024], P(None, 'row', None, 'chan'), may hold values from -6 to 6
- cotangent: bfloat16 [1, 192, 448, 1024], P(None, 'row', None, 'chan'), may hold values from -6 to 6
- ln_gain: float32 [1024], P('chan'), may hold values from 0.1 to 1.9
- ln_shift: float32 [1024], P('chan'), may hold values from -3 to 3
- first_weight: bfloat16 [2, 1024, 128], P(None, 'chan'), may hold values from -0.375 to 0.375
- first_bias: float32 [2, 1024], P(None, 'chan'), may hold values from -3 to 3
- second_weight: bfloat16 [2, 1024, 128], P(None, 'chan'), may hold values from -0.375 to 0.375
- second_bias: float32 [2, 1024], P(None, 'chan'), may hold values from -3 to 3
Outputs:
- input_grad: bfloat16 [1, 192, 448, 1024], P(None, 'row', None, 'chan')
- first_weight_grad: float32 [2, 1024, 128], P(None, 'chan')
- first_bias_grad: float32 [2, 1024], P(None, 'chan')
- second_weight_grad: float32 [2, 1024, 128], P(None, 'chan')
- second_bias_grad: float32 [2, 1024], P(None, 'chan')
- gain_grad: float32 [1024], P('chan')
- shift_grad: float32 [1024], P('chan')
The draws below stay inside these ranges and needn't reach their ends.
All inputs are finite; a program needn't handle non-finite values.
Results may differ from the reference program's by a relative error of at most 0.03.
The reference program's roundings to bfloat16 on the way count: a program that leaves them out, or rounds other values in their place, can miss the bound.
Values sent between devices are 32-bit elements; how exact they have to be, the bound alone decides.
No kernel may reach another device: no remote copies, remote signals or barrier semaphores. Data moves between devices by JAX's collectives and lax.ppermute only.
A program may use at most 128 MiB of HBM per device.

```python
import math
import jax
import jax.numpy as jnp
from jax import lax

BATCH = 1
H = 192
W = 448
K = 192
NB = 8
BS = 128
C = 1024


def levels(own_key, extent, pieces, low, high):
    def one(dim, blocks):
        steps = jax.random.uniform(jax.random.fold_in(jax.random.fold_in(own_key, 6), dim), (blocks,), jnp.float32, low / len(pieces), high / len(pieces))
        return jnp.repeat(jnp.exp(steps), extent[dim] // blocks).reshape((-1,) + (1,) * (len(extent) - dim - 1))

    loudness = one(*pieces[0])
    for cut in pieces[1:]:
        loudness = loudness * one(*cut)
    return loudness


def bell_draw(rng, dims, scale, reach, shards=(), kind=jnp.bfloat16):
    array = scale * jax.random.normal(rng, dims, jnp.float32)
    if shards:
        array = array * levels(rng, dims, shards, -0.22, 0.18)
    return jnp.clip(array, -reach, reach).astype(kind)


def setup_inputs(seed: int = 0) -> dict:
    key_of = jax.random.split(jax.random.key(seed), 9)
    inputs = bell_draw(key_of[0], (BATCH, H, W, C), 1.0, 6.0, ((1, 16), (3, 2)))
    cotangent = bell_draw(key_of[1], (BATCH, H, W, C), 1.0, 6.0, ((1, 16), (3, 2)))
    ln_gain = jnp.clip(1.0 + 0.18 * jax.random.normal(key_of[2], (C,), jnp.float32), 0.1, 1.9)
    ln_shift = bell_draw(key_of[3], (C,), 0.5, 3.0, ((0, 2),), jnp.float32)
    first_weight = bell_draw(key_of[4], (2, C, BS), (2 * BS) ** -0.5, 0.375, ((1, 2),))
    first_bias = bell_draw(key_of[5], (2, C), 0.5, 3.0, ((1, 2),), jnp.float32)
    second_weight = bell_draw(key_of[6], (2, C, BS), (2 * BS) ** -0.5, 0.375, ((1, 2),))
    second_bias = bell_draw(key_of[7], (2, C), 0.5, 3.0, ((1, 2),), jnp.float32)
    return {"inputs": inputs, "cotangent": cotangent, "ln_gain": ln_gain, "ln_shift": ln_shift, "first_weight": first_weight, "first_bias": first_bias, "second_weight": second_weight, "second_bias": second_bias}


EPS = 1e-05
LAMBDA = 0.01
ROOT_TWO_PI = math.sqrt(2.0 / math.pi)

def gelu_parts(values):
    inner = ROOT_TWO_PI * (values + 0.044715 * values * values * values)
    tangent = jnp.tanh(inner)
    output = 0.5 * values * (1.0 + tangent)
    slope = 0.5 * (1.0 + tangent) + 0.5 * values * (1.0 - tangent * tangent) * ROOT_TWO_PI * (1.0 + 3.0 * 0.044715 * values * values)
    return (output, slope)

def shrink_slope(values):
    tangent = jnp.tanh(values / LAMBDA)
    return tangent * tangent

def mult(left, right):
    return jnp.einsum('gkni,nio->gkno', left.astype(jnp.float32), right)

def mult_t(left, right):
    return jnp.einsum('gkno,nio->gkni', left.astype(jnp.float32), right)

def outer(left, right):
    return jnp.einsum('gkni,gkno->nio', left.astype(jnp.float32), right.astype(jnp.float32))

def rounded(values):
    return lax.optimization_barrier(values.astype(jnp.bfloat16))

def reference(inputs, cotangent, ln_gain, ln_shift, first_weight, first_bias, second_weight, second_bias):
    w_one = first_weight.astype(jnp.float32).reshape(2, NB, BS, BS)
    w_two = second_weight.astype(jnp.float32).reshape(2, NB, BS, BS)
    b_one = first_bias.reshape(2, NB, BS)
    b_two = second_bias.reshape(2, NB, BS)
    kept = jnp.where(jnp.arange(K) == 0, 1.0, 2.0).astype(jnp.float32)
    dw_one = jnp.zeros((2, NB, BS, BS), jnp.float32)
    dw_two = jnp.zeros((2, NB, BS, BS), jnp.float32)
    db_one = jnp.zeros((2, NB, BS), jnp.float32)
    db_two = jnp.zeros((2, NB, BS), jnp.float32)
    gain_sum = jnp.zeros((C,), jnp.float32)
    shift_sum = jnp.zeros((C,), jnp.float32)
    grads = []
    for sample in range(BATCH):
        values = inputs[sample].astype(jnp.float32)
        mean = lax.optimization_barrier(jnp.mean(values, -1, keepdims=True))
        centred = values - mean
        variance = lax.optimization_barrier(jnp.mean(centred * centred, -1, keepdims=True))
        rstd = lax.rsqrt(variance + EPS)
        normed = centred * rstd
        mixed_in = normed * ln_gain + ln_shift
        spectrum = jnp.fft.fft(jnp.fft.rfft(mixed_in, axis=1, norm='ortho')[:, :K, :], axis=0, norm='ortho')
        spec_re = rounded(spectrum.real).reshape(H, K, NB, BS)
        spec_im = rounded(spectrum.imag).reshape(H, K, NB, BS)
        pre_one_re = mult(spec_re, w_one[0]) - mult(spec_im, w_one[1]) + b_one[0]
        pre_one_im = mult(spec_re, w_one[1]) + mult(spec_im, w_one[0]) + b_one[1]
        act_re, slope_re = gelu_parts(pre_one_re)
        act_im, slope_im = gelu_parts(pre_one_im)
        hid_re = rounded(act_re)
        hid_im = rounded(act_im)
        pre_two_re = mult(hid_re, w_two[0]) - mult(hid_im, w_two[1]) + b_two[0]
        pre_two_im = mult(hid_re, w_two[1]) + mult(hid_im, w_two[0]) + b_two[1]
        cot_values = cotangent[sample].astype(jnp.float32)
        cot_lon = jnp.fft.rfft(cot_values, axis=1, norm='ortho')[:, :K, :] * kept[None, :, None]
        cot_spec = jnp.fft.fft(cot_lon, axis=0, norm='ortho')
        cot_re = cot_spec.real.reshape(H, K, NB, BS)
        cot_im = cot_spec.imag.reshape(H, K, NB, BS)
        grad_two_re = rounded(cot_re * shrink_slope(pre_two_re))
        grad_two_im = rounded(cot_im * shrink_slope(pre_two_im))
        grad_hid_re = mult_t(grad_two_re, w_two[0]) + mult_t(grad_two_im, w_two[1])
        grad_hid_im = mult_t(grad_two_im, w_two[0]) - mult_t(grad_two_re, w_two[1])
        dw_two = dw_two + jnp.stack([outer(hid_re, grad_two_re) + outer(hid_im, grad_two_im), outer(hid_re, grad_two_im) - outer(hid_im, grad_two_re)])
        db_two = db_two + jnp.stack([lax.optimization_barrier(jnp.sum(grad_two_re.astype(jnp.float32), (0, 1))), lax.optimization_barrier(jnp.sum(grad_two_im.astype(jnp.float32), (0, 1)))])
        grad_pre_re = rounded(grad_hid_re * slope_re)
        grad_pre_im = rounded(grad_hid_im * slope_im)
        dw_one = dw_one + jnp.stack([outer(spec_re, grad_pre_re) + outer(spec_im, grad_pre_im), outer(spec_re, grad_pre_im) - outer(spec_im, grad_pre_re)])
        db_one = db_one + jnp.stack([lax.optimization_barrier(jnp.sum(grad_pre_re.astype(jnp.float32), (0, 1))), lax.optimization_barrier(jnp.sum(grad_pre_im.astype(jnp.float32), (0, 1)))])
        grad_spec_re = mult_t(grad_pre_re, w_one[0]) + mult_t(grad_pre_im, w_one[1])
        grad_spec_im = mult_t(grad_pre_im, w_one[0]) - mult_t(grad_pre_re, w_one[1])
        grad_spec = lax.complex(grad_spec_re.reshape(H, K, C), grad_spec_im.reshape(H, K, C))
        grad_lon = jnp.fft.ifft(grad_spec, axis=0, norm='ortho') / kept[None, :, None]
        padded = jnp.pad(grad_lon, ((0, 0), (0, W // 2 + 1 - K), (0, 0)))
        grad_mixed = jnp.fft.irfft(padded, n=W, axis=1, norm='ortho')
        grad_norm = grad_mixed * ln_gain
        mean_one = lax.optimization_barrier(jnp.mean(grad_norm, -1, keepdims=True))
        mean_two = lax.optimization_barrier(jnp.mean(grad_norm * normed, -1, keepdims=True))
        input_part = cot_values + rstd * (grad_norm - mean_one - normed * mean_two)
        grads.append(input_part.astype(jnp.bfloat16))
        gain_sum = gain_sum + lax.optimization_barrier(jnp.sum(grad_mixed * normed, (0, 1)))
        shift_sum = shift_sum + lax.optimization_barrier(jnp.sum(grad_mixed, (0, 1)))
    spec_scale = 1.0 / (BATCH * H * K) ** 0.5
    ln_scale = 1.0 / (BATCH * H * W) ** 0.5
    return (jnp.stack(grads), (dw_one * spec_scale).reshape(2, C, BS), (db_one * spec_scale).reshape(2, C), (dw_two * spec_scale).reshape(2, C, BS), (db_two * spec_scale).reshape(2, C), gain_sum * ln_scale, shift_sum * ln_scale)
```

```python
import functools
import math

import jax
import jax.numpy as jnp
import numpy as np
from jax import lax
from jax.experimental import pallas as pl
from jax.experimental.pallas import tpu as pltpu
from jax.sharding import PartitionSpec as P

K = 192
BS = 128
EPS = 1e-05
LAMBDA = 0.01
ROOT_TWO_PI = math.sqrt(2.0 / math.pi)
BF16 = jnp.bfloat16
F32 = jnp.float32
VMEM_LIMIT = 48 * 1024 * 1024


def gelu_parts(values):
    inner = ROOT_TWO_PI * (values + 0.044715 * values * values * values)
    tangent = jnp.tanh(inner)
    output = 0.5 * values * (1.0 + tangent)
    slope = 0.5 * (1.0 + tangent) + 0.5 * values * (1.0 - tangent * tangent) * ROOT_TWO_PI * (
        1.0 + 3.0 * 0.044715 * values * values
    )
    return (output, slope)


def shrink_slope(values):
    tangent = jnp.tanh(values / LAMBDA)
    return tangent * tangent


def high_low(table):
    high = np.asarray(table, np.float32).astype(jnp.bfloat16)
    low = (np.asarray(table, np.float32) - high.astype(np.float32)).astype(jnp.bfloat16)
    return high, low


def lon_table(width, owners, padded):
    own = K // owners
    number = np.arange(K)[:, None]
    column = np.arange(width)[None, :]
    phase = (number * column % width) * (2.0 * math.pi / width)
    parts = np.stack([np.cos(phase), -np.sin(phase)]) / math.sqrt(width)
    parts = parts.reshape(2, owners, own, width).transpose(1, 0, 2, 3)
    table = np.zeros((owners, padded, width))
    table[:, : 2 * own] = parts.reshape(owners, 2 * own, width)
    return table.reshape(owners * padded, width)


def kept_scale(owners, padded):
    own = K // owners
    scale = np.full((2, K), 2.0)
    scale[:, 0] = 1.0
    out = np.ones((owners, padded))
    out[:, : 2 * own] = scale.reshape(2, owners, own).transpose(1, 0, 2).reshape(owners, 2 * own)
    return out.reshape(owners * padded, 1)


def lat_table(length):
    first = np.arange(length)
    phase = (first[:, None] * first[None, :] % length) * (2.0 * math.pi / length)
    cosine = np.cos(phase) / math.sqrt(length)
    sine = np.sin(phase) / math.sqrt(length)
    return np.block([[cosine, sine], [-sine, cosine]])


def dot(left, right):
    return jnp.dot(left, right, preferred_element_type=F32)


def dot_rows(left, right):
    return lax.dot_general(left, right, (((0,), (0,)), ((), ())), preferred_element_type=F32)


def dot_cols(left, right):
    return lax.dot_general(left, right, (((1,), (1,)), ((), ())), preferred_element_type=F32)


def split(values):
    high = values.astype(BF16)
    return high, (values - high.astype(F32)).astype(BF16)


def columns_of(stats):
    count = stats.shape[0]
    high, rest = split(stats)
    mid, low = split(stats - high.astype(F32))
    stacked = jnp.concatenate([high.astype(F32), mid.astype(F32), low.astype(F32)], 0)
    pad = -stacked.shape[0] % 16
    if pad:
        stacked = jnp.concatenate([stacked, jnp.zeros((pad, stacked.shape[1]), F32)], 0)
    rows = stacked.shape[0]
    row = lax.broadcasted_iota(jnp.int32, (rows, count * 128), 0)
    lane = lax.broadcasted_iota(jnp.int32, (rows, count * 128), 1)
    pick = (row % count == lane // 128) & (row < 3 * count)
    wide = dot_rows(stacked.astype(BF16), pick.astype(F32).astype(BF16))
    return [wide[:, i * 128 : (i + 1) * 128] for i in range(count)]


def cot_lon_kernel(high_ref, low_ref, cot_ref, out_ref):
    owners, blocks, _, padded, _ = out_ref.shape
    values = cot_ref[0, 0]
    result = dot(high_ref[...], values) + dot(low_ref[...], values)
    for b in range(blocks):
        out_ref[:, b, 0] = result[:, b * BS : (b + 1) * BS].reshape(owners, padded, BS)


def input_lon_kernel(high_ref, low_ref, in_ref, stat_ref, gain_ref, *out_refs):
    mean, rstd = columns_of(stat_ref[0])
    at = 0
    for out_ref in out_refs:
        owners, blocks, _, padded, _ = out_ref.shape
        pieces = []
        for b in range(at, at + blocks):
            lanes = slice(b * BS, (b + 1) * BS)
            values = in_ref[0, 0, :, lanes].astype(F32)
            pieces.append((values - mean) * rstd * gain_ref[:, lanes])
        at += blocks
        high, low = split(jnp.concatenate(pieces, 1))
        result = dot(high_ref[...], high) + dot(high_ref[...], low) + dot(low_ref[...], high)
        for b in range(blocks):
            out_ref[:, b, 0] = result[:, b * BS : (b + 1) * BS].reshape(owners, padded, BS)


def mixer_kernel(
    own,
    group,
    fwd_high_ref,
    fwd_low_ref,
    inv_high_ref,
    inv_low_ref,
    w_one_ref,
    w_one_t_ref,
    w_two_ref,
    w_two_t_ref,
    bias_ref,
    shift_ref,
    x_ref,
    c_ref,
    grad_ref,
    sums_ref,
    x_scr,
    c_scr,
    high_scr,
    low_scr,
    spec_scr,
    hid_scr,
    two_scr,
    pre_scr,
    gain_scr,
):
    sources, _, span, _ = x_ref.shape
    length = fwd_high_ref.shape[0] // 2
    padded = sources * span // length
    steps = own // group
    for s in range(sources):
        x_scr[s * span : (s + 1) * span] = x_ref[s, 0]
        c_scr[s * span : (s + 1) * span] = c_ref[s, 0]
    for k in range(own):
        step, place = divmod(k, group)
        for which, scr in enumerate((x_scr, c_scr)):
            lanes = slice((which * group + place) * BS, (which * group + place + 1) * BS)
            for part in range(2):
                values = scr[pl.ds(part * own + k, length, stride=padded), :]
                rows = slice(part * length, (part + 1) * length)
                high, low = split(values)
                high_scr[step, rows, lanes] = high
                low_scr[step, rows, lanes] = low
    gain_scr[...] = jnp.zeros_like(gain_scr)
    w_one = w_one_ref[0]
    w_two = w_two_ref[0]
    first = lax.broadcasted_iota(jnp.int32, (group * length, 1), 0) == 0

    def gather(full, which):
        rows = []
        for place in range(group):
            at = (which * group + place) * BS
            re = full[:length, at : at + BS]
            im = full[length:, at : at + BS]
            rows.append(jnp.concatenate([re, im], 1))
        return jnp.concatenate(rows, 0)

    def body(step, carry):
        high = high_scr[step]
        low = low_scr[step]
        full = dot(fwd_high_ref[...], high) + dot(fwd_high_ref[...], low)
        full = full + dot(fwd_low_ref[...], high)
        plain = gather(full, 0)
        cot = gather(full, 1)
        at = pl.ds(pl.multiple_of(step * (group * length), group * length), group * length)
        is_first = jnp.where(first & (step == 0), 1.0, 0.0)
        spec = (plain + is_first * shift_ref[0, 0:1]).astype(BF16)
        pre_one = dot(spec, w_one) + bias_ref[0, 0:1]
        act, slope = gelu_parts(pre_one)
        hid = act.astype(BF16)
        pre_two = dot(hid, w_two) + bias_ref[0, 1:2]
        grad_two = (cot * shrink_slope(pre_two)).astype(BF16)
        grad_pre = (dot(grad_two, w_two_t_ref[0]) * slope).astype(BF16)
        grad_spec = dot(grad_pre, w_one_t_ref[0])
        spec_scr[at] = spec
        hid_scr[at] = hid
        two_scr[at] = grad_two
        pre_scr[at] = grad_pre
        gain_scr[0:1] += jnp.sum(grad_spec * plain, 0, keepdims=True)
        gain_scr[1:2] += jnp.sum(grad_two.astype(F32), 0, keepdims=True)
        gain_scr[2:3] += jnp.sum(grad_pre.astype(F32), 0, keepdims=True)
        gain_scr[3:4] += jnp.sum(grad_spec * is_first, 0, keepdims=True)
        for place in range(group):
            piece = grad_spec[place * length : (place + 1) * length]
            stacked = jnp.concatenate([piece[:, :BS], piece[:, BS:]], 0)
            grad_high, grad_low = split(stacked)
            high_scr[step, :, place * BS : (place + 1) * BS] = grad_high
            low_scr[step, :, place * BS : (place + 1) * BS] = grad_low
        return carry

    lax.fori_loop(0, steps, body, 0)
    for step in range(steps):
        high = high_scr[step, :, : group * BS]
        low = low_scr[step, :, : group * BS]
        lon = dot(inv_high_ref[...], high) + dot(inv_high_ref[...], low)
        lon = lon + dot(inv_low_ref[...], high)
        for place in range(group):
            k = step * group + place
            for part in range(2):
                piece = lon[part * length : (part + 1) * length, place * BS : (place + 1) * BS]
                x_scr[pl.ds(part * own + k, length, stride=padded), :] = piece
    for k in range(2 * own, padded):
        x_scr[pl.ds(k, length, stride=padded), :] = jnp.zeros((length, BS), F32)
    for s in range(sources):
        grad_ref[s, 0] = x_scr[s * span : (s + 1) * span]
    for i, (left, right) in enumerate(((spec_scr, pre_scr), (hid_scr, two_scr))):
        square = dot_rows(left[...], right[...])
        sums_ref[0, 2 * i * BS : (2 * i + 1) * BS] = square[:BS, :BS] + square[BS:, BS:]
        sums_ref[0, (2 * i + 1) * BS : (2 * i + 2) * BS] = square[:BS, BS:] - square[BS:, :BS]
    total = gain_scr[...]
    sums_ref[0, 4 * BS : 4 * BS + 8] = jnp.concatenate(
        [
            total[2:3, :BS],
            total[2:3, BS:],
            total[1:2, :BS],
            total[1:2, BS:],
            total[0:1, :BS] + total[0:1, BS:],
            total[3:4, :BS] * shift_ref[0, 1:2, :BS],
            jnp.zeros((2, BS), F32),
        ],
        0,
    )


def lon_back_kernel(offset, carry_in, table_ref, grad_ref, in_ref, stat_ref, gain_ref, *refs):
    if carry_in:
        before_ref, out_ref, sums_ref = refs
    else:
        out_ref, sums_ref = refs
    sources, blocks, _, padded, _ = grad_ref.shape
    mean, rstd = columns_of(stat_ref[0])
    pieces = [grad_ref[:, b, 0].reshape(sources * padded, BS).astype(BF16) for b in range(blocks)]
    mixed = dot(table_ref[...], jnp.concatenate(pieces, 1))
    ones = jnp.ones((16, BS), BF16)
    grads = jnp.zeros((in_ref.shape[2], BS), F32)
    products = jnp.zeros((in_ref.shape[2], BS), F32)
    for b in range(blocks):
        lanes = slice((offset + b) * BS, (offset + b + 1) * BS)
        grad = mixed[:, b * BS : (b + 1) * BS] * gain_ref[:, lanes]
        values = in_ref[0, 0, :, b * BS : (b + 1) * BS].astype(F32)
        out_ref[0, :, b * BS : (b + 1) * BS] = grad
        grads = grads + grad
        products = products + grad * ((values - mean) * rstd)
    rows = []
    for values in (grads, products):
        high, low = split(values)
        rows.append((dot_cols(ones, high) + dot_cols(ones, low))[0:1])
    sums = jnp.concatenate(rows, 0)
    if carry_in:
        sums = sums + before_ref[0]
    sums_ref[0] = sums


def finish_kernel(chunks, channels, *refs):
    in_ref, cot_ref, stat_ref, sums_ref = refs[:4]
    grad_refs = refs[4 : 4 + len(chunks)]
    out_ref = refs[-1]
    stats = jnp.concatenate([stat_ref[0], sums_ref[0] / channels], 0)
    mean, rstd, one, two = columns_of(stats)
    at = 0
    for grad_ref, blocks in zip(grad_refs, chunks):
        for b in range(blocks):
            lanes = slice(at * BS, (at + 1) * BS)
            normed = (in_ref[0, 0, :, lanes].astype(F32) - mean) * rstd
            grad = grad_ref[0, :, b * BS : (b + 1) * BS]
            cot = cot_ref[0, 0, :, lanes].astype(F32)
            out_ref[0, 0, :, lanes] = (cot + rstd * (grad - one - normed * two)).astype(BF16)
            at += 1


def params():
    return pltpu.CompilerParams(vmem_limit_bytes=VMEM_LIMIT)


def whole(shape):
    return pl.BlockSpec(shape, lambda *_: (0,) * len(shape))


def cost(flops, moved, transcendentals=0):
    return pl.CostEstimate(
        flops=int(flops), bytes_accessed=int(moved), transcendentals=int(transcendentals)
    )


def on_device(
    inputs, cotangent, ln_gain, ln_shift, first_weight, first_bias, second_weight, second_bias
):
    batch, rows, width, local = inputs.shape
    blocks = local // BS
    owners = lax.axis_size("row")
    height = rows * owners
    own = K // owners
    padded = -(-2 * own // 8) * 8
    tall = owners * padded
    group = 2 if own % 2 == 0 else 1
    total_chan = local * lax.axis_size("chan")
    chunks = (blocks - 1, 1) if blocks > 1 else (1,)
    starts = [sum(chunks[:i]) for i in range(len(chunks))]
    gain = ln_gain.reshape(1, local)

    lon = lon_table(width, owners, padded)
    lon_high, lon_low = high_low(lon)
    cot_high, cot_low = high_low(lon * kept_scale(owners, padded))
    back = np.ascontiguousarray(lon.T).astype(np.float32).astype(jnp.bfloat16)
    fwd_high, fwd_low = high_low(lat_table(height))
    inv_high, inv_low = high_low(lat_table(height).T)

    def exchange(piece):
        return lax.all_to_all(piece, "row", split_axis=0, concat_axis=0, tiled=True)

    row_spec = pl.BlockSpec((1, 1, width, local), lambda h: (0, h, 0, 0))
    stat_spec = pl.BlockSpec((1, 2, width), lambda h: (h, 0, 0))

    def spectrum_spec(count):
        return pl.BlockSpec((owners, count, 1, padded, BS), lambda h: (0, 0, h, 0, 0))

    def spectrum_shape(count):
        return jax.ShapeDtypeStruct((owners, count, rows, padded, BS), F32)

    lon_flops = 2 * rows * tall * width * local
    cot_lon = pl.pallas_call(
        cot_lon_kernel,
        grid=(rows,),
        in_specs=[whole((tall, width)), whole((tall, width)), row_spec],
        out_specs=spectrum_spec(blocks),
        out_shape=spectrum_shape(blocks),
        compiler_params=params(),
        cost_estimate=cost(2 * lon_flops, rows * local * (2 * width + 4 * tall)),
        name="cot_lon",
    )(cot_high, cot_low, cotangent)
    cot_lon, inputs = lax.optimization_barrier((cot_lon, inputs))
    cot_spec = exchange(cot_lon)

    values = inputs.astype(F32)
    mean = lax.psum(jnp.sum(values, -1), "chan") / total_chan
    centred = values - mean[..., None]
    variance = lax.psum(jnp.sum(centred * centred, -1), "chan") / total_chan
    stats = jnp.stack([mean[0], lax.rsqrt(variance + EPS)[0]], 1)

    input_lon = pl.pallas_call(
        input_lon_kernel,
        grid=(rows,),
        in_specs=[
            whole((tall, width)),
            whole((tall, width)),
            row_spec,
            stat_spec,
            whole((1, local)),
        ],
        out_specs=[spectrum_spec(count) for count in chunks],
        out_shape=[spectrum_shape(count) for count in chunks],
        compiler_params=params(),
        cost_estimate=cost(3 * lon_flops, rows * local * (2 * width + 4 * tall)),
        name="input_lon",
    )(lon_high, lon_low, inputs, stats, gain)

    def square(weight):
        re, im = weight.reshape(2, blocks, BS, BS)
        return jnp.concatenate(
            [jnp.concatenate([re, im], 2), jnp.concatenate([-im, re], 2)], 1
        )

    w_one = square(first_weight)
    w_two = square(second_weight)
    w_one_t = w_one.swapaxes(1, 2)
    w_two_t = w_two.swapaxes(1, 2)
    bias = jnp.stack([first_bias, second_bias]).reshape(2, 2, blocks, BS)
    bias = bias.transpose(2, 0, 1, 3).reshape(blocks, 2, 2 * BS)
    is_origin = (lax.axis_index("row") == 0).astype(F32)
    shift = (ln_shift * (math.sqrt(height * width) * is_origin)).reshape(blocks, 1, BS)
    shift = jnp.concatenate([shift, jnp.zeros_like(shift)], 2)
    shift = jnp.concatenate([shift, jnp.full_like(shift, is_origin)], 1)

    span = rows * padded
    mat = pl.BlockSpec((1, 2 * BS, 2 * BS), lambda b: (b, 0, 0))

    def mix(index, x_spec):
        count = chunks[index]
        start = starts[index]

        def at(shape):
            return pl.BlockSpec(shape, lambda b: (b + start,) + (0,) * (len(shape) - 1))

        tokens = own * height
        flops = 2 * count * tokens * 2 * BS * (3 * 2 * height * 3 + 6 * 2 * BS)
        return pl.pallas_call(
            functools.partial(mixer_kernel, own, group),
            grid=(count,),
            in_specs=[whole((2 * height, 2 * height))] * 4
            + [at((1, 2 * BS, 2 * BS))] * 4
            + [
                at((1, 2, 2 * BS)),
                at((1, 2, 2 * BS)),
                pl.BlockSpec((owners, 1, span, BS), lambda b: (0, b, 0, 0)),
                pl.BlockSpec((owners, 1, span, BS), lambda b: (0, b + start, 0, 0)),
            ],
            out_specs=[
                pl.BlockSpec((owners, 1, span, BS), lambda b: (0, b, 0, 0)),
                pl.BlockSpec((1, 4 * BS + 8, BS), lambda b: (b, 0, 0)),
            ],
            out_shape=[
                jax.ShapeDtypeStruct((owners, count, span, BS), F32),
                jax.ShapeDtypeStruct((count, 4 * BS + 8, BS), F32),
            ],
            scratch_shapes=[
                pltpu.VMEM((owners * span, BS), F32),
                pltpu.VMEM((owners * span, BS), F32),
                pltpu.VMEM((own // group, 2 * height, 2 * group * BS), BF16),
                pltpu.VMEM((own // group, 2 * height, 2 * group * BS), BF16),
                pltpu.VMEM((tokens, 2 * BS), BF16),
                pltpu.VMEM((tokens, 2 * BS), BF16),
                pltpu.VMEM((tokens, 2 * BS), BF16),
                pltpu.VMEM((tokens, 2 * BS), BF16),
                pltpu.VMEM((8, 2 * BS), F32),
            ],
            compiler_params=params(),
            cost_estimate=cost(flops, 3 * count * owners * span * BS * 4, 4 * tokens * BS * count),
            name=f"mixer_{index}",
        )(
            fwd_high,
            fwd_low,
            inv_high,
            inv_low,
            w_one,
            w_one_t,
            w_two,
            w_two_t,
            bias,
            shift,
            x_spec.reshape(owners, count, span, BS),
            cot_spec.reshape(owners, blocks, span, BS),
        )

    mixed = [mix(i, exchange(piece)) for i, piece in enumerate(input_lon)]
    param_sums = lax.psum(jnp.concatenate([m[1] for m in mixed], 0), "row")

    grads = []
    sums = None
    for index, count in enumerate(chunks):
        start = starts[index]
        piece = exchange(mixed[index][0].reshape(owners, count, rows, padded, BS))
        in_spec = pl.BlockSpec(
            (1, 1, width, count * BS), lambda h, at=start // count: (0, h, 0, at)
        )
        carry_in = sums is not None
        grad, sums = pl.pallas_call(
            functools.partial(lon_back_kernel, start, carry_in),
            grid=(rows,),
            in_specs=[
                whole((width, tall)),
                spectrum_spec(count),
                in_spec,
                stat_spec,
                whole((1, local)),
            ]
            + [stat_spec] * carry_in,
            out_specs=[pl.BlockSpec((1, width, count * BS), lambda h: (h, 0, 0)), stat_spec],
            out_shape=[
                jax.ShapeDtypeStruct((rows, width, count * BS), F32),
                jax.ShapeDtypeStruct((rows, 2, width), F32),
            ],
            compiler_params=params(),
            cost_estimate=cost(
                2 * rows * tall * width * count * BS, rows * count * BS * (6 * width + 4 * tall)
            ),
            name=f"lon_back_{index}",
        )(back, piece, inputs, stats, gain, *([sums] * carry_in))
        grads.append(grad)

    input_grad = pl.pallas_call(
        functools.partial(finish_kernel, chunks, total_chan),
        grid=(rows,),
        in_specs=[row_spec, row_spec, stat_spec, stat_spec]
        + [pl.BlockSpec((1, width, count * BS), lambda h: (h, 0, 0)) for count in chunks],
        out_specs=row_spec,
        out_shape=jax.ShapeDtypeStruct(inputs.shape, BF16),
        compiler_params=params(),
        cost_estimate=cost(10 * rows * width * local, rows * width * local * 10),
        name="finish",
    )(inputs, cotangent, stats, lax.psum(sums, "chan"), *grads)

    spec_scale = 1.0 / math.sqrt(batch * height * K)
    dw = param_sums[:, : 4 * BS].reshape(blocks, 2, 2, BS, BS).transpose(1, 2, 0, 3, 4) * spec_scale
    db = param_sums[:, 4 * BS : 4 * BS + 4].reshape(blocks, 2, 2, BS).transpose(1, 2, 0, 3)
    db = db * spec_scale
    ln_scale = 1.0 / math.sqrt(batch * height * width)
    gain_grad = param_sums[:, 4 * BS + 4].reshape(local) / ln_gain * ln_scale
    return (
        input_grad,
        dw[0].reshape(2, local, BS),
        db[0].reshape(2, local),
        dw[1].reshape(2, local, BS),
        db[1].reshape(2, local),
        gain_grad,
        param_sums[:, 4 * BS + 5].reshape(local),
    )


def solution(mesh):
    placed = (
        P(None, "row", None, "chan"),
        P(None, "row", None, "chan"),
        P("chan"),
        P("chan"),
        P(None, "chan", None),
        P(None, "chan"),
        P(None, "chan", None),
        P(None, "chan"),
    )
    return jax.shard_map(
        on_device,
        mesh=mesh,
        in_specs=placed,
        out_specs=(
            P(None, "row", None, "chan"),
            P(None, "chan", None),
            P(None, "chan"),
            P(None, "chan", None),
            P(None, "chan"),
            P("chan"),
            P("chan"),
        ),
        check_vma=False,
    )
```

```python
import functools
import math

import jax
import jax.numpy as jnp
import numpy as np
from jax import lax
from jax.experimental import pallas as pl
from jax.experimental.pallas import tpu as pltpu
from jax.sharding import PartitionSpec as P

K = 192
BS = 128
EPS = 1e-05
LAMBDA = 0.01
ROOT_TWO_PI = math.sqrt(2.0 / math.pi)
BF16 = jnp.bfloat16
F32 = jnp.float32
VMEM_LIMIT = 60 * 1024 * 1024


def gelu_parts(values):
    inner = ROOT_TWO_PI * (values + 0.044715 * values * values * values)
    tangent = jnp.tanh(inner)
    output = 0.5 * values * (1.0 + tangent)
    slope = 0.5 * (1.0 + tangent) + 0.5 * values * (1.0 - tangent * tangent) * ROOT_TWO_PI * (
        1.0 + 3.0 * 0.044715 * values * values
    )
    return (output, slope)


def shrink_slope(values):
    tangent = jnp.tanh(values / LAMBDA)
    return tangent * tangent


def high_low(table):
    high = np.asarray(table, np.float32).astype(jnp.bfloat16)
    low = (np.asarray(table, np.float32) - high.astype(np.float32)).astype(jnp.bfloat16)
    return high, low


def lon_table(width, owners, padded):
    own = K // owners
    number = np.arange(K)[:, None]
    column = np.arange(width)[None, :]
    phase = (number * column % width) * (2.0 * math.pi / width)
    parts = np.stack([np.cos(phase), -np.sin(phase)]) / math.sqrt(width)
    parts = parts.reshape(2, owners, own, width).transpose(1, 0, 2, 3)
    table = np.zeros((owners, padded, width))
    table[:, : 2 * own] = parts.reshape(owners, 2 * own, width)
    return table.reshape(owners * padded, width)


def kept_scale(owners, padded):
    own = K // owners
    scale = np.full((2, K), 2.0)
    scale[:, 0] = 1.0
    out = np.ones((owners, padded))
    out[:, : 2 * own] = scale.reshape(2, owners, own).transpose(1, 0, 2).reshape(owners, 2 * own)
    return out.reshape(owners * padded, 1)


def lat_table(length):
    first = np.arange(length)
    phase = (first[:, None] * first[None, :] % length) * (2.0 * math.pi / length)
    cosine = np.cos(phase) / math.sqrt(length)
    sine = np.sin(phase) / math.sqrt(length)
    return np.block([[cosine, sine], [-sine, cosine]])


def dot(left, right):
    return jnp.dot(left, right, preferred_element_type=F32)


def dot_rows(left, right):
    return lax.dot_general(left, right, (((0,), (0,)), ((), ())), preferred_element_type=F32)


def dot_cols(left, right):
    return lax.dot_general(left, right, (((1,), (1,)), ((), ())), preferred_element_type=F32)


def split(values):
    high = values.astype(BF16)
    return high, (values - high.astype(F32)).astype(BF16)


def columns_of(stats):
    count = stats.shape[0]
    high, rest = split(stats)
    mid, low = split(stats - high.astype(F32))
    stacked = jnp.concatenate([high.astype(F32), mid.astype(F32), low.astype(F32)], 0)
    pad = -stacked.shape[0] % 16
    if pad:
        stacked = jnp.concatenate([stacked, jnp.zeros((pad, stacked.shape[1]), F32)], 0)
    rows = stacked.shape[0]
    row = lax.broadcasted_iota(jnp.int32, (rows, count * 128), 0)
    lane = lax.broadcasted_iota(jnp.int32, (rows, count * 128), 1)
    pick = (row % count == lane // 128) & (row < 3 * count)
    wide = dot_rows(stacked.astype(BF16), pick.astype(F32).astype(BF16))
    return [wide[:, i * 128 : (i + 1) * 128] for i in range(count)]


def cot_lon_kernel(table_ref, cot_ref, out_ref):
    owners, blocks, rows, padded, _ = out_ref.shape
    for r in range(rows):
        result = dot(table_ref[...], cot_ref[0, r])
        for b in range(blocks):
            out_ref[:, b, r] = result[:, b * BS : (b + 1) * BS].reshape(owners, padded, BS)


def input_lon_kernel(table_ref, in_ref, stat_ref, gain_ref, *out_refs):
    tall = table_ref.shape[0] // 2
    for r in range(in_ref.shape[1]):
        mean, rstd = columns_of(stat_ref[r])
        at = 0
        for out_ref in out_refs:
            owners, blocks, _, padded, _ = out_ref.shape
            pieces = []
            for b in range(at, at + blocks):
                lanes = slice(b * BS, (b + 1) * BS)
                values = in_ref[0, r, :, lanes].astype(F32)
                pieces.append((values - mean) * rstd * gain_ref[:, lanes])
            at += blocks
            high, low = split(jnp.concatenate(pieces, 1))
            both = dot(table_ref[...], high)
            result = both[:tall] + both[tall:] + dot(table_ref[:tall], low)
            for b in range(blocks):
                out_ref[:, b, r] = result[:, b * BS : (b + 1) * BS].reshape(owners, padded, BS)


def mixer_kernel(
    own,
    group,
    fwd_high_ref,
    fwd_low_ref,
    inv_high_ref,
    inv_low_ref,
    w_one_ref,
    w_one_t_ref,
    w_two_ref,
    w_two_t_ref,
    bias_ref,
    shift_ref,
    x_ref,
    c_ref,
    grad_ref,
    sums_ref,
    x_scr,
    c_scr,
    high_scr,
    low_scr,
    spec_scr,
    hid_scr,
    two_scr,
    pre_scr,
    gain_scr,
):
    sources, _, span, _ = x_ref.shape
    length = fwd_high_ref.shape[0] // 2
    padded = sources * span // length
    steps = own // group
    for s in range(sources):
        x_scr[s * span : (s + 1) * span] = x_ref[s, 0]
        c_scr[s * span : (s + 1) * span] = c_ref[s, 0]
    for k in range(own):
        step, place = divmod(k, group)
        for which, scr in enumerate((x_scr, c_scr)):
            lanes = slice((which * group + place) * BS, (which * group + place + 1) * BS)
            for part in range(2):
                values = scr[pl.ds(part * own + k, length, stride=padded), :]
                rows = slice(part * length, (part + 1) * length)
                high, low = split(values)
                high_scr[step, rows, lanes] = high
                low_scr[step, rows, lanes] = low
    gain_scr[...] = jnp.zeros_like(gain_scr)
    w_one = w_one_ref[0]
    w_two = w_two_ref[0]
    first = lax.broadcasted_iota(jnp.int32, (group * length, 1), 0) == 0

    def gather(full, which):
        rows = []
        for place in range(group):
            at = (which * group + place) * BS
            re = full[:length, at : at + BS]
            im = full[length:, at : at + BS]
            rows.append(jnp.concatenate([re, im], 1))
        return jnp.concatenate(rows, 0)

    def body(step, carry):
        high = high_scr[step]
        low = low_scr[step]
        full = dot(fwd_high_ref[...], high) + dot(fwd_high_ref[...], low)
        full = full + dot(fwd_low_ref[...], high)
        plain = gather(full, 0)
        cot = gather(full, 1)
        at = pl.ds(pl.multiple_of(step * (group * length), group * length), group * length)
        is_first = jnp.where(first & (step == 0), 1.0, 0.0)
        spec = (plain + is_first * shift_ref[0, 0:1]).astype(BF16)
        pre_one = dot(spec, w_one) + bias_ref[0, 0:1]
        act, slope = gelu_parts(pre_one)
        hid = act.astype(BF16)
        pre_two = dot(hid, w_two) + bias_ref[0, 1:2]
        grad_two = (cot * shrink_slope(pre_two)).astype(BF16)
        grad_pre = (dot(grad_two, w_two_t_ref[0]) * slope).astype(BF16)
        grad_spec = dot(grad_pre, w_one_t_ref[0])
        spec_scr[at] = spec
        hid_scr[at] = hid
        two_scr[at] = grad_two
        pre_scr[at] = grad_pre
        gain_scr[0:1] += jnp.sum(grad_spec * plain, 0, keepdims=True)
        gain_scr[1:2] += jnp.sum(grad_two.astype(F32), 0, keepdims=True)
        gain_scr[2:3] += jnp.sum(grad_pre.astype(F32), 0, keepdims=True)
        gain_scr[3:4] += jnp.sum(grad_spec * is_first, 0, keepdims=True)
        for place in range(group):
            piece = grad_spec[place * length : (place + 1) * length]
            stacked = jnp.concatenate([piece[:, :BS], piece[:, BS:]], 0)
            grad_high, grad_low = split(stacked)
            high_scr[step, :, place * BS : (place + 1) * BS] = grad_high
            low_scr[step, :, place * BS : (place + 1) * BS] = grad_low
        return carry

    lax.fori_loop(0, steps, body, 0)
    for step in range(steps):
        high = high_scr[step, :, : group * BS]
        low = low_scr[step, :, : group * BS]
        lon = dot(inv_high_ref[...], high) + dot(inv_high_ref[...], low)
        lon = lon + dot(inv_low_ref[...], high)
        for place in range(group):
            k = step * group + place
            for part in range(2):
                piece = lon[part * length : (part + 1) * length, place * BS : (place + 1) * BS]
                x_scr[pl.ds(part * own + k, length, stride=padded), :] = piece
    for k in range(2 * own, padded):
        x_scr[pl.ds(k, length, stride=padded), :] = jnp.zeros((length, BS), F32)
    for s in range(sources):
        grad_ref[s, 0] = x_scr[s * span : (s + 1) * span]
    for i, (left, right) in enumerate(((spec_scr, pre_scr), (hid_scr, two_scr))):
        square = dot_rows(left[...], right[...])
        sums_ref[0, 2 * i * BS : (2 * i + 1) * BS] = square[:BS, :BS] + square[BS:, BS:]
        sums_ref[0, (2 * i + 1) * BS : (2 * i + 2) * BS] = square[:BS, BS:] - square[BS:, :BS]
    total = gain_scr[...]
    sums_ref[0, 4 * BS : 4 * BS + 8] = jnp.concatenate(
        [
            total[2:3, :BS],
            total[2:3, BS:],
            total[1:2, :BS],
            total[1:2, BS:],
            total[0:1, :BS] + total[0:1, BS:],
            total[3:4, :BS] * shift_ref[0, 1:2, :BS],
            jnp.zeros((2, BS), F32),
        ],
        0,
    )


def lon_back_kernel(
    offset, carry_in, table_ref, grad_ref, in_ref, cot_ref, stat_ref, gain_ref, *refs
):
    if carry_in:
        before_ref, out_ref, sums_ref = refs
    else:
        out_ref, sums_ref = refs
    sources, blocks, rows, padded, _ = grad_ref.shape
    ones = jnp.ones((16, BS), BF16)
    for r in range(rows):
        mean, rstd = columns_of(stat_ref[r])
        pieces = [
            grad_ref[:, b, r].reshape(sources * padded, BS).astype(BF16) for b in range(blocks)
        ]
        mixed = dot(table_ref[...], jnp.concatenate(pieces, 1))
        grads = jnp.zeros((in_ref.shape[2], BS), F32)
        products = jnp.zeros((in_ref.shape[2], BS), F32)
        for b in range(blocks):
            lanes = slice((offset + b) * BS, (offset + b + 1) * BS)
            grad = mixed[:, b * BS : (b + 1) * BS] * gain_ref[:, lanes]
            values = in_ref[0, r, :, b * BS : (b + 1) * BS].astype(F32)
            cot = cot_ref[0, r, :, b * BS : (b + 1) * BS].astype(F32)
            out_ref[r, :, b * BS : (b + 1) * BS] = cot + rstd * grad
            grads = grads + grad
            products = products + grad * ((values - mean) * rstd)
        both = []
        for values in (grads, products):
            high, low = split(values)
            both.append((dot_cols(ones, high) + dot_cols(ones, low))[0:1])
        sums = jnp.concatenate(both, 0)
        if carry_in:
            sums = sums + before_ref[r]
        sums_ref[r] = sums


def finish_kernel(chunks, channels, *refs):
    in_ref, stat_ref, sums_ref = refs[:3]
    base_refs = refs[3 : 3 + len(chunks)]
    out_ref = refs[-1]
    for r in range(in_ref.shape[1]):
        mean, rstd = stat_ref[r, 0:1], stat_ref[r, 1:2]
        slope = rstd * rstd * (sums_ref[r, 1:2] / channels)
        level = rstd * (sums_ref[r, 0:1] / channels) - mean * slope
        level, slope = columns_of(jnp.concatenate([level, slope], 0))
        at = 0
        for base_ref, blocks in zip(base_refs, chunks):
            for b in range(blocks):
                lanes = slice(at * BS, (at + 1) * BS)
                values = in_ref[0, r, :, lanes].astype(F32)
                base = base_ref[r, :, b * BS : (b + 1) * BS]
                out_ref[0, r, :, lanes] = (base - level - slope * values).astype(BF16)
                at += 1


def xor_permute(piece, axis, bit):
    size = lax.axis_size(axis)
    return lax.ppermute(piece, axis, [(i, i ^ bit) for i in range(size)])


def sum_small(piece, axis):
    bit = 1
    while bit < lax.axis_size(axis):
        piece = piece + xor_permute(piece, axis, bit)
        bit *= 2
    return piece


def sum_halving(piece, axis):
    size = lax.axis_size(axis)
    index = lax.axis_index(axis)
    bits = [1 << i for i in range(size.bit_length() - 1)]
    for bit in bits:
        half = piece.shape[0] // 2
        low, high = piece[:half], piece[half:]
        upper = (index & bit) != 0
        piece = jnp.where(upper, high, low) + xor_permute(jnp.where(upper, low, high), axis, bit)
    for bit in reversed(bits):
        other = xor_permute(piece, axis, bit)
        upper = (index & bit) != 0
        piece = jnp.concatenate(
            [jnp.where(upper, other, piece), jnp.where(upper, piece, other)], 0
        )
    return piece


def divisor(count, limit):
    return max(n for n in range(1, limit + 1) if count % n == 0)


def params():
    return pltpu.CompilerParams(vmem_limit_bytes=VMEM_LIMIT)


def whole(shape):
    return pl.BlockSpec(shape, lambda *_: (0,) * len(shape))


def cost(flops, moved, transcendentals=0):
    return pl.CostEstimate(
        flops=int(flops), bytes_accessed=int(moved), transcendentals=int(transcendentals)
    )


def on_device(
    inputs, cotangent, ln_gain, ln_shift, first_weight, first_bias, second_weight, second_bias
):
    batch, rows, width, local = inputs.shape
    blocks = local // BS
    owners = lax.axis_size("row")
    height = rows * owners
    own = K // owners
    padded = -(-2 * own // 8) * 8
    tall = owners * padded
    group = 2 if own % 2 == 0 else 1
    total_chan = local * lax.axis_size("chan")
    chunks = (blocks - 1, 1) if blocks > 1 else (1,)
    starts = [sum(chunks[:i]) for i in range(len(chunks))]
    gain = ln_gain.reshape(1, local)

    lon = lon_table(width, owners, padded)
    lon_high, lon_low = high_low(lon)
    lon_both = np.concatenate([lon_high, lon_low], 0)
    cot_high, _ = high_low(lon * kept_scale(owners, padded))
    back = np.ascontiguousarray(lon.T).astype(np.float32).astype(jnp.bfloat16)
    fwd_high, fwd_low = high_low(lat_table(height))
    inv_high, inv_low = high_low(lat_table(height).T)

    def exchange(piece):
        return lax.all_to_all(piece, "row", split_axis=0, concat_axis=0, tiled=True)

    few = divisor(rows, 2)
    many = divisor(rows, 4)

    def row_spec(step):
        return pl.BlockSpec((1, step, width, local), lambda h: (0, h, 0, 0))

    def stat_spec(step):
        return pl.BlockSpec((step, 2, width), lambda h: (h, 0, 0))

    def grad_spec(step, count):
        return pl.BlockSpec((step, width, count * BS), lambda h: (h, 0, 0))

    def spectrum_spec(step, count):
        return pl.BlockSpec((owners, count, step, padded, BS), lambda h: (0, 0, h, 0, 0))

    def spectrum_shape(count):
        return jax.ShapeDtypeStruct((owners, count, rows, padded, BS), F32)

    lon_flops = 2 * rows * tall * width * local
    cot_lon = pl.pallas_call(
        cot_lon_kernel,
        grid=(rows // few,),
        in_specs=[whole((tall, width)), row_spec(few)],
        out_specs=spectrum_spec(few, blocks),
        out_shape=spectrum_shape(blocks),
        compiler_params=params(),
        cost_estimate=cost(lon_flops, rows * local * (2 * width + 4 * tall)),
        name="cot_lon",
    )(cot_high, cotangent)
    cot_lon, inputs = lax.optimization_barrier((cot_lon, inputs))
    cot_spec = exchange(cot_lon)

    values = inputs.astype(F32)
    mean = lax.psum(jnp.sum(values, -1), "chan") / total_chan
    centred = values - mean[..., None]
    variance = lax.psum(jnp.sum(centred * centred, -1), "chan") / total_chan
    stats = jnp.stack([mean[0], lax.rsqrt(variance + EPS)[0]], 1)

    input_lon = pl.pallas_call(
        input_lon_kernel,
        grid=(rows // few,),
        in_specs=[whole((2 * tall, width)), row_spec(few), stat_spec(few), whole((1, local))],
        out_specs=[spectrum_spec(few, count) for count in chunks],
        out_shape=[spectrum_shape(count) for count in chunks],
        compiler_params=params(),
        cost_estimate=cost(3 * lon_flops, rows * local * (2 * width + 4 * tall)),
        name="input_lon",
    )(lon_both, inputs, stats, gain)
    first_piece, cot_spec = lax.optimization_barrier((input_lon[0], cot_spec))
    input_lon = [first_piece, *input_lon[1:]]

    def square(weight):
        re, im = weight.reshape(2, blocks, BS, BS)
        return jnp.concatenate(
            [jnp.concatenate([re, im], 2), jnp.concatenate([-im, re], 2)], 1
        )

    w_one = square(first_weight)
    w_two = square(second_weight)
    w_one_t = w_one.swapaxes(1, 2)
    w_two_t = w_two.swapaxes(1, 2)
    bias = jnp.stack([first_bias, second_bias]).reshape(2, 2, blocks, BS)
    bias = bias.transpose(2, 0, 1, 3).reshape(blocks, 2, 2 * BS)
    is_origin = (lax.axis_index("row") == 0).astype(F32)
    shift = (ln_shift * (math.sqrt(height * width) * is_origin)).reshape(blocks, 1, BS)
    shift = jnp.concatenate([shift, jnp.zeros_like(shift)], 2)
    shift = jnp.concatenate([shift, jnp.full_like(shift, is_origin)], 1)

    span = rows * padded
    mat = pl.BlockSpec((1, 2 * BS, 2 * BS), lambda b: (b, 0, 0))

    def mix(index, x_spec):
        count = chunks[index]
        start = starts[index]

        def at(shape):
            return pl.BlockSpec(shape, lambda b: (b + start,) + (0,) * (len(shape) - 1))

        tokens = own * height
        flops = 2 * count * tokens * 2 * BS * (3 * 2 * height * 3 + 6 * 2 * BS)
        return pl.pallas_call(
            functools.partial(mixer_kernel, own, group),
            grid=(count,),
            in_specs=[whole((2 * height, 2 * height))] * 4
            + [at((1, 2 * BS, 2 * BS))] * 4
            + [
                at((1, 2, 2 * BS)),
                at((1, 2, 2 * BS)),
                pl.BlockSpec((owners, 1, span, BS), lambda b: (0, b, 0, 0)),
                pl.BlockSpec((owners, 1, span, BS), lambda b: (0, b + start, 0, 0)),
            ],
            out_specs=[
                pl.BlockSpec((owners, 1, span, BS), lambda b: (0, b, 0, 0)),
                pl.BlockSpec((1, 4 * BS + 8, BS), lambda b: (b, 0, 0)),
            ],
            out_shape=[
                jax.ShapeDtypeStruct((owners, count, span, BS), F32),
                jax.ShapeDtypeStruct((count, 4 * BS + 8, BS), F32),
            ],
            scratch_shapes=[
                pltpu.VMEM((owners * span, BS), F32),
                pltpu.VMEM((owners * span, BS), F32),
                pltpu.VMEM((own // group, 2 * height, 2 * group * BS), BF16),
                pltpu.VMEM((own // group, 2 * height, 2 * group * BS), BF16),
                pltpu.VMEM((tokens, 2 * BS), BF16),
                pltpu.VMEM((tokens, 2 * BS), BF16),
                pltpu.VMEM((tokens, 2 * BS), BF16),
                pltpu.VMEM((tokens, 2 * BS), BF16),
                pltpu.VMEM((8, 2 * BS), F32),
            ],
            compiler_params=params(),
            cost_estimate=cost(flops, 3 * count * owners * span * BS * 4, 4 * tokens * BS * count),
            name=f"mixer_{index}",
        )(
            fwd_high,
            fwd_low,
            inv_high,
            inv_low,
            w_one,
            w_one_t,
            w_two,
            w_two_t,
            bias,
            shift,
            x_spec.reshape(owners, count, span, BS),
            cot_spec.reshape(owners, blocks, span, BS),
        )

    mixed = [mix(i, exchange(piece)) for i, piece in enumerate(input_lon)]
    param_rows = 4 * BS + 8
    unit = 8 * owners // math.gcd(8 * owners, blocks)
    tail = -(blocks * param_rows) % (unit * blocks)
    flat = jnp.concatenate([m[1].reshape(-1, BS) for m in mixed], 0)
    flat = jnp.pad(flat, ((0, tail), (0, 0)))
    param_sums = sum_halving(flat, "row")[: blocks * param_rows]
    param_sums = param_sums.reshape(blocks, param_rows, BS)

    grads = []
    sums = None
    for index, count in enumerate(chunks):
        start = starts[index]
        piece = mixed[index][0].reshape(owners, count, rows, padded, BS)
        carry_in = sums is not None
        if index == len(chunks) - 1 and carry_in:
            piece, param_sums = lax.optimization_barrier((piece, param_sums))
        piece = exchange(piece)
        in_spec = pl.BlockSpec(
            (1, many, width, count * BS), lambda h, at=start // count: (0, h, 0, at)
        )
        grad, sums = pl.pallas_call(
            functools.partial(lon_back_kernel, start, carry_in),
            grid=(rows // many,),
            in_specs=[
                whole((width, tall)),
                spectrum_spec(many, count),
                in_spec,
                in_spec,
                stat_spec(many),
                whole((1, local)),
            ]
            + [stat_spec(many)] * carry_in,
            out_specs=[grad_spec(many, count), stat_spec(many)],
            out_shape=[
                jax.ShapeDtypeStruct((rows, width, count * BS), F32),
                jax.ShapeDtypeStruct((rows, 2, width), F32),
            ],
            compiler_params=params(),
            cost_estimate=cost(
                2 * rows * tall * width * count * BS, rows * count * BS * (6 * width + 4 * tall)
            ),
            name=f"lon_back_{index}",
        )(back, piece, inputs, cotangent, stats, gain, *([sums] * carry_in))
        grads.append(grad)

    input_grad = pl.pallas_call(
        functools.partial(finish_kernel, chunks, total_chan),
        grid=(rows // few,),
        in_specs=[row_spec(few), stat_spec(few), stat_spec(few)]
        + [grad_spec(few, count) for count in chunks],
        out_specs=row_spec(few),
        out_shape=jax.ShapeDtypeStruct(inputs.shape, BF16),
        compiler_params=params(),
        cost_estimate=cost(10 * rows * width * local, rows * width * local * 10),
        name="finish",
    )(inputs, stats, sum_small(sums, "chan"), *grads)

    spec_scale = 1.0 / math.sqrt(batch * height * K)
    dw = param_sums[:, : 4 * BS].reshape(blocks, 2, 2, BS, BS).transpose(1, 2, 0, 3, 4) * spec_scale
    db = param_sums[:, 4 * BS : 4 * BS + 4].reshape(blocks, 2, 2, BS).transpose(1, 2, 0, 3)
    db = db * spec_scale
    ln_scale = 1.0 / math.sqrt(batch * height * width)
    gain_grad = param_sums[:, 4 * BS + 4].reshape(local) / ln_gain * ln_scale
    return (
        input_grad,
        dw[0].reshape(2, local, BS),
        db[0].reshape(2, local),
        dw[1].reshape(2, local, BS),
        db[1].reshape(2, local),
        gain_grad,
        param_sums[:, 4 * BS + 5].reshape(local),
    )


def solution(mesh):
    placed = (
        P(None, "row", None, "chan"),
        P(None, "row", None, "chan"),
        P("chan"),
        P("chan"),
        P(None, "chan", None),
        P(None, "chan"),
        P(None, "chan", None),
        P(None, "chan"),
    )
    return jax.shard_map(
        on_device,
        mesh=mesh,
        in_specs=placed,
        out_specs=(
            P(None, "row", None, "chan"),
            P(None, "chan", None),
            P(None, "chan"),
            P(None, "chan", None),
            P(None, "chan"),
            P("chan"),
            P("chan"),
        ),
        check_vma=False,
    )
```

```python
import functools
import math

import jax
import jax.numpy as jnp
import numpy as np
from jax import lax
from jax.experimental import pallas as pl
from jax.experimental.pallas import tpu as pltpu
from jax.sharding import PartitionSpec as P

K = 192
BS = 128
EPS = 1e-05
LAMBDA = 0.01
ROOT_TWO_PI = math.sqrt(2.0 / math.pi)
BF16 = jnp.bfloat16
F32 = jnp.float32
VMEM_LIMIT = 60 * 1024 * 1024


def gelu_parts(values):
    inner = ROOT_TWO_PI * (values + 0.044715 * values * values * values)
    tangent = jnp.tanh(inner)
    output = 0.5 * values * (1.0 + tangent)
    slope = 0.5 * (1.0 + tangent) + 0.5 * values * (1.0 - tangent * tangent) * ROOT_TWO_PI * (
        1.0 + 3.0 * 0.044715 * values * values
    )
    return (output, slope)


def shrink_slope(values):
    tangent = jnp.tanh(values / LAMBDA)
    return tangent * tangent


def high_low(table):
    high = np.asarray(table, np.float32).astype(jnp.bfloat16)
    low = (np.asarray(table, np.float32) - high.astype(np.float32)).astype(jnp.bfloat16)
    return high, low


def lon_table(width, owners, padded):
    own = K // owners
    number = np.arange(K)[:, None]
    column = np.arange(width)[None, :]
    phase = (number * column % width) * (2.0 * math.pi / width)
    parts = np.stack([np.cos(phase), -np.sin(phase)]) / math.sqrt(width)
    parts = parts.reshape(2, owners, own, width).transpose(1, 0, 2, 3)
    table = np.zeros((owners, padded, width))
    table[:, : 2 * own] = parts.reshape(owners, 2 * own, width)
    return table.reshape(owners * padded, width)


def kept_scale(owners, padded):
    own = K // owners
    scale = np.full((2, K), 2.0)
    scale[:, 0] = 1.0
    out = np.ones((owners, padded))
    out[:, : 2 * own] = scale.reshape(2, owners, own).transpose(1, 0, 2).reshape(owners, 2 * own)
    return out.reshape(owners * padded, 1)


def lat_table(length):
    first = np.arange(length)
    phase = (first[:, None] * first[None, :] % length) * (2.0 * math.pi / length)
    cosine = np.cos(phase) / math.sqrt(length)
    sine = np.sin(phase) / math.sqrt(length)
    return np.block([[cosine, sine], [-sine, cosine]])


def dot(left, right):
    return jnp.dot(left, right, preferred_element_type=F32)


def dot_rows(left, right):
    return lax.dot_general(left, right, (((0,), (0,)), ((), ())), preferred_element_type=F32)


def dot_cols(left, right):
    return lax.dot_general(left, right, (((1,), (1,)), ((), ())), preferred_element_type=F32)


def split(values):
    high = values.astype(BF16)
    return high, (values - high.astype(F32)).astype(BF16)


def columns_of(stats):
    count = stats.shape[0]
    high, rest = split(stats)
    mid, low = split(stats - high.astype(F32))
    stacked = jnp.concatenate([high.astype(F32), mid.astype(F32), low.astype(F32)], 0)
    pad = -stacked.shape[0] % 16
    if pad:
        stacked = jnp.concatenate([stacked, jnp.zeros((pad, stacked.shape[1]), F32)], 0)
    rows = stacked.shape[0]
    row = lax.broadcasted_iota(jnp.int32, (rows, count * 128), 0)
    lane = lax.broadcasted_iota(jnp.int32, (rows, count * 128), 1)
    pick = (row % count == lane // 128) & (row < 3 * count)
    wide = dot_rows(stacked.astype(BF16), pick.astype(F32).astype(BF16))
    return [wide[:, i * 128 : (i + 1) * 128] for i in range(count)]


def cot_lon_kernel(table_ref, cot_ref, out_ref):
    owners, blocks, rows, padded, _ = out_ref.shape
    for r in range(rows):
        result = dot(table_ref[...], cot_ref[0, r])
        for b in range(blocks):
            out_ref[:, b, r] = result[:, b * BS : (b + 1) * BS].reshape(owners, padded, BS)


def input_lon_kernel(table_ref, in_ref, stat_ref, gain_ref, *out_refs):
    tall = table_ref.shape[0] // 2
    for r in range(in_ref.shape[1]):
        mean, rstd = columns_of(stat_ref[r])
        at = 0
        for out_ref in out_refs:
            owners, blocks, _, padded, _ = out_ref.shape
            pieces = []
            for b in range(at, at + blocks):
                lanes = slice(b * BS, (b + 1) * BS)
                values = in_ref[0, r, :, lanes].astype(F32)
                pieces.append((values - mean) * rstd * gain_ref[:, lanes])
            at += blocks
            high, low = split(jnp.concatenate(pieces, 1))
            both = dot(table_ref[...], high)
            result = both[:tall] + both[tall:] + dot(table_ref[:tall], low)
            for b in range(blocks):
                out_ref[:, b, r] = result[:, b * BS : (b + 1) * BS].reshape(owners, padded, BS)


def mixer_kernel(
    own,
    group,
    fwd_high_ref,
    fwd_low_ref,
    inv_high_ref,
    inv_low_ref,
    w_one_ref,
    w_one_t_ref,
    w_two_ref,
    w_two_t_ref,
    bias_ref,
    shift_ref,
    x_ref,
    c_ref,
    grad_ref,
    sums_ref,
    x_scr,
    c_scr,
    high_scr,
    low_scr,
    spec_scr,
    hid_scr,
    two_scr,
    pre_scr,
    gain_scr,
):
    sources, _, span, _ = x_ref.shape
    length = fwd_high_ref.shape[0] // 2
    padded = sources * span // length
    steps = own // group
    for s in range(sources):
        x_scr[s * span : (s + 1) * span] = x_ref[s, 0]
        c_scr[s * span : (s + 1) * span] = c_ref[s, 0]
    for k in range(own):
        step, place = divmod(k, group)
        for which, scr in enumerate((x_scr, c_scr)):
            lanes = slice((which * group + place) * BS, (which * group + place + 1) * BS)
            for part in range(2):
                values = scr[pl.ds(part * own + k, length, stride=padded), :]
                rows = slice(part * length, (part + 1) * length)
                high, low = split(values)
                high_scr[step, rows, lanes] = high
                low_scr[step, rows, lanes] = low
    gain_scr[...] = jnp.zeros_like(gain_scr)
    w_one = w_one_ref[0]
    w_two = w_two_ref[0]
    first = lax.broadcasted_iota(jnp.int32, (group * length, 1), 0) == 0

    def gather(full, which):
        rows = []
        for place in range(group):
            at = (which * group + place) * BS
            re = full[:length, at : at + BS]
            im = full[length:, at : at + BS]
            rows.append(jnp.concatenate([re, im], 1))
        return jnp.concatenate(rows, 0)

    def body(step, carry):
        high = high_scr[step]
        low = low_scr[step]
        full = dot(fwd_high_ref[...], high) + dot(fwd_high_ref[...], low)
        full = full + dot(fwd_low_ref[...], high)
        plain = gather(full, 0)
        cot = gather(full, 1)
        at = pl.ds(pl.multiple_of(step * (group * length), group * length), group * length)
        is_first = jnp.where(first & (step == 0), 1.0, 0.0)
        spec = (plain + is_first * shift_ref[0, 0:1]).astype(BF16)
        pre_one = dot(spec, w_one) + bias_ref[0, 0:1]
        act, slope = gelu_parts(pre_one)
        hid = act.astype(BF16)
        pre_two = dot(hid, w_two) + bias_ref[0, 1:2]
        grad_two = (cot * shrink_slope(pre_two)).astype(BF16)
        grad_pre = (dot(grad_two, w_two_t_ref[0]) * slope).astype(BF16)
        grad_spec = dot(grad_pre, w_one_t_ref[0])
        spec_scr[at] = spec
        hid_scr[at] = hid
        two_scr[at] = grad_two
        pre_scr[at] = grad_pre
        gain_scr[0:1] += jnp.sum(grad_spec * plain, 0, keepdims=True)
        gain_scr[1:2] += jnp.sum(grad_two.astype(F32), 0, keepdims=True)
        gain_scr[2:3] += jnp.sum(grad_pre.astype(F32), 0, keepdims=True)
        gain_scr[3:4] += jnp.sum(grad_spec * is_first, 0, keepdims=True)
        for place in range(group):
            piece = grad_spec[place * length : (place + 1) * length]
            stacked = jnp.concatenate([piece[:, :BS], piece[:, BS:]], 0)
            grad_high, grad_low = split(stacked)
            high_scr[step, :, place * BS : (place + 1) * BS] = grad_high
            low_scr[step, :, place * BS : (place + 1) * BS] = grad_low
        return carry

    lax.fori_loop(0, steps, body, 0)
    for step in range(steps):
        high = high_scr[step, :, : group * BS]
        low = low_scr[step, :, : group * BS]
        lon = dot(inv_high_ref[...], high) + dot(inv_high_ref[...], low)
        lon = lon + dot(inv_low_ref[...], high)
        for place in range(group):
            k = step * group + place
            for part in range(2):
                piece = lon[part * length : (part + 1) * length, place * BS : (place + 1) * BS]
                x_scr[pl.ds(part * own + k, length, stride=padded), :] = piece
    for k in range(2 * own, padded):
        x_scr[pl.ds(k, length, stride=padded), :] = jnp.zeros((length, BS), F32)
    for s in range(sources):
        grad_ref[s, 0] = x_scr[s * span : (s + 1) * span]
    for i, (left, right) in enumerate(((spec_scr, pre_scr), (hid_scr, two_scr))):
        square = dot_rows(left[...], right[...])
        sums_ref[0, 2 * i * BS : (2 * i + 1) * BS] = square[:BS, :BS] + square[BS:, BS:]
        sums_ref[0, (2 * i + 1) * BS : (2 * i + 2) * BS] = square[:BS, BS:] - square[BS:, :BS]
    total = gain_scr[...]
    sums_ref[0, 4 * BS : 4 * BS + 8] = jnp.concatenate(
        [
            total[2:3, :BS],
            total[2:3, BS:],
            total[1:2, :BS],
            total[1:2, BS:],
            total[0:1, :BS] + total[0:1, BS:],
            total[3:4, :BS] * shift_ref[0, 1:2, :BS],
            jnp.zeros((2, BS), F32),
        ],
        0,
    )


def lon_back_kernel(
    offset, carry_in, table_ref, grad_ref, in_ref, cot_ref, stat_ref, gain_ref, *refs
):
    if carry_in:
        before_ref, out_ref, sums_ref = refs
    else:
        out_ref, sums_ref = refs
    sources, blocks, rows, padded, _ = grad_ref.shape
    ones = jnp.ones((16, BS), BF16)
    for r in range(rows):
        mean, rstd = columns_of(stat_ref[r])
        pieces = [
            grad_ref[:, b, r].reshape(sources * padded, BS).astype(BF16) for b in range(blocks)
        ]
        mixed = dot(table_ref[...], jnp.concatenate(pieces, 1))
        grads = jnp.zeros((in_ref.shape[2], BS), F32)
        products = jnp.zeros((in_ref.shape[2], BS), F32)
        for b in range(blocks):
            lanes = slice((offset + b) * BS, (offset + b + 1) * BS)
            grad = mixed[:, b * BS : (b + 1) * BS] * gain_ref[:, lanes]
            values = in_ref[0, r, :, b * BS : (b + 1) * BS].astype(F32)
            cot = cot_ref[0, r, :, b * BS : (b + 1) * BS].astype(F32)
            out_ref[r, :, b * BS : (b + 1) * BS] = cot + rstd * grad
            grads = grads + grad
            products = products + grad * ((values - mean) * rstd)
        both = [dot_cols(ones, values.astype(BF16))[0:1] for values in (grads, products)]
        sums = jnp.concatenate(both, 0)
        if carry_in:
            sums = sums + before_ref[r]
        sums_ref[r] = sums


def finish_kernel(chunks, channels, *refs):
    in_ref, stat_ref, sums_ref = refs[:3]
    base_refs = refs[3 : 3 + len(chunks)]
    out_ref = refs[-1]
    for r in range(in_ref.shape[1]):
        mean, rstd = stat_ref[r, 0:1], stat_ref[r, 1:2]
        slope = rstd * rstd * (sums_ref[r, 1:2] / channels)
        level = rstd * (sums_ref[r, 0:1] / channels) - mean * slope
        level, slope = columns_of(jnp.concatenate([level, slope], 0))
        at = 0
        for base_ref, blocks in zip(base_refs, chunks):
            for b in range(blocks):
                lanes = slice(at * BS, (at + 1) * BS)
                values = in_ref[0, r, :, lanes].astype(F32)
                base = base_ref[r, :, b * BS : (b + 1) * BS]
                out_ref[0, r, :, lanes] = (base - level - slope * values).astype(BF16)
                at += 1


def xor_permute(piece, axis, bit):
    size = lax.axis_size(axis)
    return lax.ppermute(piece, axis, [(i, i ^ bit) for i in range(size)])


def sum_small(piece, axis):
    bit = 1
    while bit < lax.axis_size(axis):
        piece = piece + xor_permute(piece, axis, bit)
        bit *= 2
    return piece


def scatter_sum(piece, axis):
    size = lax.axis_size(axis)
    index = lax.axis_index(axis)
    low_bits = (size.bit_length() - 1) // 2
    for i in range(low_bits):
        half = piece.shape[0] // 2
        low, high = piece[:half], piece[half:]
        upper = (index & (1 << i)) != 0
        piece = jnp.where(upper, high, low) + xor_permute(
            jnp.where(upper, low, high), axis, 1 << i
        )
    far = size >> low_bits
    parts = piece.reshape(far, -1, piece.shape[-1])
    place = index >> low_bits
    total = lax.dynamic_index_in_dim(parts, place, 0, False)
    for d in range(1, far):
        part = lax.dynamic_index_in_dim(parts, place ^ d, 0, False)
        total = total + xor_permute(part, axis, d << low_bits)
    return total


def gather_sum(total, axis):
    size = lax.axis_size(axis)
    index = lax.axis_index(axis)
    low_bits = (size.bit_length() - 1) // 2
    far = size >> low_bits
    place = index >> low_bits
    parts = [total] + [xor_permute(total, axis, d << low_bits) for d in range(1, far)]
    parts = jnp.stack(parts)
    piece = jnp.concatenate(
        [lax.dynamic_index_in_dim(parts, place ^ d, 0, False) for d in range(far)], 0
    )
    for i in reversed(range(low_bits)):
        other = xor_permute(piece, axis, 1 << i)
        upper = (index & (1 << i)) != 0
        piece = jnp.concatenate(
            [jnp.where(upper, other, piece), jnp.where(upper, piece, other)], 0
        )
    return piece


def divisor(count, limit):
    return max(n for n in range(1, limit + 1) if count % n == 0)


def params():
    return pltpu.CompilerParams(vmem_limit_bytes=VMEM_LIMIT)


def whole(shape):
    return pl.BlockSpec(shape, lambda *_: (0,) * len(shape))


def cost(flops, moved, transcendentals=0):
    return pl.CostEstimate(
        flops=int(flops), bytes_accessed=int(moved), transcendentals=int(transcendentals)
    )


def on_device(
    inputs, cotangent, ln_gain, ln_shift, first_weight, first_bias, second_weight, second_bias
):
    batch, rows, width, local = inputs.shape
    blocks = local // BS
    owners = lax.axis_size("row")
    height = rows * owners
    own = K // owners
    padded = -(-2 * own // 8) * 8
    tall = owners * padded
    group = 2 if own % 2 == 0 else 1
    total_chan = local * lax.axis_size("chan")
    chunks = (blocks - 1, 1) if blocks > 1 else (1,)
    starts = [sum(chunks[:i]) for i in range(len(chunks))]
    gain = ln_gain.reshape(1, local)

    lon = lon_table(width, owners, padded)
    lon_high, lon_low = high_low(lon)
    lon_both = np.concatenate([lon_high, lon_low], 0)
    cot_high, _ = high_low(lon * kept_scale(owners, padded))
    back = np.ascontiguousarray(lon.T).astype(np.float32).astype(jnp.bfloat16)
    fwd_high, fwd_low = high_low(lat_table(height))
    inv_high, inv_low = high_low(lat_table(height).T)

    def exchange(piece):
        return lax.all_to_all(piece, "row", split_axis=0, concat_axis=0, tiled=True)

    few = divisor(rows, 2)
    many = divisor(rows, 4)

    def row_spec(step):
        return pl.BlockSpec((1, step, width, local), lambda h: (0, h, 0, 0))

    def stat_spec(step):
        return pl.BlockSpec((step, 2, width), lambda h: (h, 0, 0))

    def grad_spec(step, count):
        return pl.BlockSpec((step, width, count * BS), lambda h: (h, 0, 0))

    def spectrum_spec(step, count):
        return pl.BlockSpec((owners, count, step, padded, BS), lambda h: (0, 0, h, 0, 0))

    def spectrum_shape(count):
        return jax.ShapeDtypeStruct((owners, count, rows, padded, BS), F32)

    lon_flops = 2 * rows * tall * width * local
    cot_lon = pl.pallas_call(
        cot_lon_kernel,
        grid=(rows // few,),
        in_specs=[whole((tall, width)), row_spec(few)],
        out_specs=spectrum_spec(few, blocks),
        out_shape=spectrum_shape(blocks),
        compiler_params=params(),
        cost_estimate=cost(lon_flops, rows * local * (2 * width + 4 * tall)),
        name="cot_lon",
    )(cot_high, cotangent)
    cot_lon, inputs = lax.optimization_barrier((cot_lon, inputs))
    cot_spec = exchange(cot_lon)

    values = inputs.astype(F32)
    mean = lax.psum(jnp.sum(values, -1), "chan") / total_chan
    centred = values - mean[..., None]
    variance = lax.psum(jnp.sum(centred * centred, -1), "chan") / total_chan
    stats = jnp.stack([mean[0], lax.rsqrt(variance + EPS)[0]], 1)

    input_lon = pl.pallas_call(
        input_lon_kernel,
        grid=(rows // few,),
        in_specs=[whole((2 * tall, width)), row_spec(few), stat_spec(few), whole((1, local))],
        out_specs=[spectrum_spec(few, count) for count in chunks],
        out_shape=[spectrum_shape(count) for count in chunks],
        compiler_params=params(),
        cost_estimate=cost(3 * lon_flops, rows * local * (2 * width + 4 * tall)),
        name="input_lon",
    )(lon_both, inputs, stats, gain)
    first_piece, cot_spec = lax.optimization_barrier((input_lon[0], cot_spec))
    input_lon = [first_piece, *input_lon[1:]]

    def square(weight):
        re, im = weight.reshape(2, blocks, BS, BS)
        return jnp.concatenate(
            [jnp.concatenate([re, im], 2), jnp.concatenate([-im, re], 2)], 1
        )

    w_one = square(first_weight)
    w_two = square(second_weight)
    w_one_t = w_one.swapaxes(1, 2)
    w_two_t = w_two.swapaxes(1, 2)
    bias = jnp.stack([first_bias, second_bias]).reshape(2, 2, blocks, BS)
    bias = bias.transpose(2, 0, 1, 3).reshape(blocks, 2, 2 * BS)
    is_origin = (lax.axis_index("row") == 0).astype(F32)
    shift = (ln_shift * (math.sqrt(height * width) * is_origin)).reshape(blocks, 1, BS)
    shift = jnp.concatenate([shift, jnp.zeros_like(shift)], 2)
    shift = jnp.concatenate([shift, jnp.full_like(shift, is_origin)], 1)

    span = rows * padded
    mat = pl.BlockSpec((1, 2 * BS, 2 * BS), lambda b: (b, 0, 0))

    def mix(index, x_spec):
        count = chunks[index]
        start = starts[index]

        def at(shape):
            return pl.BlockSpec(shape, lambda b: (b + start,) + (0,) * (len(shape) - 1))

        tokens = own * height
        flops = 2 * count * tokens * 2 * BS * (3 * 2 * height * 3 + 6 * 2 * BS)
        return pl.pallas_call(
            functools.partial(mixer_kernel, own, group),
            grid=(count,),
            in_specs=[whole((2 * height, 2 * height))] * 4
            + [at((1, 2 * BS, 2 * BS))] * 4
            + [
                at((1, 2, 2 * BS)),
                at((1, 2, 2 * BS)),
                pl.BlockSpec((owners, 1, span, BS), lambda b: (0, b, 0, 0)),
                pl.BlockSpec((owners, 1, span, BS), lambda b: (0, b + start, 0, 0)),
            ],
            out_specs=[
                pl.BlockSpec((owners, 1, span, BS), lambda b: (0, b, 0, 0)),
                pl.BlockSpec((1, 4 * BS + 8, BS), lambda b: (b, 0, 0)),
            ],
            out_shape=[
                jax.ShapeDtypeStruct((owners, count, span, BS), F32),
                jax.ShapeDtypeStruct((count, 4 * BS + 8, BS), F32),
            ],
            scratch_shapes=[
                pltpu.VMEM((owners * span, BS), F32),
                pltpu.VMEM((owners * span, BS), F32),
                pltpu.VMEM((own // group, 2 * height, 2 * group * BS), BF16),
                pltpu.VMEM((own // group, 2 * height, 2 * group * BS), BF16),
                pltpu.VMEM((tokens, 2 * BS), BF16),
                pltpu.VMEM((tokens, 2 * BS), BF16),
                pltpu.VMEM((tokens, 2 * BS), BF16),
                pltpu.VMEM((tokens, 2 * BS), BF16),
                pltpu.VMEM((8, 2 * BS), F32),
            ],
            compiler_params=params(),
            cost_estimate=cost(flops, 3 * count * owners * span * BS * 4, 4 * tokens * BS * count),
            name=f"mixer_{index}",
        )(
            fwd_high,
            fwd_low,
            inv_high,
            inv_low,
            w_one,
            w_one_t,
            w_two,
            w_two_t,
            bias,
            shift,
            x_spec.reshape(owners, count, span, BS),
            cot_spec.reshape(owners, blocks, span, BS),
        )

    mixed = [mix(i, exchange(piece)) for i, piece in enumerate(input_lon)]
    param_rows = 4 * BS + 8
    unit = 8 * owners // math.gcd(8 * owners, blocks)
    tail = -(blocks * param_rows) % (unit * blocks)
    flat = jnp.concatenate([m[1].reshape(-1, BS) for m in mixed], 0)
    flat = jnp.pad(flat, ((0, tail), (0, 0)))
    param_part = scatter_sum(flat, "row")

    grads = []
    sums = None
    for index, count in enumerate(chunks):
        start = starts[index]
        piece = mixed[index][0].reshape(owners, count, rows, padded, BS)
        carry_in = sums is not None
        if index == len(chunks) - 1 and carry_in:
            piece, param_part = lax.optimization_barrier((piece, param_part))
        piece = exchange(piece)
        in_spec = pl.BlockSpec(
            (1, many, width, count * BS), lambda h, at=start // count: (0, h, 0, at)
        )
        grad, sums = pl.pallas_call(
            functools.partial(lon_back_kernel, start, carry_in),
            grid=(rows // many,),
            in_specs=[
                whole((width, tall)),
                spectrum_spec(many, count),
                in_spec,
                in_spec,
                stat_spec(many),
                whole((1, local)),
            ]
            + [stat_spec(many)] * carry_in,
            out_specs=[grad_spec(many, count), stat_spec(many)],
            out_shape=[
                jax.ShapeDtypeStruct((rows, width, count * BS), F32),
                jax.ShapeDtypeStruct((rows, 2, width), F32),
            ],
            compiler_params=params(),
            cost_estimate=cost(
                2 * rows * tall * width * count * BS, rows * count * BS * (6 * width + 4 * tall)
            ),
            name=f"lon_back_{index}",
        )(back, piece, inputs, cotangent, stats, gain, *([sums] * carry_in))
        grads.append(grad)

    input_grad = pl.pallas_call(
        functools.partial(finish_kernel, chunks, total_chan),
        grid=(rows // few,),
        in_specs=[row_spec(few), stat_spec(few), stat_spec(few)]
        + [grad_spec(few, count) for count in chunks],
        out_specs=row_spec(few),
        out_shape=jax.ShapeDtypeStruct(inputs.shape, BF16),
        compiler_params=params(),
        cost_estimate=cost(10 * rows * width * local, rows * width * local * 10),
        name="finish",
    )(inputs, stats, sum_small(sums, "chan"), *grads)

    param_sums = gather_sum(param_part, "row")[: blocks * param_rows]
    param_sums = param_sums.reshape(blocks, param_rows, BS)
    spec_scale = 1.0 / math.sqrt(batch * height * K)
    dw = param_sums[:, : 4 * BS].reshape(blocks, 2, 2, BS, BS).transpose(1, 2, 0, 3, 4) * spec_scale
    db = param_sums[:, 4 * BS : 4 * BS + 4].reshape(blocks, 2, 2, BS).transpose(1, 2, 0, 3)
    db = db * spec_scale
    ln_scale = 1.0 / math.sqrt(batch * height * width)
    gain_grad = param_sums[:, 4 * BS + 4].reshape(local) / ln_gain * ln_scale
    return (
        input_grad,
        dw[0].reshape(2, local, BS),
        db[0].reshape(2, local),
        dw[1].reshape(2, local, BS),
        db[1].reshape(2, local),
        gain_grad,
        param_sums[:, 4 * BS + 5].reshape(local),
    )


def solution(mesh):
    placed = (
        P(None, "row", None, "chan"),
        P(None, "row", None, "chan"),
        P("chan"),
        P("chan"),
        P(None, "chan", None),
        P(None, "chan"),
        P(None, "chan", None),
        P(None, "chan"),
    )
    return jax.shard_map(
        on_device,
        mesh=mesh,
        in_specs=placed,
        out_specs=(
            P(None, "row", None, "chan"),
            P(None, "chan", None),
            P(None, "chan"),
            P(None, "chan", None),
            P(None, "chan"),
            P("chan"),
            P("chan"),
        ),
        check_vma=False,
    )
```

```python
import functools
import math

import jax
import jax.numpy as jnp
import numpy as np
from jax import lax
from jax.experimental import pallas as pl
from jax.experimental.pallas import tpu as pltpu
from jax.sharding import PartitionSpec as P

K = 192
BS = 128
EPS = 1e-05
LAMBDA = 0.01
ROOT_TWO_PI = math.sqrt(2.0 / math.pi)
BF16 = jnp.bfloat16
F32 = jnp.float32
VMEM_LIMIT = 60 * 1024 * 1024


def gelu_parts(values):
    inner = ROOT_TWO_PI * (values + 0.044715 * values * values * values)
    tangent = jnp.tanh(inner)
    output = 0.5 * values * (1.0 + tangent)
    slope = 0.5 * (1.0 + tangent) + 0.5 * values * (1.0 - tangent * tangent) * ROOT_TWO_PI * (
        1.0 + 3.0 * 0.044715 * values * values
    )
    return (output, slope)


def shrink_slope(values):
    tangent = jnp.tanh(values / LAMBDA)
    return tangent * tangent


def high_low(table):
    high = np.asarray(table, np.float32).astype(jnp.bfloat16)
    low = (np.asarray(table, np.float32) - high.astype(np.float32)).astype(jnp.bfloat16)
    return high, low


def lon_table(width, owners, padded):
    own = K // owners
    number = np.arange(K)[:, None]
    column = np.arange(width)[None, :]
    phase = (number * column % width) * (2.0 * math.pi / width)
    parts = np.stack([np.cos(phase), -np.sin(phase)]) / math.sqrt(width)
    parts = parts.reshape(2, owners, own, width).transpose(1, 0, 2, 3)
    table = np.zeros((owners, padded, width))
    table[:, : 2 * own] = parts.reshape(owners, 2 * own, width)
    return table.reshape(owners * padded, width)


def kept_scale(owners, padded):
    own = K // owners
    scale = np.full((2, K), 2.0)
    scale[:, 0] = 1.0
    out = np.ones((owners, padded))
    out[:, : 2 * own] = scale.reshape(2, owners, own).transpose(1, 0, 2).reshape(owners, 2 * own)
    return out.reshape(owners * padded, 1)


def lat_table(length):
    first = np.arange(length)
    phase = (first[:, None] * first[None, :] % length) * (2.0 * math.pi / length)
    cosine = np.cos(phase) / math.sqrt(length)
    sine = np.sin(phase) / math.sqrt(length)
    return np.block([[cosine, sine], [-sine, cosine]])


def dot(left, right):
    return jnp.dot(left, right, preferred_element_type=F32)


def dot_rows(left, right):
    return lax.dot_general(left, right, (((0,), (0,)), ((), ())), preferred_element_type=F32)


def dot_cols(left, right):
    return lax.dot_general(left, right, (((1,), (1,)), ((), ())), preferred_element_type=F32)


def split(values):
    high = values.astype(BF16)
    return high, (values - high.astype(F32)).astype(BF16)


def columns_of(stats):
    count = stats.shape[0]
    high, rest = split(stats)
    mid, low = split(stats - high.astype(F32))
    stacked = jnp.concatenate([high.astype(F32), mid.astype(F32), low.astype(F32)], 0)
    pad = -stacked.shape[0] % 16
    if pad:
        stacked = jnp.concatenate([stacked, jnp.zeros((pad, stacked.shape[1]), F32)], 0)
    rows = stacked.shape[0]
    row = lax.broadcasted_iota(jnp.int32, (rows, count * 128), 0)
    lane = lax.broadcasted_iota(jnp.int32, (rows, count * 128), 1)
    pick = (row % count == lane // 128) & (row < 3 * count)
    wide = dot_rows(stacked.astype(BF16), pick.astype(F32).astype(BF16))
    return [wide[:, i * 128 : (i + 1) * 128] for i in range(count)]


def cot_lon_kernel(table_ref, cot_ref, out_ref):
    owners, blocks, rows, padded, _ = out_ref.shape
    for r in range(rows):
        result = dot(table_ref[...], cot_ref[0, r])
        for b in range(blocks):
            out_ref[:, b, r] = result[:, b * BS : (b + 1) * BS].reshape(owners, padded, BS)


def input_lon_kernel(table_ref, in_ref, stat_ref, gain_ref, *out_refs):
    tall = table_ref.shape[0] // 2
    for r in range(in_ref.shape[1]):
        mean, rstd = columns_of(stat_ref[r])
        at = 0
        for out_ref in out_refs:
            owners, blocks, _, padded, _ = out_ref.shape
            pieces = []
            for b in range(at, at + blocks):
                lanes = slice(b * BS, (b + 1) * BS)
                values = in_ref[0, r, :, lanes].astype(F32)
                pieces.append((values - mean) * rstd * gain_ref[:, lanes])
            at += blocks
            high, low = split(jnp.concatenate(pieces, 1))
            both = dot(table_ref[...], high)
            result = both[:tall] + both[tall:] + dot(table_ref[:tall], low)
            for b in range(blocks):
                out_ref[:, b, r] = result[:, b * BS : (b + 1) * BS].reshape(owners, padded, BS)


def mixer_kernel(
    own,
    group,
    fwd_high_ref,
    fwd_low_ref,
    inv_high_ref,
    inv_low_ref,
    w_one_ref,
    w_one_t_ref,
    w_two_ref,
    w_two_t_ref,
    bias_ref,
    shift_ref,
    x_ref,
    c_ref,
    grad_ref,
    sums_ref,
    x_scr,
    c_scr,
    high_scr,
    low_scr,
    spec_scr,
    hid_scr,
    two_scr,
    pre_scr,
    gain_scr,
):
    sources, _, span, _ = x_ref.shape
    length = fwd_high_ref.shape[0] // 2
    padded = sources * span // length
    steps = own // group
    for s in range(sources):
        x_scr[s * span : (s + 1) * span] = x_ref[s, 0]
        c_scr[s * span : (s + 1) * span] = c_ref[s, 0]
    for k in range(own):
        step, place = divmod(k, group)
        for which, scr in enumerate((x_scr, c_scr)):
            lanes = slice((which * group + place) * BS, (which * group + place + 1) * BS)
            for part in range(2):
                values = scr[pl.ds(part * own + k, length, stride=padded), :]
                rows = slice(part * length, (part + 1) * length)
                high, low = split(values)
                high_scr[step, rows, lanes] = high
                low_scr[step, rows, lanes] = low
    gain_scr[...] = jnp.zeros_like(gain_scr)
    w_one = w_one_ref[0]
    w_two = w_two_ref[0]
    first = lax.broadcasted_iota(jnp.int32, (group * length, 1), 0) == 0

    def gather(full, which):
        rows = []
        for place in range(group):
            at = (which * group + place) * BS
            re = full[:length, at : at + BS]
            im = full[length:, at : at + BS]
            rows.append(jnp.concatenate([re, im], 1))
        return jnp.concatenate(rows, 0)

    def body(step, carry):
        high = high_scr[step]
        low = low_scr[step]
        full = dot(fwd_high_ref[...], high) + dot(fwd_high_ref[...], low)
        full = full + dot(fwd_low_ref[...], high)
        plain = gather(full, 0)
        cot = gather(full, 1)
        at = pl.ds(pl.multiple_of(step * (group * length), group * length), group * length)
        is_first = jnp.where(first & (step == 0), 1.0, 0.0)
        spec = (plain + is_first * shift_ref[0, 0:1]).astype(BF16)
        pre_one = dot(spec, w_one) + bias_ref[0, 0:1]
        act, slope = gelu_parts(pre_one)
        hid = act.astype(BF16)
        pre_two = dot(hid, w_two) + bias_ref[0, 1:2]
        grad_two = (cot * shrink_slope(pre_two)).astype(BF16)
        grad_pre = (dot(grad_two, w_two_t_ref[0]) * slope).astype(BF16)
        grad_spec = dot(grad_pre, w_one_t_ref[0])
        spec_scr[at] = spec
        hid_scr[at] = hid
        two_scr[at] = grad_two
        pre_scr[at] = grad_pre
        gain_scr[0:1] += jnp.sum(grad_spec * plain, 0, keepdims=True)
        gain_scr[1:2] += jnp.sum(grad_two.astype(F32), 0, keepdims=True)
        gain_scr[2:3] += jnp.sum(grad_pre.astype(F32), 0, keepdims=True)
        gain_scr[3:4] += jnp.sum(grad_spec * is_first, 0, keepdims=True)
        for place in range(group):
            piece = grad_spec[place * length : (place + 1) * length]
            stacked = jnp.concatenate([piece[:, :BS], piece[:, BS:]], 0)
            grad_high, grad_low = split(stacked)
            high_scr[step, :, place * BS : (place + 1) * BS] = grad_high
            low_scr[step, :, place * BS : (place + 1) * BS] = grad_low
        return carry

    lax.fori_loop(0, steps, body, 0)
    for step in range(steps):
        high = high_scr[step, :, : group * BS]
        low = low_scr[step, :, : group * BS]
        lon = dot(inv_high_ref[...], high) + dot(inv_high_ref[...], low)
        lon = lon + dot(inv_low_ref[...], high)
        for place in range(group):
            k = step * group + place
            for part in range(2):
                piece = lon[part * length : (part + 1) * length, place * BS : (place + 1) * BS]
                x_scr[pl.ds(part * own + k, length, stride=padded), :] = piece
    for k in range(2 * own, padded):
        x_scr[pl.ds(k, length, stride=padded), :] = jnp.zeros((length, BS), F32)
    for s in range(sources):
        grad_ref[s, 0] = x_scr[s * span : (s + 1) * span]
    for i, (left, right) in enumerate(((spec_scr, pre_scr), (hid_scr, two_scr))):
        square = dot_rows(left[...], right[...])
        sums_ref[0, 2 * i * BS : (2 * i + 1) * BS] = square[:BS, :BS] + square[BS:, BS:]
        sums_ref[0, (2 * i + 1) * BS : (2 * i + 2) * BS] = square[:BS, BS:] - square[BS:, :BS]
    total = gain_scr[...]
    sums_ref[0, 4 * BS : 4 * BS + 8] = jnp.concatenate(
        [
            total[2:3, :BS],
            total[2:3, BS:],
            total[1:2, :BS],
            total[1:2, BS:],
            total[0:1, :BS] + total[0:1, BS:],
            total[3:4, :BS] * shift_ref[0, 1:2, :BS],
            jnp.zeros((2, BS), F32),
        ],
        0,
    )


def lon_back_kernel(
    offset, carry_in, table_ref, grad_ref, in_ref, cot_ref, stat_ref, gain_ref, *refs
):
    if carry_in:
        before_ref, out_ref, sums_ref = refs
    else:
        out_ref, sums_ref = refs
    sources, blocks, rows, padded, _ = grad_ref.shape
    ones = jnp.ones((16, BS), BF16)
    for r in range(rows):
        mean, rstd = columns_of(stat_ref[r])
        pieces = [
            grad_ref[:, b, r].reshape(sources * padded, BS).astype(BF16) for b in range(blocks)
        ]
        mixed = dot(table_ref[...], jnp.concatenate(pieces, 1))
        grads = jnp.zeros((in_ref.shape[2], BS), F32)
        products = jnp.zeros((in_ref.shape[2], BS), F32)
        for b in range(blocks):
            lanes = slice((offset + b) * BS, (offset + b + 1) * BS)
            grad = mixed[:, b * BS : (b + 1) * BS] * gain_ref[:, lanes]
            values = in_ref[0, r, :, b * BS : (b + 1) * BS].astype(F32)
            cot = cot_ref[0, r, :, b * BS : (b + 1) * BS].astype(F32)
            out_ref[r, :, b * BS : (b + 1) * BS] = (cot + rstd * grad).astype(BF16)
            grads = grads + grad
            products = products + grad * ((values - mean) * rstd)
        both = [dot_cols(ones, values.astype(BF16))[0:1] for values in (grads, products)]
        sums = jnp.concatenate(both, 0)
        if carry_in:
            sums = sums + before_ref[r]
        sums_ref[r] = sums


def finish_kernel(chunks, channels, *refs):
    in_ref, stat_ref, sums_ref, more_ref = refs[:4]
    base_refs = refs[4 : 4 + len(chunks)]
    out_ref = refs[-1]
    for r in range(in_ref.shape[1]):
        mean, rstd = stat_ref[r, 0:1], stat_ref[r, 1:2]
        sums = (sums_ref[r] + more_ref[r]) / channels
        slope = rstd * rstd * sums[1:2]
        level = rstd * sums[0:1] - mean * slope
        level, slope = columns_of(jnp.concatenate([level, slope], 0))
        at = 0
        for base_ref, blocks in zip(base_refs, chunks):
            for b in range(blocks):
                lanes = slice(at * BS, (at + 1) * BS)
                values = in_ref[0, r, :, lanes].astype(F32)
                base = base_ref[r, :, b * BS : (b + 1) * BS].astype(F32)
                out_ref[0, r, :, lanes] = (base - level - slope * values).astype(BF16)
                at += 1


def xor_permute(piece, axis, bit):
    size = lax.axis_size(axis)
    return lax.ppermute(piece, axis, [(i, i ^ bit) for i in range(size)])


def pair_small(piece, axis):
    other = jnp.zeros_like(piece)
    bit = 1
    while bit < lax.axis_size(axis):
        piece = piece + other if bit > 1 else piece
        other = xor_permute(piece, axis, bit)
        bit *= 2
    return piece, other


def halve(piece, axis):
    index = lax.axis_index(axis)
    for i in range(low_bits(axis)):
        half = piece.shape[0] // 2
        low, high = piece[:half], piece[half:]
        upper = (index & (1 << i)) != 0
        piece = jnp.where(upper, high, low) + xor_permute(
            jnp.where(upper, low, high), axis, 1 << i
        )
    return piece


def low_bits(axis):
    return (lax.axis_size(axis).bit_length() - 1) // 2


def scatter_far(piece, axis):
    low = low_bits(axis)
    far = lax.axis_size(axis) >> low
    parts = piece.reshape(far, -1, piece.shape[-1])
    place = lax.axis_index(axis) >> low
    total = lax.dynamic_index_in_dim(parts, place, 0, False)
    others = [lax.dynamic_index_in_dim(parts, place ^ d, 0, False) for d in range(1, far)]
    others = [xor_permute(part, axis, d << low) for d, part in enumerate(others, 1)]
    return total + others[0], others[1:]


def gather_far(total, axis):
    low = low_bits(axis)
    far = lax.axis_size(axis) >> low
    place = lax.axis_index(axis) >> low
    parts = [total] + [xor_permute(total, axis, d << low) for d in range(1, far)]
    parts = jnp.stack(parts)
    return jnp.concatenate(
        [lax.dynamic_index_in_dim(parts, place ^ d, 0, False) for d in range(far)], 0
    )


def double(piece, axis, bit):
    other = xor_permute(piece, axis, bit)
    upper = (lax.axis_index(axis) & bit) != 0
    return jnp.concatenate([jnp.where(upper, other, piece), jnp.where(upper, piece, other)], 0)


def divisor(count, limit):
    return max(n for n in range(1, limit + 1) if count % n == 0)


def params():
    return pltpu.CompilerParams(vmem_limit_bytes=VMEM_LIMIT)


def whole(shape):
    return pl.BlockSpec(shape, lambda *_: (0,) * len(shape))


def cost(flops, moved, transcendentals=0):
    return pl.CostEstimate(
        flops=int(flops), bytes_accessed=int(moved), transcendentals=int(transcendentals)
    )


def on_device(
    inputs, cotangent, ln_gain, ln_shift, first_weight, first_bias, second_weight, second_bias
):
    batch, rows, width, local = inputs.shape
    blocks = local // BS
    owners = lax.axis_size("row")
    height = rows * owners
    own = K // owners
    padded = -(-2 * own // 8) * 8
    tall = owners * padded
    group = 2 if own % 2 == 0 else 1
    total_chan = local * lax.axis_size("chan")
    chunks = (blocks - 1, 1) if blocks > 1 else (1,)
    starts = [sum(chunks[:i]) for i in range(len(chunks))]
    gain = ln_gain.reshape(1, local)

    lon = lon_table(width, owners, padded)
    lon_high, lon_low = high_low(lon)
    lon_both = np.concatenate([lon_high, lon_low], 0)
    cot_high, _ = high_low(lon * kept_scale(owners, padded))
    back = np.ascontiguousarray(lon.T).astype(np.float32).astype(jnp.bfloat16)
    fwd_high, fwd_low = high_low(lat_table(height))
    inv_high, inv_low = high_low(lat_table(height).T)

    def exchange(piece):
        return lax.all_to_all(piece, "row", split_axis=0, concat_axis=0, tiled=True)

    few = divisor(rows, 2)
    many = divisor(rows, 4)

    def row_spec(step):
        return pl.BlockSpec((1, step, width, local), lambda h: (0, h, 0, 0))

    def stat_spec(step):
        return pl.BlockSpec((step, 2, width), lambda h: (h, 0, 0))

    def grad_spec(step, count):
        return pl.BlockSpec((step, width, count * BS), lambda h: (h, 0, 0))

    def spectrum_spec(step, count):
        return pl.BlockSpec((owners, count, step, padded, BS), lambda h: (0, 0, h, 0, 0))

    def spectrum_shape(count):
        return jax.ShapeDtypeStruct((owners, count, rows, padded, BS), F32)

    lon_flops = 2 * rows * tall * width * local
    cot_lon = pl.pallas_call(
        cot_lon_kernel,
        grid=(rows // few,),
        in_specs=[whole((tall, width)), row_spec(few)],
        out_specs=spectrum_spec(few, blocks),
        out_shape=spectrum_shape(blocks),
        compiler_params=params(),
        cost_estimate=cost(lon_flops, rows * local * (2 * width + 4 * tall)),
        name="cot_lon",
    )(cot_high, cotangent)
    cot_lon, inputs = lax.optimization_barrier((cot_lon, inputs))
    cot_spec = exchange(cot_lon)

    values = inputs.astype(F32)
    mean = lax.psum(jnp.sum(values, -1), "chan") / total_chan
    centred = values - mean[..., None]
    variance = lax.psum(jnp.sum(centred * centred, -1), "chan") / total_chan
    stats = jnp.stack([mean[0], lax.rsqrt(variance + EPS)[0]], 1)

    input_lon = pl.pallas_call(
        input_lon_kernel,
        grid=(rows // few,),
        in_specs=[whole((2 * tall, width)), row_spec(few), stat_spec(few), whole((1, local))],
        out_specs=[spectrum_spec(few, count) for count in chunks],
        out_shape=[spectrum_shape(count) for count in chunks],
        compiler_params=params(),
        cost_estimate=cost(3 * lon_flops, rows * local * (2 * width + 4 * tall)),
        name="input_lon",
    )(lon_both, inputs, stats, gain)

    def square(weight):
        re, im = weight.reshape(2, blocks, BS, BS)
        return jnp.concatenate(
            [jnp.concatenate([re, im], 2), jnp.concatenate([-im, re], 2)], 1
        )

    w_one = square(first_weight)
    w_two = square(second_weight)
    w_one_t = w_one.swapaxes(1, 2)
    w_two_t = w_two.swapaxes(1, 2)
    bias = jnp.stack([first_bias, second_bias]).reshape(2, 2, blocks, BS)
    bias = bias.transpose(2, 0, 1, 3).reshape(blocks, 2, 2 * BS)
    is_origin = (lax.axis_index("row") == 0).astype(F32)
    shift = (ln_shift * (math.sqrt(height * width) * is_origin)).reshape(blocks, 1, BS)
    shift = jnp.concatenate([shift, jnp.zeros_like(shift)], 2)
    shift = jnp.concatenate([shift, jnp.full_like(shift, is_origin)], 1)

    weights = (w_one, w_one_t, w_two, w_two_t, bias, shift)
    first_piece, cot_spec, weights = lax.optimization_barrier((input_lon[0], cot_spec, weights))
    input_lon = [first_piece, *input_lon[1:]]

    span = rows * padded

    def mix(index, x_spec):
        count = chunks[index]
        start = starts[index]

        def at(shape):
            return pl.BlockSpec(shape, lambda b: (b + start,) + (0,) * (len(shape) - 1))

        tokens = own * height
        flops = 2 * count * tokens * 2 * BS * (3 * 2 * height * 3 + 6 * 2 * BS)
        return pl.pallas_call(
            functools.partial(mixer_kernel, own, group),
            grid=(count,),
            in_specs=[whole((2 * height, 2 * height))] * 4
            + [at((1, 2 * BS, 2 * BS))] * 4
            + [
                at((1, 2, 2 * BS)),
                at((1, 2, 2 * BS)),
                pl.BlockSpec((owners, 1, span, BS), lambda b: (0, b, 0, 0)),
                pl.BlockSpec((owners, 1, span, BS), lambda b: (0, b + start, 0, 0)),
            ],
            out_specs=[
                pl.BlockSpec((owners, 1, span, BS), lambda b: (0, b, 0, 0)),
                pl.BlockSpec((1, 4 * BS + 8, BS), lambda b: (b, 0, 0)),
            ],
            out_shape=[
                jax.ShapeDtypeStruct((owners, count, span, BS), F32),
                jax.ShapeDtypeStruct((count, 4 * BS + 8, BS), F32),
            ],
            scratch_shapes=[
                pltpu.VMEM((owners * span, BS), F32),
                pltpu.VMEM((owners * span, BS), F32),
                pltpu.VMEM((own // group, 2 * height, 2 * group * BS), BF16),
                pltpu.VMEM((own // group, 2 * height, 2 * group * BS), BF16),
                pltpu.VMEM((tokens, 2 * BS), BF16),
                pltpu.VMEM((tokens, 2 * BS), BF16),
                pltpu.VMEM((tokens, 2 * BS), BF16),
                pltpu.VMEM((tokens, 2 * BS), BF16),
                pltpu.VMEM((8, 2 * BS), F32),
            ],
            compiler_params=params(),
            cost_estimate=cost(flops, 3 * count * owners * span * BS * 4, 4 * tokens * BS * count),
            name=f"mixer_{index}",
        )(
            fwd_high,
            fwd_low,
            inv_high,
            inv_low,
            *weights,
            x_spec.reshape(owners, count, span, BS),
            cot_spec.reshape(owners, blocks, span, BS),
        )

    mixed = [mix(i, exchange(piece)) for i, piece in enumerate(input_lon)]
    param_rows = 4 * BS + 8
    unit = 8 * owners // math.gcd(8 * owners, blocks)
    tail = -(blocks * param_rows) % (unit * blocks)
    flat = jnp.concatenate([m[1].reshape(-1, BS) for m in mixed], 0)
    flat = jnp.pad(flat, ((0, tail), (0, 0)))
    param_part, far_parts = scatter_far(halve(flat, "row"), "row")

    grads = []
    sums = None
    for index, count in enumerate(chunks):
        start = starts[index]
        piece = mixed[index][0].reshape(owners, count, rows, padded, BS)
        carry_in = sums is not None
        if index == len(chunks) - 1 and carry_in:
            piece, param_part = lax.optimization_barrier((piece, param_part))
            param_part, sums = lax.optimization_barrier((sum(far_parts, param_part), sums))
        piece = exchange(piece)
        in_spec = pl.BlockSpec(
            (1, many, width, count * BS), lambda h, at=start // count: (0, h, 0, at)
        )
        grad, sums = pl.pallas_call(
            functools.partial(lon_back_kernel, start, carry_in),
            grid=(rows // many,),
            in_specs=[
                whole((width, tall)),
                spectrum_spec(many, count),
                in_spec,
                in_spec,
                stat_spec(many),
                whole((1, local)),
            ]
            + [stat_spec(many)] * carry_in,
            out_specs=[grad_spec(many, count), stat_spec(many)],
            out_shape=[
                jax.ShapeDtypeStruct((rows, width, count * BS), BF16),
                jax.ShapeDtypeStruct((rows, 2, width), F32),
            ],
            compiler_params=params(),
            cost_estimate=cost(
                2 * rows * tall * width * count * BS, rows * count * BS * (6 * width + 4 * tall)
            ),
            name=f"lon_back_{index}",
        )(back, piece, inputs, cotangent, stats, gain, *([sums] * carry_in))
        grads.append(grad)

    if len(chunks) == 1:
        param_part = sum(far_parts, param_part)
    param_sums = gather_far(param_part, "row")
    for i in reversed(range(low_bits("row"))):
        if i == 0:
            param_sums, sums = lax.optimization_barrier((param_sums, sums))
        param_sums = double(param_sums, "row", 1 << i)
    param_sums = param_sums[: blocks * param_rows].reshape(blocks, param_rows, BS)

    input_grad = pl.pallas_call(
        functools.partial(finish_kernel, chunks, total_chan),
        grid=(rows // few,),
        in_specs=[row_spec(few), stat_spec(few), stat_spec(few), stat_spec(few)]
        + [grad_spec(few, count) for count in chunks],
        out_specs=row_spec(few),
        out_shape=jax.ShapeDtypeStruct(inputs.shape, BF16),
        compiler_params=params(),
        cost_estimate=cost(10 * rows * width * local, rows * width * local * 10),
        name="finish",
    )(inputs, stats, *pair_small(sums, "chan"), *grads)

    spec_scale = 1.0 / math.sqrt(batch * height * K)
    dw = param_sums[:, : 4 * BS].reshape(blocks, 2, 2, BS, BS).transpose(1, 2, 0, 3, 4) * spec_scale
    db = param_sums[:, 4 * BS : 4 * BS + 4].reshape(blocks, 2, 2, BS).transpose(1, 2, 0, 3)
    db = db * spec_scale
    ln_scale = 1.0 / math.sqrt(batch * height * width)
    gain_grad = param_sums[:, 4 * BS + 4].reshape(local) / ln_gain * ln_scale
    return (
        input_grad,
        dw[0].reshape(2, local, BS),
        db[0].reshape(2, local),
        dw[1].reshape(2, local, BS),
        db[1].reshape(2, local),
        gain_grad,
        param_sums[:, 4 * BS + 5].reshape(local),
    )


def solution(mesh):
    placed = (
        P(None, "row", None, "chan"),
        P(None, "row", None, "chan"),
        P("chan"),
        P("chan"),
        P(None, "chan", None),
        P(None, "chan"),
        P(None, "chan", None),
        P(None, "chan"),
    )
    return jax.shard_map(
        on_device,
        mesh=mesh,
        in_specs=placed,
        out_specs=(
            P(None, "row", None, "chan"),
            P(None, "chan", None),
            P(None, "chan"),
            P(None, "chan", None),
            P(None, "chan"),
            P("chan"),
            P("chan"),
        ),
        check_vma=False,
    )
```

```python
import functools
import math

import jax
import jax.numpy as jnp
import numpy as np
from jax import lax
from jax.experimental import pallas as pl
from jax.experimental.pallas import tpu as pltpu
from jax.sharding import PartitionSpec as P

K = 192
BS = 128
EPS = 1e-05
LAMBDA = 0.01
ROOT_TWO_PI = math.sqrt(2.0 / math.pi)
BF16 = jnp.bfloat16
F32 = jnp.float32
VMEM_LIMIT = 60 * 1024 * 1024


def gelu_parts(values):
    inner = ROOT_TWO_PI * (values + 0.044715 * values * values * values)
    tangent = jnp.tanh(inner)
    output = 0.5 * values * (1.0 + tangent)
    slope = 0.5 * (1.0 + tangent) + 0.5 * values * (1.0 - tangent * tangent) * ROOT_TWO_PI * (
        1.0 + 3.0 * 0.044715 * values * values
    )
    return (output, slope)


def shrink_slope(values):
    tangent = jnp.tanh(values / LAMBDA)
    return tangent * tangent


def high_low(table):
    high = np.asarray(table, np.float32).astype(jnp.bfloat16)
    low = (np.asarray(table, np.float32) - high.astype(np.float32)).astype(jnp.bfloat16)
    return high, low


def lon_table(width, owners, padded):
    own = K // owners
    number = np.arange(K)[:, None]
    column = np.arange(width)[None, :]
    phase = (number * column % width) * (2.0 * math.pi / width)
    parts = np.stack([np.cos(phase), -np.sin(phase)]) / math.sqrt(width)
    parts = parts.reshape(2, owners, own, width).transpose(1, 0, 2, 3)
    table = np.zeros((owners, padded, width))
    table[:, : 2 * own] = parts.reshape(owners, 2 * own, width)
    return table.reshape(owners * padded, width)


def kept_scale(owners, padded):
    own = K // owners
    scale = np.full((2, K), 2.0)
    scale[:, 0] = 1.0
    out = np.ones((owners, padded))
    out[:, : 2 * own] = scale.reshape(2, owners, own).transpose(1, 0, 2).reshape(owners, 2 * own)
    return out.reshape(owners * padded, 1)


def lat_table(length):
    first = np.arange(length)
    phase = (first[:, None] * first[None, :] % length) * (2.0 * math.pi / length)
    cosine = np.cos(phase) / math.sqrt(length)
    sine = np.sin(phase) / math.sqrt(length)
    return np.block([[cosine, sine], [-sine, cosine]])


def dot(left, right):
    return jnp.dot(left, right, preferred_element_type=F32)


def dot_rows(left, right):
    return lax.dot_general(left, right, (((0,), (0,)), ((), ())), preferred_element_type=F32)


def dot_cols(left, right):
    return lax.dot_general(left, right, (((1,), (1,)), ((), ())), preferred_element_type=F32)


def split(values):
    high = values.astype(BF16)
    return high, (values - high.astype(F32)).astype(BF16)


def columns_of(stats):
    count = stats.shape[0]
    high, rest = split(stats)
    mid, low = split(stats - high.astype(F32))
    stacked = jnp.concatenate([high.astype(F32), mid.astype(F32), low.astype(F32)], 0)
    pad = -stacked.shape[0] % 16
    if pad:
        stacked = jnp.concatenate([stacked, jnp.zeros((pad, stacked.shape[1]), F32)], 0)
    rows = stacked.shape[0]
    row = lax.broadcasted_iota(jnp.int32, (rows, count * 128), 0)
    lane = lax.broadcasted_iota(jnp.int32, (rows, count * 128), 1)
    pick = (row % count == lane // 128) & (row < 3 * count)
    wide = dot_rows(stacked.astype(BF16), pick.astype(F32).astype(BF16))
    return [wide[:, i * 128 : (i + 1) * 128] for i in range(count)]


def cot_lon_kernel(table_ref, cot_ref, out_ref):
    owners, blocks, rows, padded, _ = out_ref.shape
    for r in range(rows):
        result = dot(table_ref[...], cot_ref[0, r])
        for b in range(blocks):
            out_ref[:, b, r] = result[:, b * BS : (b + 1) * BS].reshape(owners, padded, BS)


def input_lon_kernel(table_ref, in_ref, stat_ref, gain_ref, *out_refs):
    tall = table_ref.shape[0] // 2
    for r in range(in_ref.shape[1]):
        mean, rstd = columns_of(stat_ref[r])
        at = 0
        for out_ref in out_refs:
            owners, blocks, _, padded, _ = out_ref.shape
            pieces = []
            for b in range(at, at + blocks):
                lanes = slice(b * BS, (b + 1) * BS)
                values = in_ref[0, r, :, lanes].astype(F32)
                pieces.append((values - mean) * rstd * gain_ref[:, lanes])
            at += blocks
            high, low = split(jnp.concatenate(pieces, 1))
            both = dot(table_ref[...], high)
            result = both[:tall] + both[tall:] + dot(table_ref[:tall], low)
            for b in range(blocks):
                out_ref[:, b, r] = result[:, b * BS : (b + 1) * BS].reshape(owners, padded, BS)


def mixer_kernel(
    own,
    group,
    fwd_high_ref,
    fwd_low_ref,
    inv_high_ref,
    inv_low_ref,
    w_one_ref,
    w_one_t_ref,
    w_two_ref,
    w_two_t_ref,
    bias_ref,
    shift_ref,
    x_ref,
    c_ref,
    grad_ref,
    sums_ref,
    x_scr,
    c_scr,
    high_scr,
    low_scr,
    spec_scr,
    hid_scr,
    two_scr,
    pre_scr,
    gain_scr,
):
    sources, _, span, _ = x_ref.shape
    length = fwd_high_ref.shape[0] // 2
    padded = sources * span // length
    steps = own // group
    for s in range(sources):
        x_scr[s * span : (s + 1) * span] = x_ref[s, 0]
        c_scr[s * span : (s + 1) * span] = c_ref[s, 0]
    for k in range(own):
        step, place = divmod(k, group)
        for which, scr in enumerate((x_scr, c_scr)):
            lanes = slice((which * group + place) * BS, (which * group + place + 1) * BS)
            for part in range(2):
                values = scr[pl.ds(part * own + k, length, stride=padded), :]
                rows = slice(part * length, (part + 1) * length)
                high, low = split(values)
                high_scr[step, rows, lanes] = high
                low_scr[step, rows, lanes] = low
    gain_scr[...] = jnp.zeros_like(gain_scr)
    w_one = w_one_ref[0]
    w_two = w_two_ref[0]
    first = lax.broadcasted_iota(jnp.int32, (group * length, 1), 0) == 0

    def gather(full, which):
        rows = []
        for place in range(group):
            at = (which * group + place) * BS
            re = full[:length, at : at + BS]
            im = full[length:, at : at + BS]
            rows.append(jnp.concatenate([re, im], 1))
        return jnp.concatenate(rows, 0)

    def body(step, carry):
        high = high_scr[step]
        low = low_scr[step]
        full = dot(fwd_high_ref[...], high) + dot(fwd_high_ref[...], low)
        full = full + dot(fwd_low_ref[...], high)
        plain = gather(full, 0)
        cot = gather(full, 1)
        at = pl.ds(pl.multiple_of(step * (group * length), group * length), group * length)
        is_first = jnp.where(first & (step == 0), 1.0, 0.0)
        spec = (plain + is_first * shift_ref[0, 0:1]).astype(BF16)
        pre_one = dot(spec, w_one) + bias_ref[0, 0:1]
        act, slope = gelu_parts(pre_one)
        hid = act.astype(BF16)
        pre_two = dot(hid, w_two) + bias_ref[0, 1:2]
        grad_two = (cot * shrink_slope(pre_two)).astype(BF16)
        grad_pre = (dot(grad_two, w_two_t_ref[0]) * slope).astype(BF16)
        grad_spec = dot(grad_pre, w_one_t_ref[0])
        spec_scr[at] = spec
        hid_scr[at] = hid
        two_scr[at] = grad_two
        pre_scr[at] = grad_pre
        gain_scr[0:1] += jnp.sum(grad_spec * plain, 0, keepdims=True)
        gain_scr[1:2] += jnp.sum(grad_two.astype(F32), 0, keepdims=True)
        gain_scr[2:3] += jnp.sum(grad_pre.astype(F32), 0, keepdims=True)
        gain_scr[3:4] += jnp.sum(grad_spec * is_first, 0, keepdims=True)
        for place in range(group):
            piece = grad_spec[place * length : (place + 1) * length]
            stacked = jnp.concatenate([piece[:, :BS], piece[:, BS:]], 0)
            grad_high, grad_low = split(stacked)
            high_scr[step, :, place * BS : (place + 1) * BS] = grad_high
            low_scr[step, :, place * BS : (place + 1) * BS] = grad_low
        return carry

    lax.fori_loop(0, steps, body, 0)
    for step in range(steps):
        high = high_scr[step, :, : group * BS]
        low = low_scr[step, :, : group * BS]
        lon = dot(inv_high_ref[...], high) + dot(inv_high_ref[...], low)
        lon = lon + dot(inv_low_ref[...], high)
        for place in range(group):
            k = step * group + place
            for part in range(2):
                piece = lon[part * length : (part + 1) * length, place * BS : (place + 1) * BS]
                x_scr[pl.ds(part * own + k, length, stride=padded), :] = piece
    for k in range(2 * own, padded):
        x_scr[pl.ds(k, length, stride=padded), :] = jnp.zeros((length, BS), F32)
    for s in range(sources):
        grad_ref[s, 0] = x_scr[s * span : (s + 1) * span]
    for i, (left, right) in enumerate(((spec_scr, pre_scr), (hid_scr, two_scr))):
        square = dot_rows(left[...], right[...])
        sums_ref[0, 2 * i * BS : (2 * i + 1) * BS] = square[:BS, :BS] + square[BS:, BS:]
        sums_ref[0, (2 * i + 1) * BS : (2 * i + 2) * BS] = square[:BS, BS:] - square[BS:, :BS]
    total = gain_scr[...]
    sums_ref[0, 4 * BS : 4 * BS + 8] = jnp.concatenate(
        [
            total[2:3, :BS],
            total[2:3, BS:],
            total[1:2, :BS],
            total[1:2, BS:],
            total[0:1, :BS] + total[0:1, BS:],
            total[3:4, :BS] * shift_ref[0, 1:2, :BS],
            jnp.zeros((2, BS), F32),
        ],
        0,
    )


def lon_back_kernel(
    offset, carry_in, table_ref, grad_ref, in_ref, cot_ref, stat_ref, gain_ref, *refs
):
    if carry_in:
        before_ref, out_ref, sums_ref = refs
    else:
        out_ref, sums_ref = refs
    sources, blocks, rows, padded, _ = grad_ref.shape
    ones = jnp.ones((16, BS), BF16)
    for r in range(rows):
        mean, rstd = columns_of(stat_ref[r])
        pieces = [
            grad_ref[:, b, r].reshape(sources * padded, BS).astype(BF16) for b in range(blocks)
        ]
        mixed = dot(table_ref[...], jnp.concatenate(pieces, 1))
        grads = jnp.zeros((in_ref.shape[2], BS), F32)
        products = jnp.zeros((in_ref.shape[2], BS), F32)
        for b in range(blocks):
            lanes = slice((offset + b) * BS, (offset + b + 1) * BS)
            grad = mixed[:, b * BS : (b + 1) * BS] * gain_ref[:, lanes]
            values = in_ref[0, r, :, b * BS : (b + 1) * BS].astype(F32)
            cot = cot_ref[0, r, :, b * BS : (b + 1) * BS].astype(F32)
            out_ref[r, :, b * BS : (b + 1) * BS] = (cot + rstd * grad).astype(BF16)
            grads = grads + grad
            products = products + grad * ((values - mean) * rstd)
        both = [dot_cols(ones, values.astype(BF16))[0:1] for values in (grads, products)]
        sums = jnp.concatenate(both, 0)
        if carry_in:
            sums = sums + before_ref[r]
        sums_ref[r] = sums


def finish_kernel(chunks, channels, *refs):
    in_ref, stat_ref, sums_ref, more_ref = refs[:4]
    base_refs = refs[4 : 4 + len(chunks)]
    out_ref = refs[-1]
    for r in range(in_ref.shape[1]):
        mean, rstd = stat_ref[r, 0:1], stat_ref[r, 1:2]
        sums = (sums_ref[r] + more_ref[r]) / channels
        slope = rstd * rstd * sums[1:2]
        level = rstd * sums[0:1] - mean * slope
        level, slope = columns_of(jnp.concatenate([level, slope], 0))
        at = 0
        for base_ref, blocks in zip(base_refs, chunks):
            for b in range(blocks):
                lanes = slice(at * BS, (at + 1) * BS)
                values = in_ref[0, r, :, lanes].astype(F32)
                base = base_ref[r, :, b * BS : (b + 1) * BS].astype(F32)
                out_ref[0, r, :, lanes] = (base - level - slope * values).astype(BF16)
                at += 1


def xor_permute(piece, axis, bit):
    size = lax.axis_size(axis)
    return lax.ppermute(piece, axis, [(i, i ^ bit) for i in range(size)])


def pair_small(piece, axis):
    other = jnp.zeros_like(piece)
    bit = 1
    while bit < lax.axis_size(axis):
        piece = piece + other if bit > 1 else piece
        other = xor_permute(piece, axis, bit)
        bit *= 2
    return piece, other


def low_bits(axis):
    return max(lax.axis_size(axis).bit_length() - 2, 0)


def halve(piece, axis):
    index = lax.axis_index(axis)
    for i in range(low_bits(axis)):
        half = piece.shape[0] // 2
        low, high = piece[:half], piece[half:]
        upper = (index & (1 << i)) != 0
        piece = jnp.where(upper, high, low) + xor_permute(
            jnp.where(upper, low, high), axis, 1 << i
        )
    if lax.axis_size(axis) > 1:
        piece = piece + xor_permute(piece, axis, 1 << low_bits(axis))
    return piece


def double(piece, axis, bit):
    other = xor_permute(piece, axis, bit)
    upper = (lax.axis_index(axis) & bit) != 0
    return jnp.concatenate([jnp.where(upper, other, piece), jnp.where(upper, piece, other)], 0)


def divisor(count, limit):
    return max(n for n in range(1, limit + 1) if count % n == 0)


def params():
    return pltpu.CompilerParams(vmem_limit_bytes=VMEM_LIMIT)


def whole(shape):
    return pl.BlockSpec(shape, lambda *_: (0,) * len(shape))


def cost(flops, moved, transcendentals=0):
    return pl.CostEstimate(
        flops=int(flops), bytes_accessed=int(moved), transcendentals=int(transcendentals)
    )


def on_device(
    inputs, cotangent, ln_gain, ln_shift, first_weight, first_bias, second_weight, second_bias
):
    batch, rows, width, local = inputs.shape
    blocks = local // BS
    owners = lax.axis_size("row")
    height = rows * owners
    own = K // owners
    padded = -(-2 * own // 8) * 8
    tall = owners * padded
    group = 2 if own % 2 == 0 else 1
    total_chan = local * lax.axis_size("chan")
    chunks = (blocks - 1, 1) if blocks > 1 else (1,)
    starts = [sum(chunks[:i]) for i in range(len(chunks))]
    gain = ln_gain.reshape(1, local)

    lon = lon_table(width, owners, padded)
    lon_high, lon_low = high_low(lon)
    lon_both = np.concatenate([lon_high, lon_low], 0)
    cot_high, _ = high_low(lon * kept_scale(owners, padded))
    back = np.ascontiguousarray(lon.T).astype(np.float32).astype(jnp.bfloat16)
    fwd_high, fwd_low = high_low(lat_table(height))
    inv_high, inv_low = high_low(lat_table(height).T)

    def exchange(piece):
        return lax.all_to_all(piece, "row", split_axis=0, concat_axis=0, tiled=True)

    few = divisor(rows, 2)
    many = divisor(rows, 4)

    def row_spec(step):
        return pl.BlockSpec((1, step, width, local), lambda h: (0, h, 0, 0))

    def stat_spec(step):
        return pl.BlockSpec((step, 2, width), lambda h: (h, 0, 0))

    def grad_spec(step, count):
        return pl.BlockSpec((step, width, count * BS), lambda h: (h, 0, 0))

    def spectrum_spec(step, count):
        return pl.BlockSpec((owners, count, step, padded, BS), lambda h: (0, 0, h, 0, 0))

    def spectrum_shape(count):
        return jax.ShapeDtypeStruct((owners, count, rows, padded, BS), F32)

    lon_flops = 2 * rows * tall * width * local
    cot_lon = pl.pallas_call(
        cot_lon_kernel,
        grid=(rows // few,),
        in_specs=[whole((tall, width)), row_spec(few)],
        out_specs=spectrum_spec(few, blocks),
        out_shape=spectrum_shape(blocks),
        compiler_params=params(),
        cost_estimate=cost(lon_flops, rows * local * (2 * width + 4 * tall)),
        name="cot_lon",
    )(cot_high, cotangent)
    cot_lon, inputs = lax.optimization_barrier((cot_lon, inputs))
    cot_spec = exchange(cot_lon)

    values = inputs.astype(F32)
    mean = lax.psum(jnp.sum(values, -1), "chan") / total_chan
    centred = values - mean[..., None]
    variance = lax.psum(jnp.sum(centred * centred, -1), "chan") / total_chan
    stats = jnp.stack([mean[0], lax.rsqrt(variance + EPS)[0]], 1)

    input_lon = pl.pallas_call(
        input_lon_kernel,
        grid=(rows // few,),
        in_specs=[whole((2 * tall, width)), row_spec(few), stat_spec(few), whole((1, local))],
        out_specs=[spectrum_spec(few, count) for count in chunks],
        out_shape=[spectrum_shape(count) for count in chunks],
        compiler_params=params(),
        cost_estimate=cost(3 * lon_flops, rows * local * (2 * width + 4 * tall)),
        name="input_lon",
    )(lon_both, inputs, stats, gain)

    def square(weight):
        re, im = weight.reshape(2, blocks, BS, BS)
        return jnp.concatenate(
            [jnp.concatenate([re, im], 2), jnp.concatenate([-im, re], 2)], 1
        )

    w_one = square(first_weight)
    w_two = square(second_weight)
    w_one_t = w_one.swapaxes(1, 2)
    w_two_t = w_two.swapaxes(1, 2)
    bias = jnp.stack([first_bias, second_bias]).reshape(2, 2, blocks, BS)
    bias = bias.transpose(2, 0, 1, 3).reshape(blocks, 2, 2 * BS)
    is_origin = (lax.axis_index("row") == 0).astype(F32)
    shift = (ln_shift * (math.sqrt(height * width) * is_origin)).reshape(blocks, 1, BS)
    shift = jnp.concatenate([shift, jnp.zeros_like(shift)], 2)
    shift = jnp.concatenate([shift, jnp.full_like(shift, is_origin)], 1)

    weights = (w_one, w_one_t, w_two, w_two_t, bias, shift)
    first_piece, cot_spec, weights = lax.optimization_barrier((input_lon[0], cot_spec, weights))
    input_lon = [first_piece, *input_lon[1:]]

    span = rows * padded

    def mix(index, x_spec):
        count = chunks[index]
        start = starts[index]

        def at(shape):
            return pl.BlockSpec(shape, lambda b: (b + start,) + (0,) * (len(shape) - 1))

        tokens = own * height
        flops = 2 * count * tokens * 2 * BS * (3 * 2 * height * 3 + 6 * 2 * BS)
        return pl.pallas_call(
            functools.partial(mixer_kernel, own, group),
            grid=(count,),
            in_specs=[whole((2 * height, 2 * height))] * 4
            + [at((1, 2 * BS, 2 * BS))] * 4
            + [
                at((1, 2, 2 * BS)),
                at((1, 2, 2 * BS)),
                pl.BlockSpec((owners, 1, span, BS), lambda b: (0, b, 0, 0)),
                pl.BlockSpec((owners, 1, span, BS), lambda b: (0, b + start, 0, 0)),
            ],
            out_specs=[
                pl.BlockSpec((owners, 1, span, BS), lambda b: (0, b, 0, 0)),
                pl.BlockSpec((1, 4 * BS + 8, BS), lambda b: (b, 0, 0)),
            ],
            out_shape=[
                jax.ShapeDtypeStruct((owners, count, span, BS), F32),
                jax.ShapeDtypeStruct((count, 4 * BS + 8, BS), F32),
            ],
            scratch_shapes=[
                pltpu.VMEM((owners * span, BS), F32),
                pltpu.VMEM((owners * span, BS), F32),
                pltpu.VMEM((own // group, 2 * height, 2 * group * BS), BF16),
                pltpu.VMEM((own // group, 2 * height, 2 * group * BS), BF16),
                pltpu.VMEM((tokens, 2 * BS), BF16),
                pltpu.VMEM((tokens, 2 * BS), BF16),
                pltpu.VMEM((tokens, 2 * BS), BF16),
                pltpu.VMEM((tokens, 2 * BS), BF16),
                pltpu.VMEM((8, 2 * BS), F32),
            ],
            compiler_params=params(),
            cost_estimate=cost(flops, 3 * count * owners * span * BS * 4, 4 * tokens * BS * count),
            name=f"mixer_{index}",
        )(
            fwd_high,
            fwd_low,
            inv_high,
            inv_low,
            *weights,
            x_spec.reshape(owners, count, span, BS),
            cot_spec.reshape(owners, blocks, span, BS),
        )

    mixed = [mix(i, exchange(piece)) for i, piece in enumerate(input_lon)]
    param_rows = 4 * BS + 8
    unit = 8 * owners // math.gcd(8 * owners, blocks)
    tail = -(blocks * param_rows) % (unit * blocks)
    flat = jnp.concatenate([m[1].reshape(-1, BS) for m in mixed], 0)
    flat = jnp.pad(flat, ((0, tail), (0, 0)))
    param_part = halve(flat, "row")

    grads = []
    sums = None
    for index, count in enumerate(chunks):
        start = starts[index]
        piece = mixed[index][0].reshape(owners, count, rows, padded, BS)
        carry_in = sums is not None
        if index == len(chunks) - 1 and carry_in:
            piece, param_part = lax.optimization_barrier((piece, param_part))
            param_part, sums = lax.optimization_barrier((param_part, sums))
        piece = exchange(piece)
        in_spec = pl.BlockSpec(
            (1, many, width, count * BS), lambda h, at=start // count: (0, h, 0, at)
        )
        grad, sums = pl.pallas_call(
            functools.partial(lon_back_kernel, start, carry_in),
            grid=(rows // many,),
            in_specs=[
                whole((width, tall)),
                spectrum_spec(many, count),
                in_spec,
                in_spec,
                stat_spec(many),
                whole((1, local)),
            ]
            + [stat_spec(many)] * carry_in,
            out_specs=[grad_spec(many, count), stat_spec(many)],
            out_shape=[
                jax.ShapeDtypeStruct((rows, width, count * BS), BF16),
                jax.ShapeDtypeStruct((rows, 2, width), F32),
            ],
            compiler_params=params(),
            cost_estimate=cost(
                2 * rows * tall * width * count * BS, rows * count * BS * (6 * width + 4 * tall)
            ),
            name=f"lon_back_{index}",
        )(back, piece, inputs, cotangent, stats, gain, *([sums] * carry_in))
        grads.append(grad)

    param_sums = param_part
    for i in reversed(range(low_bits("row"))):
        param_sums = double(param_sums, "row", 1 << i)
    param_sums = param_sums[: blocks * param_rows].reshape(blocks, param_rows, BS)

    input_grad = pl.pallas_call(
        functools.partial(finish_kernel, chunks, total_chan),
        grid=(rows // few,),
        in_specs=[row_spec(few), stat_spec(few), stat_spec(few), stat_spec(few)]
        + [grad_spec(few, count) for count in chunks],
        out_specs=row_spec(few),
        out_shape=jax.ShapeDtypeStruct(inputs.shape, BF16),
        compiler_params=params(),
        cost_estimate=cost(10 * rows * width * local, rows * width * local * 10),
        name="finish",
    )(inputs, stats, *pair_small(sums, "chan"), *grads)

    spec_scale = 1.0 / math.sqrt(batch * height * K)
    dw = param_sums[:, : 4 * BS].reshape(blocks, 2, 2, BS, BS).transpose(1, 2, 0, 3, 4) * spec_scale
    db = param_sums[:, 4 * BS : 4 * BS + 4].reshape(blocks, 2, 2, BS).transpose(1, 2, 0, 3)
    db = db * spec_scale
    ln_scale = 1.0 / math.sqrt(batch * height * width)
    gain_grad = param_sums[:, 4 * BS + 4].reshape(local) / ln_gain * ln_scale
    return (
        input_grad,
        dw[0].reshape(2, local, BS),
        db[0].reshape(2, local),
        dw[1].reshape(2, local, BS),
        db[1].reshape(2, local),
        gain_grad,
        param_sums[:, 4 * BS + 5].reshape(local),
    )


def solution(mesh):
    placed = (
        P(None, "row", None, "chan"),
        P(None, "row", None, "chan"),
        P("chan"),
        P("chan"),
        P(None, "chan", None),
        P(None, "chan"),
        P(None, "chan", None),
        P(None, "chan"),
    )
    return jax.shard_map(
        on_device,
        mesh=mesh,
        in_specs=placed,
        out_specs=(
            P(None, "row", None, "chan"),
            P(None, "chan", None),
            P(None, "chan"),
            P(None, "chan", None),
            P(None, "chan"),
            P("chan"),
            P("chan"),
        ),
        check_vma=False,
    )
```

```python
import functools
import math

import jax
import jax.numpy as jnp
import numpy as np
from jax import lax
from jax.experimental import pallas as pl
from jax.experimental.pallas import tpu as pltpu
from jax.sharding import PartitionSpec as P

K = 192
BS = 128
EPS = 1e-05
LAMBDA = 0.01
ROOT_TWO_PI = math.sqrt(2.0 / math.pi)
BF16 = jnp.bfloat16
F32 = jnp.float32
VMEM_LIMIT = 60 * 1024 * 1024


def gelu_parts(values):
    inner = ROOT_TWO_PI * (values + 0.044715 * values * values * values)
    tangent = jnp.tanh(inner)
    output = 0.5 * values * (1.0 + tangent)
    slope = 0.5 * (1.0 + tangent) + 0.5 * values * (1.0 - tangent * tangent) * ROOT_TWO_PI * (
        1.0 + 3.0 * 0.044715 * values * values
    )
    return (output, slope)


def shrink_slope(values):
    tangent = jnp.tanh(values / LAMBDA)
    return tangent * tangent


def high_low(table):
    high = np.asarray(table, np.float32).astype(jnp.bfloat16)
    low = (np.asarray(table, np.float32) - high.astype(np.float32)).astype(jnp.bfloat16)
    return high, low


def lon_table(width, owners, padded):
    own = K // owners
    number = np.arange(K)[:, None]
    column = np.arange(width)[None, :]
    phase = (number * column % width) * (2.0 * math.pi / width)
    parts = np.stack([np.cos(phase), -np.sin(phase)]) / math.sqrt(width)
    parts = parts.reshape(2, owners, own, width).transpose(1, 0, 2, 3)
    table = np.zeros((owners, padded, width))
    table[:, : 2 * own] = parts.reshape(owners, 2 * own, width)
    return table.reshape(owners * padded, width)


def kept_scale(owners, padded):
    own = K // owners
    scale = np.full((2, K), 2.0)
    scale[:, 0] = 1.0
    out = np.ones((owners, padded))
    out[:, : 2 * own] = scale.reshape(2, owners, own).transpose(1, 0, 2).reshape(owners, 2 * own)
    return out.reshape(owners * padded, 1)


def lat_table(length):
    first = np.arange(length)
    phase = (first[:, None] * first[None, :] % length) * (2.0 * math.pi / length)
    cosine = np.cos(phase) / math.sqrt(length)
    sine = np.sin(phase) / math.sqrt(length)
    return np.block([[cosine, sine], [-sine, cosine]])


def dot(left, right):
    return jnp.dot(left, right, preferred_element_type=F32)


def dot_rows(left, right):
    return lax.dot_general(left, right, (((0,), (0,)), ((), ())), preferred_element_type=F32)


def dot_cols(left, right):
    return lax.dot_general(left, right, (((1,), (1,)), ((), ())), preferred_element_type=F32)


def split(values):
    high = values.astype(BF16)
    return high, (values - high.astype(F32)).astype(BF16)


def columns_of(stats):
    count = stats.shape[0]
    high, rest = split(stats)
    mid, low = split(stats - high.astype(F32))
    stacked = jnp.concatenate([high.astype(F32), mid.astype(F32), low.astype(F32)], 0)
    pad = -stacked.shape[0] % 16
    if pad:
        stacked = jnp.concatenate([stacked, jnp.zeros((pad, stacked.shape[1]), F32)], 0)
    rows = stacked.shape[0]
    row = lax.broadcasted_iota(jnp.int32, (rows, count * 128), 0)
    lane = lax.broadcasted_iota(jnp.int32, (rows, count * 128), 1)
    pick = (row % count == lane // 128) & (row < 3 * count)
    wide = dot_rows(stacked.astype(BF16), pick.astype(F32).astype(BF16))
    return [wide[:, i * 128 : (i + 1) * 128] for i in range(count)]


def cot_lon_kernel(table_ref, cot_ref, out_ref):
    owners, blocks, rows, padded, _ = out_ref.shape
    for r in range(rows):
        result = dot(table_ref[...], cot_ref[0, r])
        for b in range(blocks):
            out_ref[:, b, r] = result[:, b * BS : (b + 1) * BS].reshape(owners, padded, BS)


def piece_to(refs, me, i):
    near = len(refs)
    return refs[0].at[me ^ i] if near == 1 else refs[i % near].at[i // near]


def piece_from(refs, me, i):
    near = refs[0].shape[0]
    return refs[0].at[me ^ i] if len(refs) == 1 else refs[i // near].at[i % near]


def input_lon_kernel(chunks, me_ref, table_ref, in_ref, stat_ref, gain_ref, *refs):
    out_refs, scratch = refs[:-1], refs[-1]
    tall = table_ref.shape[0] // 2
    for r in range(in_ref.shape[1]):
        mean, rstd = columns_of(stat_ref[r])
        at = 0
        for index, blocks in enumerate(chunks):
            pieces = []
            for b in range(at, at + blocks):
                lanes = slice(b * BS, (b + 1) * BS)
                values = in_ref[0, r, :, lanes].astype(F32)
                pieces.append((values - mean) * rstd * gain_ref[:, lanes])
            at += blocks
            high, low = split(jnp.concatenate(pieces, 1))
            both = dot(table_ref[...], high)
            result = both[:tall] + both[tall:] + dot(table_ref[:tall], low)
            if index < len(chunks) - 1:
                owners, _, _, padded, _ = out_refs[index].shape
                for b in range(blocks):
                    piece = result[:, b * BS : (b + 1) * BS].reshape(owners, padded, BS)
                    out_refs[index][:, b, r] = piece
            else:
                last = out_refs[index:]
                padded = last[0].shape[3]
                scratch[r] = result
                for i in range(tall // padded):
                    place = pl.ds(pl.multiple_of((me_ref[0] ^ i) * padded, padded), padded)
                    piece_to(last, me_ref[0], i)[0, r] = scratch[r, place]


def mixer_kernel(
    own,
    group,
    x_count,
    grad_count,
    me_ref,
    fwd_high_ref,
    fwd_low_ref,
    inv_high_ref,
    inv_low_ref,
    w_one_ref,
    w_one_t_ref,
    w_two_ref,
    w_two_t_ref,
    bias_ref,
    shift_ref,
    c_ref,
    *refs,
):
    x_refs, grad_refs = refs[:x_count], refs[x_count : x_count + grad_count]
    sums_ref, x_scr, c_scr, high_scr, low_scr, spec_scr, hid_scr, two_scr, pre_scr, gain_scr = refs[
        x_count + grad_count :
    ]
    sources, _, span, _ = c_ref.shape
    length = fwd_high_ref.shape[0] // 2
    padded = sources * span // length
    steps = own // group
    places = [
        pl.ds(pl.multiple_of((me_ref[0] ^ i) * span, span), span) for i in range(sources)
    ]
    for i, place in enumerate(places):
        x_scr[place] = piece_from(x_refs, me_ref[0], i)[0]
        c_scr[i * span : (i + 1) * span] = c_ref[i, 0]
    for k in range(own):
        step, place = divmod(k, group)
        for which, scr in enumerate((x_scr, c_scr)):
            lanes = slice((which * group + place) * BS, (which * group + place + 1) * BS)
            for part in range(2):
                values = scr[pl.ds(part * own + k, length, stride=padded), :]
                rows = slice(part * length, (part + 1) * length)
                high, low = split(values)
                high_scr[step, rows, lanes] = high
                low_scr[step, rows, lanes] = low
    gain_scr[...] = jnp.zeros_like(gain_scr)
    w_one = w_one_ref[0]
    w_two = w_two_ref[0]
    first = lax.broadcasted_iota(jnp.int32, (group * length, 1), 0) == 0

    def gather(full, which):
        rows = []
        for place in range(group):
            at = (which * group + place) * BS
            re = full[:length, at : at + BS]
            im = full[length:, at : at + BS]
            rows.append(jnp.concatenate([re, im], 1))
        return jnp.concatenate(rows, 0)

    def body(step, carry):
        high = high_scr[step]
        low = low_scr[step]
        full = dot(fwd_high_ref[...], high) + dot(fwd_high_ref[...], low)
        full = full + dot(fwd_low_ref[...], high)
        plain = gather(full, 0)
        cot = gather(full, 1)
        at = pl.ds(pl.multiple_of(step * (group * length), group * length), group * length)
        is_first = jnp.where(first & (step == 0), 1.0, 0.0)
        spec = (plain + is_first * shift_ref[0, 0:1]).astype(BF16)
        pre_one = dot(spec, w_one) + bias_ref[0, 0:1]
        act, slope = gelu_parts(pre_one)
        hid = act.astype(BF16)
        pre_two = dot(hid, w_two) + bias_ref[0, 1:2]
        grad_two = (cot * shrink_slope(pre_two)).astype(BF16)
        grad_pre = (dot(grad_two, w_two_t_ref[0]) * slope).astype(BF16)
        grad_spec = dot(grad_pre, w_one_t_ref[0])
        spec_scr[at] = spec
        hid_scr[at] = hid
        two_scr[at] = grad_two
        pre_scr[at] = grad_pre
        gain_scr[0:1] += jnp.sum(grad_spec * plain, 0, keepdims=True)
        gain_scr[1:2] += jnp.sum(grad_two.astype(F32), 0, keepdims=True)
        gain_scr[2:3] += jnp.sum(grad_pre.astype(F32), 0, keepdims=True)
        gain_scr[3:4] += jnp.sum(grad_spec * is_first, 0, keepdims=True)
        for place in range(group):
            piece = grad_spec[place * length : (place + 1) * length]
            stacked = jnp.concatenate([piece[:, :BS], piece[:, BS:]], 0)
            grad_high, grad_low = split(stacked)
            high_scr[step, :, place * BS : (place + 1) * BS] = grad_high
            low_scr[step, :, place * BS : (place + 1) * BS] = grad_low
        return carry

    lax.fori_loop(0, steps, body, 0)
    for step in range(steps):
        high = high_scr[step, :, : group * BS]
        low = low_scr[step, :, : group * BS]
        lon = dot(inv_high_ref[...], high) + dot(inv_high_ref[...], low)
        lon = lon + dot(inv_low_ref[...], high)
        for place in range(group):
            k = step * group + place
            for part in range(2):
                piece = lon[part * length : (part + 1) * length, place * BS : (place + 1) * BS]
                x_scr[pl.ds(part * own + k, length, stride=padded), :] = piece
    for k in range(2 * own, padded):
        x_scr[pl.ds(k, length, stride=padded), :] = jnp.zeros((length, BS), F32)
    for i, place in enumerate(places):
        piece_to(grad_refs, me_ref[0], i)[0] = x_scr[place]
    for i, (left, right) in enumerate(((spec_scr, pre_scr), (hid_scr, two_scr))):
        square = dot_rows(left[...], right[...])
        sums_ref[0, 2 * i * BS : (2 * i + 1) * BS] = square[:BS, :BS] + square[BS:, BS:]
        sums_ref[0, (2 * i + 1) * BS : (2 * i + 2) * BS] = square[:BS, BS:] - square[BS:, :BS]
    total = gain_scr[...]
    sums_ref[0, 4 * BS : 4 * BS + 8] = jnp.concatenate(
        [
            total[2:3, :BS],
            total[2:3, BS:],
            total[1:2, :BS],
            total[1:2, BS:],
            total[0:1, :BS] + total[0:1, BS:],
            total[3:4, :BS] * shift_ref[0, 1:2, :BS],
            jnp.zeros((2, BS), F32),
        ],
        0,
    )


def lon_back_kernel(
    offset, carry_in, count_in, me_ref, table_ref, in_ref, cot_ref, stat_ref, gain_ref, *refs
):
    grad_refs = refs[:count_in]
    if carry_in:
        before_ref, out_ref, sums_ref, scratch = refs[count_in:]
    else:
        out_ref, sums_ref, scratch = refs[count_in:]
    _, blocks, rows, padded, _ = grad_refs[0].shape
    ones = jnp.ones((16, BS), BF16)
    for r in range(rows):
        mean, rstd = columns_of(stat_ref[r])
        if count_in == 1:
            pieces = [grad_refs[0][:, b, r].reshape(-1, BS).astype(BF16) for b in range(blocks)]
            spectrum = jnp.concatenate(pieces, 1)
        else:
            for i in range(table_ref.shape[1] // padded):
                place = pl.ds(pl.multiple_of((me_ref[0] ^ i) * padded, padded), padded)
                for b in range(blocks):
                    lanes = slice(b * BS, (b + 1) * BS)
                    scratch[r, place, lanes] = piece_from(grad_refs, me_ref[0], i)[b, r]
            spectrum = scratch[r].astype(BF16)
        mixed = dot(table_ref[...], spectrum)
        grads = jnp.zeros((in_ref.shape[2], BS), F32)
        products = jnp.zeros((in_ref.shape[2], BS), F32)
        for b in range(blocks):
            lanes = slice((offset + b) * BS, (offset + b + 1) * BS)
            grad = mixed[:, b * BS : (b + 1) * BS] * gain_ref[:, lanes]
            values = in_ref[0, r, :, b * BS : (b + 1) * BS].astype(F32)
            cot = cot_ref[0, r, :, b * BS : (b + 1) * BS].astype(F32)
            out_ref[r, :, b * BS : (b + 1) * BS] = (cot + rstd * grad).astype(BF16)
            grads = grads + grad
            products = products + grad * ((values - mean) * rstd)
        both = [dot_cols(ones, values.astype(BF16))[0:1] for values in (grads, products)]
        sums = jnp.concatenate(both, 0)
        if carry_in:
            sums = sums + before_ref[r]
        sums_ref[r] = sums


def finish_kernel(chunks, channels, *refs):
    in_ref, stat_ref, sums_ref, more_ref = refs[:4]
    base_refs = refs[4 : 4 + len(chunks)]
    out_ref = refs[-1]
    for r in range(in_ref.shape[1]):
        mean, rstd = stat_ref[r, 0:1], stat_ref[r, 1:2]
        sums = (sums_ref[r] + more_ref[r]) / channels
        slope = rstd * rstd * sums[1:2]
        level = rstd * sums[0:1] - mean * slope
        level, slope = columns_of(jnp.concatenate([level, slope], 0))
        at = 0
        for base_ref, blocks in zip(base_refs, chunks):
            for b in range(blocks):
                lanes = slice(at * BS, (at + 1) * BS)
                values = in_ref[0, r, :, lanes].astype(F32)
                base = base_ref[r, :, b * BS : (b + 1) * BS].astype(F32)
                out_ref[0, r, :, lanes] = (base - level - slope * values).astype(BF16)
                at += 1


def xor_permute(piece, axis, bit):
    size = lax.axis_size(axis)
    return lax.ppermute(piece, axis, [(i, i ^ bit) for i in range(size)])


def pair_small(piece, axis):
    other = jnp.zeros_like(piece)
    bit = 1
    while bit < lax.axis_size(axis):
        piece = piece + other if bit > 1 else piece
        other = xor_permute(piece, axis, bit)
        bit *= 2
    return piece, other


def low_bits(axis):
    return max(lax.axis_size(axis).bit_length() - 2, 0)


def halve(piece, axis):
    index = lax.axis_index(axis)
    for i in range(low_bits(axis)):
        half = piece.shape[0] // 2
        low, high = piece[:half], piece[half:]
        upper = (index & (1 << i)) != 0
        piece = jnp.where(upper, high, low) + xor_permute(
            jnp.where(upper, low, high), axis, 1 << i
        )
    return piece


def double(piece, axis, bit):
    other = xor_permute(piece, axis, bit)
    upper = (lax.axis_index(axis) & bit) != 0
    return jnp.concatenate([jnp.where(upper, other, piece), jnp.where(upper, piece, other)], 0)


def divisor(count, limit):
    return max(n for n in range(1, limit + 1) if count % n == 0)


def params():
    return pltpu.CompilerParams(vmem_limit_bytes=VMEM_LIMIT)


def whole(shape):
    return pl.BlockSpec(shape, lambda *_: (0,) * len(shape))


def cost(flops, moved, transcendentals=0):
    return pl.CostEstimate(
        flops=int(flops), bytes_accessed=int(moved), transcendentals=int(transcendentals)
    )


def on_device(
    inputs, cotangent, ln_gain, ln_shift, first_weight, first_bias, second_weight, second_bias
):
    batch, rows, width, local = inputs.shape
    blocks = local // BS
    owners = lax.axis_size("row")
    height = rows * owners
    own = K // owners
    padded = -(-2 * own // 8) * 8
    tall = owners * padded
    group = 2 if own % 2 == 0 else 1
    total_chan = local * lax.axis_size("chan")
    chunks = (blocks - 1, 1) if blocks > 1 else (1,)
    starts = [sum(chunks[:i]) for i in range(len(chunks))]
    gain = ln_gain.reshape(1, local)

    lon = lon_table(width, owners, padded)
    lon_high, lon_low = high_low(lon)
    lon_both = np.concatenate([lon_high, lon_low], 0)
    cot_high, _ = high_low(lon * kept_scale(owners, padded))
    back = np.ascontiguousarray(lon.T).astype(np.float32).astype(jnp.bfloat16)
    fwd_high, fwd_low = high_low(lat_table(height))
    inv_high, inv_low = high_low(lat_table(height).T)

    def exchange(piece):
        return lax.all_to_all(piece, "row", split_axis=0, concat_axis=0, tiled=True)

    me = lax.axis_index("row").astype(jnp.int32).reshape(1)
    me_spec = pl.BlockSpec(memory_space=pltpu.SMEM)
    near = 1 << ((owners.bit_length() - 1) // 2)
    far = owners // near

    def exchange_near(pieces):
        got = [pieces[0]] + [xor_permute(pieces[r], "row", r) for r in range(1, near)]
        return [jnp.concatenate([g[s : s + 1] for g in got], 0) for s in range(far)]

    def exchange_far(pieces):
        got = [pieces[0]] + [xor_permute(pieces[s], "row", s * near) for s in range(1, far)]
        return got

    few = divisor(rows, 2)
    many = divisor(rows, 4)

    def row_spec(step):
        return pl.BlockSpec((1, step, width, local), lambda h: (0, h, 0, 0))

    def stat_spec(step):
        return pl.BlockSpec((step, 2, width), lambda h: (h, 0, 0))

    def grad_spec(step, count):
        return pl.BlockSpec((step, width, count * BS), lambda h: (h, 0, 0))

    def spectrum_spec(step, count, parts=owners):
        return pl.BlockSpec((parts, count, step, padded, BS), lambda h: (0, 0, h, 0, 0))

    def spectrum_shape(count, parts=owners):
        return jax.ShapeDtypeStruct((parts, count, rows, padded, BS), F32)

    lon_flops = 2 * rows * tall * width * local
    cot_lon = pl.pallas_call(
        cot_lon_kernel,
        grid=(rows // few,),
        in_specs=[whole((tall, width)), row_spec(few)],
        out_specs=spectrum_spec(few, blocks),
        out_shape=spectrum_shape(blocks),
        compiler_params=params(),
        cost_estimate=cost(lon_flops, rows * local * (2 * width + 4 * tall)),
        name="cot_lon",
    )(cot_high, cotangent)
    cot_lon, inputs = lax.optimization_barrier((cot_lon, inputs))
    cot_spec = exchange(cot_lon)

    values = inputs.astype(F32)
    mean = lax.psum(jnp.sum(values, -1), "chan") / total_chan
    centred = values - mean[..., None]
    variance = lax.psum(jnp.sum(centred * centred, -1), "chan") / total_chan
    stats = jnp.stack([mean[0], lax.rsqrt(variance + EPS)[0]], 1)

    input_lon = pl.pallas_call(
        functools.partial(input_lon_kernel, chunks),
        grid=(rows // few,),
        in_specs=[
            me_spec,
            whole((2 * tall, width)),
            row_spec(few),
            stat_spec(few),
            whole((1, local)),
        ],
        out_specs=[spectrum_spec(few, count) for count in chunks[:-1]]
        + [spectrum_spec(few, 1, far)] * near,
        out_shape=[spectrum_shape(count) for count in chunks[:-1]]
        + [spectrum_shape(1, far)] * near,
        scratch_shapes=[pltpu.VMEM((few, tall, BS), F32)],
        compiler_params=params(),
        cost_estimate=cost(3 * lon_flops, rows * local * (2 * width + 4 * tall)),
        name="input_lon",
    )(me, lon_both, inputs, stats, gain)

    def square(weight):
        re, im = weight.reshape(2, blocks, BS, BS)
        return jnp.concatenate(
            [jnp.concatenate([re, im], 2), jnp.concatenate([-im, re], 2)], 1
        )

    w_one = square(first_weight)
    w_two = square(second_weight)
    w_one_t = w_one.swapaxes(1, 2)
    w_two_t = w_two.swapaxes(1, 2)
    bias = jnp.stack([first_bias, second_bias]).reshape(2, 2, blocks, BS)
    bias = bias.transpose(2, 0, 1, 3).reshape(blocks, 2, 2 * BS)
    is_origin = (lax.axis_index("row") == 0).astype(F32)
    shift = (ln_shift * (math.sqrt(height * width) * is_origin)).reshape(blocks, 1, BS)
    shift = jnp.concatenate([shift, jnp.zeros_like(shift)], 2)
    shift = jnp.concatenate([shift, jnp.full_like(shift, is_origin)], 1)

    weights = (w_one, w_one_t, w_two, w_two_t, bias, shift)
    first_piece, cot_spec, weights = lax.optimization_barrier((input_lon[0], cot_spec, weights))
    last = len(chunks) - 1
    input_lon = [first_piece, *input_lon[1:]]
    x_out = [[exchange(piece)] for piece in input_lon[:last]]
    x_out.append(exchange_far(exchange_near(input_lon[last:])))

    span = rows * padded

    def mix(index, x_spec):
        count = chunks[index]
        start = starts[index]

        def at(shape):
            return pl.BlockSpec(shape, lambda b: (b + start,) + (0,) * (len(shape) - 1))

        x_count, grad_count = (1 if index < last else far), 1
        tokens = own * height
        flops = 2 * count * tokens * 2 * BS * (3 * 2 * height * 3 + 6 * 2 * BS)
        return pl.pallas_call(
            functools.partial(mixer_kernel, own, group, x_count, grad_count),
            grid=(count,),
            in_specs=[me_spec]
            + [whole((2 * height, 2 * height))] * 4
            + [at((1, 2 * BS, 2 * BS))] * 4
            + [
                at((1, 2, 2 * BS)),
                at((1, 2, 2 * BS)),
                pl.BlockSpec((owners, 1, span, BS), lambda b: (0, b + start, 0, 0)),
            ]
            + [pl.BlockSpec((owners // x_count, 1, span, BS), lambda b: (0, b, 0, 0))] * x_count,
            out_specs=[pl.BlockSpec((owners // grad_count, 1, span, BS), lambda b: (0, b, 0, 0))]
            * grad_count
            + [pl.BlockSpec((1, 4 * BS + 8, BS), lambda b: (b, 0, 0))],
            out_shape=[jax.ShapeDtypeStruct((owners // grad_count, count, span, BS), F32)]
            * grad_count
            + [jax.ShapeDtypeStruct((count, 4 * BS + 8, BS), F32)],
            scratch_shapes=[
                pltpu.VMEM((owners * span, BS), F32),
                pltpu.VMEM((owners * span, BS), F32),
                pltpu.VMEM((own // group, 2 * height, 2 * group * BS), BF16),
                pltpu.VMEM((own // group, 2 * height, 2 * group * BS), BF16),
                pltpu.VMEM((tokens, 2 * BS), BF16),
                pltpu.VMEM((tokens, 2 * BS), BF16),
                pltpu.VMEM((tokens, 2 * BS), BF16),
                pltpu.VMEM((tokens, 2 * BS), BF16),
                pltpu.VMEM((8, 2 * BS), F32),
            ],
            compiler_params=params(),
            cost_estimate=cost(flops, 3 * count * owners * span * BS * 4, 4 * tokens * BS * count),
            name=f"mixer_{index}",
        )(
            me,
            fwd_high,
            fwd_low,
            inv_high,
            inv_low,
            *weights,
            cot_spec.reshape(owners, blocks, span, BS),
            *[x.reshape(-1, count, span, BS) for x in x_spec],
        )

    mixed = [mix(i, pieces) for i, pieces in enumerate(x_out)]
    param_rows = 4 * BS + 8
    unit = 8 * owners // math.gcd(8 * owners, blocks)
    tail = -(blocks * param_rows) % (unit * blocks)
    flat = jnp.concatenate([m[-1].reshape(-1, BS) for m in mixed], 0)
    flat = jnp.pad(flat, ((0, tail), (0, 0)))
    param_part = halve(flat, "row")

    grads = []
    sums = None
    for index, count in enumerate(chunks):
        start = starts[index]
        pieces = [p.reshape(-1, count, rows, padded, BS) for p in mixed[index][:-1]]
        carry_in = sums is not None
        if index == last:
            param_part = param_part + xor_permute(param_part, "row", 1 << low_bits("row"))
            pieces[0], param_part = lax.optimization_barrier((pieces[0], param_part))
        pieces = [exchange(pieces[0])]
        if carry_in:
            param_part, sums = lax.optimization_barrier((param_part, sums))
        in_spec = pl.BlockSpec(
            (1, many, width, count * BS), lambda h, at=start // count: (0, h, 0, at)
        )
        grad, sums = pl.pallas_call(
            functools.partial(lon_back_kernel, start, carry_in, len(pieces)),
            grid=(rows // many,),
            in_specs=[
                me_spec,
                whole((width, tall)),
                in_spec,
                in_spec,
                stat_spec(many),
                whole((1, local)),
            ]
            + [spectrum_spec(many, count, owners // len(pieces))] * len(pieces)
            + [stat_spec(many)] * carry_in,
            scratch_shapes=[pltpu.VMEM((many, tall, count * BS), F32)],
            out_specs=[grad_spec(many, count), stat_spec(many)],
            out_shape=[
                jax.ShapeDtypeStruct((rows, width, count * BS), BF16),
                jax.ShapeDtypeStruct((rows, 2, width), F32),
            ],
            compiler_params=params(),
            cost_estimate=cost(
                2 * rows * tall * width * count * BS, rows * count * BS * (6 * width + 4 * tall)
            ),
            name=f"lon_back_{index}",
        )(me, back, inputs, cotangent, stats, gain, *pieces, *([sums] * carry_in))
        grads.append(grad)

    param_sums = param_part
    for i in reversed(range(low_bits("row"))):
        param_sums = double(param_sums, "row", 1 << i)
    param_sums = param_sums[: blocks * param_rows].reshape(blocks, param_rows, BS)

    spec_scale = 1.0 / math.sqrt(batch * height * K)
    dw = param_sums[:, : 4 * BS].reshape(blocks, 2, 2, BS, BS).transpose(1, 2, 0, 3, 4) * spec_scale
    db = param_sums[:, 4 * BS : 4 * BS + 4].reshape(blocks, 2, 2, BS).transpose(1, 2, 0, 3)
    db = db * spec_scale
    ln_scale = 1.0 / math.sqrt(batch * height * width)
    gain_grad = param_sums[:, 4 * BS + 4].reshape(local) / ln_gain * ln_scale
    outputs = (
        dw[0].reshape(2, local, BS),
        db[0].reshape(2, local),
        dw[1].reshape(2, local, BS),
        db[1].reshape(2, local),
        gain_grad,
        param_sums[:, 4 * BS + 5].reshape(local),
    )
    first, second = pair_small(sums, "chan")
    second, outputs = lax.optimization_barrier((second, outputs))

    input_grad = pl.pallas_call(
        functools.partial(finish_kernel, chunks, total_chan),
        grid=(rows // few,),
        in_specs=[row_spec(few), stat_spec(few), stat_spec(few), stat_spec(few)]
        + [grad_spec(few, count) for count in chunks],
        out_specs=row_spec(few),
        out_shape=jax.ShapeDtypeStruct(inputs.shape, BF16),
        compiler_params=params(),
        cost_estimate=cost(10 * rows * width * local, rows * width * local * 10),
        name="finish",
    )(inputs, stats, first, second, *grads)
    return (input_grad, *outputs)


def solution(mesh):
    placed = (
        P(None, "row", None, "chan"),
        P(None, "row", None, "chan"),
        P("chan"),
        P("chan"),
        P(None, "chan", None),
        P(None, "chan"),
        P(None, "chan", None),
        P(None, "chan"),
    )
    return jax.shard_map(
        on_device,
        mesh=mesh,
        in_specs=placed,
        out_specs=(
            P(None, "row", None, "chan"),
            P(None, "chan", None),
            P(None, "chan"),
            P(None, "chan", None),
            P(None, "chan"),
            P("chan"),
            P("chan"),
        ),
        check_vma=False,
    )
```

```python
import functools
import math

import jax
import jax.numpy as jnp
import numpy as np
from jax import lax
from jax.experimental import pallas as pl
from jax.experimental.pallas import tpu as pltpu
from jax.sharding import PartitionSpec as P

K = 192
BS = 128
EPS = 1e-05
LAMBDA = 0.01
ROOT_TWO_PI = math.sqrt(2.0 / math.pi)
BF16 = jnp.bfloat16
F32 = jnp.float32


def gelu_parts(values):
    inner = ROOT_TWO_PI * (values + 0.044715 * values * values * values)
    tangent = jnp.tanh(inner)
    output = 0.5 * values * (1.0 + tangent)
    slope = 0.5 * (1.0 + tangent) + 0.5 * values * (1.0 - tangent * tangent) * ROOT_TWO_PI * (
        1.0 + 3.0 * 0.044715 * values * values
    )
    return (output, slope)


def shrink_slope(values):
    tangent = jnp.tanh(values / LAMBDA)
    return tangent * tangent


def high_low(table):
    high = np.asarray(table, np.float32).astype(jnp.bfloat16)
    low = (np.asarray(table, np.float32) - high.astype(np.float32)).astype(jnp.bfloat16)
    return high, low


def lon_table(width, owners, padded):
    own = K // owners
    number = np.arange(K)[:, None]
    column = np.arange(width)[None, :]
    phase = (number * column % width) * (2.0 * math.pi / width)
    parts = np.stack([np.cos(phase), -np.sin(phase)]) / math.sqrt(width)
    parts = parts.reshape(2, owners, own, width).transpose(1, 0, 2, 3)
    table = np.zeros((owners, padded, width))
    table[:, : 2 * own] = parts.reshape(owners, 2 * own, width)
    return table.reshape(owners * padded, width)


def kept_scale(owners, padded):
    own = K // owners
    scale = np.full((2, K), 2.0)
    scale[:, 0] = 1.0
    out = np.ones((owners, padded))
    out[:, : 2 * own] = scale.reshape(2, owners, own).transpose(1, 0, 2).reshape(owners, 2 * own)
    return out.reshape(owners * padded, 1)


def lat_table(length):
    first = np.arange(length)
    phase = (first[:, None] * first[None, :] % length) * (2.0 * math.pi / length)
    cosine = np.cos(phase) / math.sqrt(length)
    sine = np.sin(phase) / math.sqrt(length)
    return np.block([[cosine, sine], [-sine, cosine]])


def dot(left, right):
    return jnp.dot(left, right, preferred_element_type=F32)


def dot_rows(left, right):
    return lax.dot_general(left, right, (((0,), (0,)), ((), ())), preferred_element_type=F32)


def dot_cols(left, right):
    return lax.dot_general(left, right, (((1,), (1,)), ((), ())), preferred_element_type=F32)


def split(values):
    high = values.astype(BF16)
    return high, (values - high.astype(F32)).astype(BF16)


def columns_of(stats):
    count = stats.shape[0]
    high, rest = split(stats)
    mid, low = split(stats - high.astype(F32))
    stacked = jnp.concatenate([high.astype(F32), mid.astype(F32), low.astype(F32)], 0)
    pad = -stacked.shape[0] % 16
    if pad:
        stacked = jnp.concatenate([stacked, jnp.zeros((pad, stacked.shape[1]), F32)], 0)
    rows = stacked.shape[0]
    row = lax.broadcasted_iota(jnp.int32, (rows, count * 128), 0)
    lane = lax.broadcasted_iota(jnp.int32, (rows, count * 128), 1)
    pick = (row % count == lane // 128) & (row < 3 * count)
    wide = dot_rows(stacked.astype(BF16), pick.astype(F32).astype(BF16))
    return [wide[:, i * 128 : (i + 1) * 128] for i in range(count)]


def cot_lon_kernel(table_ref, cot_ref, out_ref):
    owners, blocks, rows, padded, _ = out_ref.shape
    for r in range(rows):
        result = dot(table_ref[...], cot_ref[0, r])
        for b in range(blocks):
            out_ref[:, b, r] = result[:, b * BS : (b + 1) * BS].reshape(owners, padded, BS)


def input_lon_kernel(table_ref, in_ref, stat_ref, gain_ref, *out_refs):
    tall = table_ref.shape[0] // 2
    for r in range(in_ref.shape[1]):
        mean, rstd = columns_of(stat_ref[r])
        at = 0
        for out_ref in out_refs:
            owners, blocks, _, padded, _ = out_ref.shape
            pieces = []
            for b in range(at, at + blocks):
                lanes = slice(b * BS, (b + 1) * BS)
                values = in_ref[0, r, :, lanes].astype(F32)
                pieces.append((values - mean) * rstd * gain_ref[:, lanes])
            at += blocks
            high, low = split(jnp.concatenate(pieces, 1))
            both = dot(table_ref[...], high)
            result = both[:tall] + both[tall:] + dot(table_ref[:tall], low)
            for b in range(blocks):
                out_ref[:, b, r] = result[:, b * BS : (b + 1) * BS].reshape(owners, padded, BS)


def mixer_kernel(
    own,
    group,
    fwd_high_ref,
    fwd_low_ref,
    inv_high_ref,
    inv_low_ref,
    w_one_ref,
    w_one_t_ref,
    w_two_ref,
    w_two_t_ref,
    bias_ref,
    shift_ref,
    x_ref,
    c_ref,
    grad_ref,
    sums_ref,
    x_scr,
    c_scr,
    high_scr,
    low_scr,
    spec_scr,
    hid_scr,
    two_scr,
    pre_scr,
    gain_scr,
):
    sources, _, span, _ = x_ref.shape
    length = fwd_high_ref.shape[0] // 2
    padded = sources * span // length
    steps = own // group
    for s in range(sources):
        x_scr[s * span : (s + 1) * span] = x_ref[s, 0]
        c_scr[s * span : (s + 1) * span] = c_ref[s, 0]
    for k in range(own):
        step, place = divmod(k, group)
        for which, scr in enumerate((x_scr, c_scr)):
            lanes = slice((which * group + place) * BS, (which * group + place + 1) * BS)
            for part in range(2):
                values = scr[pl.ds(part * own + k, length, stride=padded), :]
                rows = slice(part * length, (part + 1) * length)
                high, low = split(values)
                high_scr[step, rows, lanes] = high
                low_scr[step, rows, lanes] = low
    gain_scr[...] = jnp.zeros_like(gain_scr)
    w_one = w_one_ref[0]
    w_two = w_two_ref[0]
    first = lax.broadcasted_iota(jnp.int32, (group * length, 1), 0) == 0

    def gather(full, which):
        rows = []
        for place in range(group):
            at = (which * group + place) * BS
            re = full[:length, at : at + BS]
            im = full[length:, at : at + BS]
            rows.append(jnp.concatenate([re, im], 1))
        return jnp.concatenate(rows, 0)

    def body(step, carry):
        high = high_scr[step]
        low = low_scr[step]
        full = dot(fwd_high_ref[...], high) + dot(fwd_high_ref[...], low)
        full = full + dot(fwd_low_ref[...], high)
        plain = gather(full, 0)
        cot = gather(full, 1)
        at = pl.ds(pl.multiple_of(step * (group * length), group * length), group * length)
        is_first = jnp.where(first & (step == 0), 1.0, 0.0)
        spec = (plain + is_first * shift_ref[0, 0:1]).astype(BF16)
        pre_one = dot(spec, w_one) + bias_ref[0, 0:1]
        act, slope = gelu_parts(pre_one)
        hid = act.astype(BF16)
        pre_two = dot(hid, w_two) + bias_ref[0, 1:2]
        grad_two = (cot * shrink_slope(pre_two)).astype(BF16)
        grad_pre = (dot(grad_two, w_two_t_ref[0]) * slope).astype(BF16)
        grad_spec = dot(grad_pre, w_one_t_ref[0])
        spec_scr[at] = spec
        hid_scr[at] = hid
        two_scr[at] = grad_two
        pre_scr[at] = grad_pre
        gain_scr[0:1] += jnp.sum(grad_spec * plain, 0, keepdims=True)
        gain_scr[1:2] += jnp.sum(grad_two.astype(F32), 0, keepdims=True)
        gain_scr[2:3] += jnp.sum(grad_pre.astype(F32), 0, keepdims=True)
        gain_scr[3:4] += jnp.sum(grad_spec * is_first, 0, keepdims=True)
        for place in range(group):
            piece = grad_spec[place * length : (place + 1) * length]
            stacked = jnp.concatenate([piece[:, :BS], piece[:, BS:]], 0)
            grad_high, grad_low = split(stacked)
            high_scr[step, :, place * BS : (place + 1) * BS] = grad_high
            low_scr[step, :, place * BS : (place + 1) * BS] = grad_low
        return carry

    lax.fori_loop(0, steps, body, 0)
    for step in range(steps):
        high = high_scr[step, :, : group * BS]
        low = low_scr[step, :, : group * BS]
        lon = dot(inv_high_ref[...], high) + dot(inv_high_ref[...], low)
        lon = lon + dot(inv_low_ref[...], high)
        for place in range(group):
            k = step * group + place
            for part in range(2):
                piece = lon[part * length : (part + 1) * length, place * BS : (place + 1) * BS]
                x_scr[pl.ds(part * own + k, length, stride=padded), :] = piece
    for k in range(2 * own, padded):
        x_scr[pl.ds(k, length, stride=padded), :] = jnp.zeros((length, BS), F32)
    for s in range(sources):
        grad_ref[s, 0] = x_scr[s * span : (s + 1) * span]
    for i, (left, right) in enumerate(((spec_scr, pre_scr), (hid_scr, two_scr))):
        square = dot_rows(left[...], right[...])
        sums_ref[0, 2 * i * BS : (2 * i + 1) * BS] = square[:BS, :BS] + square[BS:, BS:]
        sums_ref[0, (2 * i + 1) * BS : (2 * i + 2) * BS] = square[:BS, BS:] - square[BS:, :BS]
    total = gain_scr[...]
    sums_ref[0, 4 * BS : 4 * BS + 8] = jnp.concatenate(
        [
            total[2:3, :BS],
            total[2:3, BS:],
            total[1:2, :BS],
            total[1:2, BS:],
            total[0:1, :BS] + total[0:1, BS:],
            total[3:4, :BS] * shift_ref[0, 1:2, :BS],
            jnp.zeros((2, BS), F32),
        ],
        0,
    )


def lon_back_kernel(
    offset, carry_in, table_ref, grad_ref, in_ref, cot_ref, stat_ref, gain_ref, *refs
):
    if carry_in:
        before_ref, out_ref, sums_ref = refs
    else:
        out_ref, sums_ref = refs
    sources, blocks, rows, padded, _ = grad_ref.shape
    ones = jnp.ones((16, BS), BF16)
    for r in range(rows):
        mean, rstd = columns_of(stat_ref[r])
        pieces = [
            grad_ref[:, b, r].reshape(sources * padded, BS).astype(BF16) for b in range(blocks)
        ]
        mixed = dot(table_ref[...], jnp.concatenate(pieces, 1))
        grads = jnp.zeros((in_ref.shape[2], BS), F32)
        products = jnp.zeros((in_ref.shape[2], BS), F32)
        for b in range(blocks):
            lanes = slice((offset + b) * BS, (offset + b + 1) * BS)
            grad = mixed[:, b * BS : (b + 1) * BS] * gain_ref[:, lanes]
            values = in_ref[0, r, :, b * BS : (b + 1) * BS].astype(F32)
            cot = cot_ref[0, r, :, b * BS : (b + 1) * BS].astype(F32)
            out_ref[r, :, b * BS : (b + 1) * BS] = (cot + rstd * grad).astype(BF16)
            grads = grads + grad
            products = products + grad * ((values - mean) * rstd)
        both = [dot_cols(ones, values.astype(BF16))[0:1] for values in (grads, products)]
        sums = jnp.concatenate(both, 0)
        if carry_in:
            sums = sums + before_ref[r]
        sums_ref[r] = sums


def finish_kernel(chunks, channels, *refs):
    in_ref, stat_ref, sums_ref, more_ref = refs[:4]
    base_refs = refs[4 : 4 + len(chunks)]
    out_ref = refs[-1]
    for r in range(in_ref.shape[1]):
        mean, rstd = stat_ref[r, 0:1], stat_ref[r, 1:2]
        sums = (sums_ref[r] + more_ref[r]) / channels
        slope = rstd * rstd * sums[1:2]
        level = rstd * sums[0:1] - mean * slope
        level, slope = columns_of(jnp.concatenate([level, slope], 0))
        at = 0
        for base_ref, blocks in zip(base_refs, chunks):
            for b in range(blocks):
                lanes = slice(at * BS, (at + 1) * BS)
                values = in_ref[0, r, :, lanes].astype(F32)
                base = base_ref[r, :, b * BS : (b + 1) * BS].astype(F32)
                out_ref[0, r, :, lanes] = (base - level - slope * values).astype(BF16)
                at += 1


def xor_permute(piece, axis, bit):
    size = lax.axis_size(axis)
    return lax.ppermute(piece, axis, [(i, i ^ bit) for i in range(size)])


def pair_small(piece, axis):
    other = jnp.zeros_like(piece)
    bit = 1
    while bit < lax.axis_size(axis):
        piece = piece + other if bit > 1 else piece
        other = xor_permute(piece, axis, bit)
        bit *= 2
    return piece, other


def low_bits(axis):
    return max(lax.axis_size(axis).bit_length() - 2, 0)


def halve(piece, axis):
    index = lax.axis_index(axis)
    for i in range(low_bits(axis)):
        half = piece.shape[0] // 2
        low, high = piece[:half], piece[half:]
        upper = (index & (1 << i)) != 0
        piece = jnp.where(upper, high, low) + xor_permute(
            jnp.where(upper, low, high), axis, 1 << i
        )
    if lax.axis_size(axis) > 1:
        piece = piece + xor_permute(piece, axis, 1 << low_bits(axis))
    return piece


def double(piece, axis, bit):
    other = xor_permute(piece, axis, bit)
    upper = (lax.axis_index(axis) & bit) != 0
    return jnp.concatenate([jnp.where(upper, other, piece), jnp.where(upper, piece, other)], 0)


def divisor(count, limit):
    return max(n for n in range(1, limit + 1) if count % n == 0)


def params(mib=60):
    return pltpu.CompilerParams(vmem_limit_bytes=mib * 1024 * 1024)


def whole(shape):
    return pl.BlockSpec(shape, lambda *_: (0,) * len(shape))


def cost(flops, moved, transcendentals=0):
    return pl.CostEstimate(
        flops=int(flops), bytes_accessed=int(moved), transcendentals=int(transcendentals)
    )


def on_device(
    inputs, cotangent, ln_gain, ln_shift, first_weight, first_bias, second_weight, second_bias
):
    batch, rows, width, local = inputs.shape
    blocks = local // BS
    owners = lax.axis_size("row")
    height = rows * owners
    own = K // owners
    padded = -(-2 * own // 8) * 8
    tall = owners * padded
    group = 2 if own % 2 == 0 else 1
    total_chan = local * lax.axis_size("chan")
    chunks = (blocks - 1, 1) if blocks > 1 else (1,)
    starts = [sum(chunks[:i]) for i in range(len(chunks))]
    gain = ln_gain.reshape(1, local)

    lon = lon_table(width, owners, padded)
    lon_high, lon_low = high_low(lon)
    lon_both = np.concatenate([lon_high, lon_low], 0)
    cot_high, _ = high_low(lon * kept_scale(owners, padded))
    back = np.ascontiguousarray(lon.T).astype(np.float32).astype(jnp.bfloat16)
    fwd_high, fwd_low = high_low(lat_table(height))
    inv_high, inv_low = high_low(lat_table(height).T)

    def exchange(piece):
        return lax.all_to_all(piece, "row", split_axis=0, concat_axis=0, tiled=True)

    few = divisor(rows, 2)
    many = divisor(rows, 4)

    def row_spec(step):
        return pl.BlockSpec((1, step, width, local), lambda h: (0, h, 0, 0))

    def stat_spec(step):
        return pl.BlockSpec((step, 2, width), lambda h: (h, 0, 0))

    def grad_spec(step, count):
        return pl.BlockSpec((step, width, count * BS), lambda h: (h, 0, 0))

    def spectrum_spec(step, count):
        return pl.BlockSpec((owners, count, step, padded, BS), lambda h: (0, 0, h, 0, 0))

    def spectrum_shape(count):
        return jax.ShapeDtypeStruct((owners, count, rows, padded, BS), F32)

    lon_flops = 2 * rows * tall * width * local
    cot_lon = pl.pallas_call(
        cot_lon_kernel,
        grid=(rows // many,),
        in_specs=[whole((tall, width)), row_spec(many)],
        out_specs=spectrum_spec(many, blocks),
        out_shape=spectrum_shape(blocks),
        compiler_params=params(),
        cost_estimate=cost(lon_flops, rows * local * (2 * width + 4 * tall)),
        name="cot_lon",
    )(cot_high, cotangent)
    cot_lon, inputs = lax.optimization_barrier((cot_lon, inputs))
    cot_spec = exchange(cot_lon)

    values = inputs.astype(F32)
    mean = lax.psum(jnp.sum(values, -1), "chan") / total_chan
    centred = values - mean[..., None]
    variance = lax.psum(jnp.sum(centred * centred, -1), "chan") / total_chan
    stats = jnp.stack([mean[0], lax.rsqrt(variance + EPS)[0]], 1)

    input_lon = pl.pallas_call(
        input_lon_kernel,
        grid=(rows // few,),
        in_specs=[whole((2 * tall, width)), row_spec(few), stat_spec(few), whole((1, local))],
        out_specs=[spectrum_spec(few, count) for count in chunks],
        out_shape=[spectrum_shape(count) for count in chunks],
        compiler_params=params(),
        cost_estimate=cost(3 * lon_flops, rows * local * (2 * width + 4 * tall)),
        name="input_lon",
    )(lon_both, inputs, stats, gain)

    def square(weight):
        re, im = weight.reshape(2, blocks, BS, BS)
        return jnp.concatenate(
            [jnp.concatenate([re, im], 2), jnp.concatenate([-im, re], 2)], 1
        )

    w_one = square(first_weight)
    w_two = square(second_weight)
    w_one_t = w_one.swapaxes(1, 2)
    w_two_t = w_two.swapaxes(1, 2)
    bias = jnp.stack([first_bias, second_bias]).reshape(2, 2, blocks, BS)
    bias = bias.transpose(2, 0, 1, 3).reshape(blocks, 2, 2 * BS)
    is_origin = (lax.axis_index("row") == 0).astype(F32)
    shift = (ln_shift * (math.sqrt(height * width) * is_origin)).reshape(blocks, 1, BS)
    shift = jnp.concatenate([shift, jnp.zeros_like(shift)], 2)
    shift = jnp.concatenate([shift, jnp.full_like(shift, is_origin)], 1)

    weights = (w_one, w_one_t, w_two, w_two_t, bias, shift)
    first_piece, cot_spec, weights = lax.optimization_barrier((input_lon[0], cot_spec, weights))
    input_lon = [first_piece, *input_lon[1:]]

    span = rows * padded

    def mix(index, x_spec):
        count = chunks[index]
        start = starts[index]

        def at(shape):
            return pl.BlockSpec(shape, lambda b: (b + start,) + (0,) * (len(shape) - 1))

        tokens = own * height
        flops = 2 * count * tokens * 2 * BS * (3 * 2 * height * 3 + 6 * 2 * BS)
        return pl.pallas_call(
            functools.partial(mixer_kernel, own, group),
            grid=(count,),
            in_specs=[whole((2 * height, 2 * height))] * 4
            + [at((1, 2 * BS, 2 * BS))] * 4
            + [
                at((1, 2, 2 * BS)),
                at((1, 2, 2 * BS)),
                pl.BlockSpec((owners, 1, span, BS), lambda b: (0, b, 0, 0)),
                pl.BlockSpec((owners, 1, span, BS), lambda b: (0, b + start, 0, 0)),
            ],
            out_specs=[
                pl.BlockSpec((owners, 1, span, BS), lambda b: (0, b, 0, 0)),
                pl.BlockSpec((1, 4 * BS + 8, BS), lambda b: (b, 0, 0)),
            ],
            out_shape=[
                jax.ShapeDtypeStruct((owners, count, span, BS), F32),
                jax.ShapeDtypeStruct((count, 4 * BS + 8, BS), F32),
            ],
            scratch_shapes=[
                pltpu.VMEM((owners * span, BS), F32),
                pltpu.VMEM((owners * span, BS), F32),
                pltpu.VMEM((own // group, 2 * height, 2 * group * BS), BF16),
                pltpu.VMEM((own // group, 2 * height, 2 * group * BS), BF16),
                pltpu.VMEM((tokens, 2 * BS), BF16),
                pltpu.VMEM((tokens, 2 * BS), BF16),
                pltpu.VMEM((tokens, 2 * BS), BF16),
                pltpu.VMEM((tokens, 2 * BS), BF16),
                pltpu.VMEM((8, 2 * BS), F32),
            ],
            compiler_params=params(60 if index < len(chunks) - 1 else 44),
            cost_estimate=cost(flops, 3 * count * owners * span * BS * 4, 4 * tokens * BS * count),
            name=f"mixer_{index}",
        )(
            fwd_high,
            fwd_low,
            inv_high,
            inv_low,
            *weights,
            x_spec.reshape(owners, count, span, BS),
            cot_spec.reshape(owners, blocks, span, BS),
        )

    mixed = [mix(i, exchange(piece)) for i, piece in enumerate(input_lon)]
    param_rows = 4 * BS + 8
    unit = 8 * owners // math.gcd(8 * owners, blocks)
    tail = -(blocks * param_rows) % (unit * blocks)
    flat = jnp.concatenate([m[1].reshape(-1, BS) for m in mixed], 0)
    flat = jnp.pad(flat, ((0, tail), (0, 0)))
    param_part = halve(flat, "row")

    grads = []
    sums = None
    for index, count in enumerate(chunks):
        start = starts[index]
        piece = mixed[index][0].reshape(owners, count, rows, padded, BS)
        carry_in = sums is not None
        if index == len(chunks) - 1 and carry_in:
            piece, param_part = lax.optimization_barrier((piece, param_part))
            param_part, sums = lax.optimization_barrier((param_part, sums))
        piece = exchange(piece)
        in_spec = pl.BlockSpec(
            (1, many, width, count * BS), lambda h, at=start // count: (0, h, 0, at)
        )
        grad, sums = pl.pallas_call(
            functools.partial(lon_back_kernel, start, carry_in),
            grid=(rows // many,),
            in_specs=[
                whole((width, tall)),
                spectrum_spec(many, count),
                in_spec,
                in_spec,
                stat_spec(many),
                whole((1, local)),
            ]
            + [stat_spec(many)] * carry_in,
            out_specs=[grad_spec(many, count), stat_spec(many)],
            out_shape=[
                jax.ShapeDtypeStruct((rows, width, count * BS), BF16),
                jax.ShapeDtypeStruct((rows, 2, width), F32),
            ],
            compiler_params=params(59 if carry_in else 60),
            cost_estimate=cost(
                2 * rows * tall * width * count * BS, rows * count * BS * (6 * width + 4 * tall)
            ),
            name=f"lon_back_{index}",
        )(back, piece, inputs, cotangent, stats, gain, *([sums] * carry_in))
        grads.append(grad)

    param_sums = param_part
    for i in reversed(range(low_bits("row"))):
        param_sums = double(param_sums, "row", 1 << i)
    param_sums = param_sums[: blocks * param_rows].reshape(blocks, param_rows, BS)

    spec_scale = 1.0 / math.sqrt(batch * height * K)
    dw = param_sums[:, : 4 * BS].reshape(blocks, 2, 2, BS, BS).transpose(1, 2, 0, 3, 4) * spec_scale
    db = param_sums[:, 4 * BS : 4 * BS + 4].reshape(blocks, 2, 2, BS).transpose(1, 2, 0, 3)
    db = db * spec_scale
    ln_scale = 1.0 / math.sqrt(batch * height * width)
    gain_grad = param_sums[:, 4 * BS + 4].reshape(local) / ln_gain * ln_scale
    outputs = (
        dw[0].reshape(2, local, BS),
        db[0].reshape(2, local),
        dw[1].reshape(2, local, BS),
        db[1].reshape(2, local),
        gain_grad,
        param_sums[:, 4 * BS + 5].reshape(local),
    )
    first, second = pair_small(sums, "chan")
    second, outputs = lax.optimization_barrier((second, outputs))

    input_grad = pl.pallas_call(
        functools.partial(finish_kernel, chunks, total_chan),
        grid=(rows // many,),
        in_specs=[row_spec(many), stat_spec(many), stat_spec(many), stat_spec(many)]
        + [grad_spec(many, count) for count in chunks],
        out_specs=row_spec(many),
        out_shape=jax.ShapeDtypeStruct(inputs.shape, BF16),
        compiler_params=params(),
        cost_estimate=cost(10 * rows * width * local, rows * width * local * 10),
        name="finish",
    )(inputs, stats, first, second, *grads)
    return (input_grad, *outputs)


def solution(mesh):
    placed = (
        P(None, "row", None, "chan"),
        P(None, "row", None, "chan"),
        P("chan"),
        P("chan"),
        P(None, "chan", None),
        P(None, "chan"),
        P(None, "chan", None),
        P(None, "chan"),
    )
    return jax.shard_map(
        on_device,
        mesh=mesh,
        in_specs=placed,
        out_specs=(
            P(None, "row", None, "chan"),
            P(None, "chan", None),
            P(None, "chan"),
            P(None, "chan", None),
            P(None, "chan"),
            P("chan"),
            P("chan"),
        ),
        check_vma=False,
    )
```

```python
import functools
import math

import jax
import jax.numpy as jnp
import numpy as np
from jax import lax
from jax.experimental import pallas as pl
from jax.experimental.pallas import tpu as pltpu
from jax.sharding import PartitionSpec as P

K = 192
BS = 128
EPS = 1e-05
LAMBDA = 0.01
ROOT_TWO_PI = math.sqrt(2.0 / math.pi)
BF16 = jnp.bfloat16
F32 = jnp.float32


def gelu_parts(values):
    inner = ROOT_TWO_PI * (values + 0.044715 * values * values * values)
    tangent = jnp.tanh(inner)
    output = 0.5 * values * (1.0 + tangent)
    slope = 0.5 * (1.0 + tangent) + 0.5 * values * (1.0 - tangent * tangent) * ROOT_TWO_PI * (
        1.0 + 3.0 * 0.044715 * values * values
    )
    return (output, slope)


def shrink_slope(values):
    tangent = jnp.tanh(values / LAMBDA)
    return tangent * tangent


def high_low(table):
    high = np.asarray(table, np.float32).astype(jnp.bfloat16)
    low = (np.asarray(table, np.float32) - high.astype(np.float32)).astype(jnp.bfloat16)
    return high, low


def lon_table(width, owners, padded):
    own = K // owners
    number = np.arange(K)[:, None]
    column = np.arange(width)[None, :]
    phase = (number * column % width) * (2.0 * math.pi / width)
    parts = np.stack([np.cos(phase), -np.sin(phase)]) / math.sqrt(width)
    parts = parts.reshape(2, owners, own, width).transpose(1, 0, 2, 3)
    table = np.zeros((owners, padded, width))
    table[:, : 2 * own] = parts.reshape(owners, 2 * own, width)
    return table.reshape(owners * padded, width)


def kept_scale(owners, padded):
    own = K // owners
    scale = np.full((2, K), 2.0)
    scale[:, 0] = 1.0
    out = np.ones((owners, padded))
    out[:, : 2 * own] = scale.reshape(2, owners, own).transpose(1, 0, 2).reshape(owners, 2 * own)
    return out.reshape(owners * padded, 1)


def lat_table(length):
    first = np.arange(length)
    phase = (first[:, None] * first[None, :] % length) * (2.0 * math.pi / length)
    cosine = np.cos(phase) / math.sqrt(length)
    sine = np.sin(phase) / math.sqrt(length)
    return np.block([[cosine, sine], [-sine, cosine]])


def dot(left, right):
    return jnp.dot(left, right, preferred_element_type=F32)


def dot_rows(left, right):
    return lax.dot_general(left, right, (((0,), (0,)), ((), ())), preferred_element_type=F32)


def dot_cols(left, right):
    return lax.dot_general(left, right, (((1,), (1,)), ((), ())), preferred_element_type=F32)


def split(values):
    high = values.astype(BF16)
    return high, (values - high.astype(F32)).astype(BF16)


def columns_of(stats):
    count = stats.shape[0]
    high, rest = split(stats)
    mid, low = split(stats - high.astype(F32))
    stacked = jnp.concatenate([high.astype(F32), mid.astype(F32), low.astype(F32)], 0)
    pad = -stacked.shape[0] % 16
    if pad:
        stacked = jnp.concatenate([stacked, jnp.zeros((pad, stacked.shape[1]), F32)], 0)
    rows = stacked.shape[0]
    row = lax.broadcasted_iota(jnp.int32, (rows, count * 128), 0)
    lane = lax.broadcasted_iota(jnp.int32, (rows, count * 128), 1)
    pick = (row % count == lane // 128) & (row < 3 * count)
    wide = dot_rows(stacked.astype(BF16), pick.astype(F32).astype(BF16))
    return [wide[:, i * 128 : (i + 1) * 128] for i in range(count)]


def cot_lon_kernel(table_ref, cot_ref, out_ref):
    owners, blocks, rows, padded, _ = out_ref.shape
    for r in range(rows):
        result = dot(table_ref[...], cot_ref[0, r])
        for b in range(blocks):
            out_ref[:, b, r] = result[:, b * BS : (b + 1) * BS].reshape(owners, padded, BS)


def input_lon_kernel(table_ref, in_ref, stat_ref, gain_ref, *out_refs):
    tall = table_ref.shape[0] // 2
    for r in range(in_ref.shape[1]):
        mean, rstd = columns_of(stat_ref[r])
        at = 0
        for out_ref in out_refs:
            owners, blocks, _, padded, _ = out_ref.shape
            pieces = []
            for b in range(at, at + blocks):
                lanes = slice(b * BS, (b + 1) * BS)
                values = in_ref[0, r, :, lanes].astype(F32)
                pieces.append((values - mean) * rstd * gain_ref[:, lanes])
            at += blocks
            high, low = split(jnp.concatenate(pieces, 1))
            both = dot(table_ref[...], high)
            result = both[:tall] + both[tall:] + dot(table_ref[:tall], low)
            for b in range(blocks):
                out_ref[:, b, r] = result[:, b * BS : (b + 1) * BS].reshape(owners, padded, BS)


def mixer_kernel(
    own,
    group,
    fwd_high_ref,
    fwd_low_ref,
    inv_high_ref,
    inv_low_ref,
    w_one_ref,
    w_one_t_ref,
    w_two_ref,
    w_two_t_ref,
    bias_ref,
    shift_ref,
    x_ref,
    c_ref,
    grad_ref,
    sums_ref,
    x_scr,
    c_scr,
    high_scr,
    low_scr,
    spec_scr,
    hid_scr,
    two_scr,
    pre_scr,
    gain_scr,
):
    sources, _, span, _ = x_ref.shape
    length = fwd_high_ref.shape[0] // 2
    padded = sources * span // length
    steps = own // group
    for s in range(sources):
        x_scr[s * span : (s + 1) * span] = x_ref[s, 0]
        c_scr[s * span : (s + 1) * span] = c_ref[s, 0]
    for k in range(own):
        step, place = divmod(k, group)
        for which, scr in enumerate((x_scr, c_scr)):
            lanes = slice((which * group + place) * BS, (which * group + place + 1) * BS)
            for part in range(2):
                values = scr[pl.ds(part * own + k, length, stride=padded), :]
                rows = slice(part * length, (part + 1) * length)
                high, low = split(values)
                high_scr[step, rows, lanes] = high
                low_scr[step, rows, lanes] = low
    gain_scr[...] = jnp.zeros_like(gain_scr)
    w_one = w_one_ref[0]
    w_two = w_two_ref[0]
    first = lax.broadcasted_iota(jnp.int32, (group * length, 1), 0) == 0

    def gather(full, which):
        rows = []
        for place in range(group):
            at = (which * group + place) * BS
            re = full[:length, at : at + BS]
            im = full[length:, at : at + BS]
            rows.append(jnp.concatenate([re, im], 1))
        return jnp.concatenate(rows, 0)

    def body(step, carry):
        high = high_scr[step]
        low = low_scr[step]
        full = dot(fwd_high_ref[...], high) + dot(fwd_high_ref[...], low)
        full = full + dot(fwd_low_ref[...], high)
        plain = gather(full, 0)
        cot = gather(full, 1)
        at = pl.ds(pl.multiple_of(step * (group * length), group * length), group * length)
        is_first = jnp.where(first & (step == 0), 1.0, 0.0)
        spec = (plain + is_first * shift_ref[0, 0:1]).astype(BF16)
        pre_one = dot(spec, w_one) + bias_ref[0, 0:1]
        act, slope = gelu_parts(pre_one)
        hid = act.astype(BF16)
        pre_two = dot(hid, w_two) + bias_ref[0, 1:2]
        grad_two = (cot * shrink_slope(pre_two)).astype(BF16)
        grad_pre = (dot(grad_two, w_two_t_ref[0]) * slope).astype(BF16)
        grad_spec = dot(grad_pre, w_one_t_ref[0])
        spec_scr[at] = spec
        hid_scr[at] = hid
        two_scr[at] = grad_two
        pre_scr[at] = grad_pre
        gain_scr[0:1] += jnp.sum(grad_spec * plain, 0, keepdims=True)
        gain_scr[1:2] += jnp.sum(grad_two.astype(F32), 0, keepdims=True)
        gain_scr[2:3] += jnp.sum(grad_pre.astype(F32), 0, keepdims=True)
        gain_scr[3:4] += jnp.sum(grad_spec * is_first, 0, keepdims=True)
        for place in range(group):
            piece = grad_spec[place * length : (place + 1) * length]
            stacked = jnp.concatenate([piece[:, :BS], piece[:, BS:]], 0)
            grad_high, grad_low = split(stacked)
            high_scr[step, :, place * BS : (place + 1) * BS] = grad_high
            low_scr[step, :, place * BS : (place + 1) * BS] = grad_low
        return carry

    lax.fori_loop(0, steps, body, 0)
    for step in range(steps):
        high = high_scr[step, :, : group * BS]
        low = low_scr[step, :, : group * BS]
        lon = dot(inv_high_ref[...], high) + dot(inv_high_ref[...], low)
        lon = lon + dot(inv_low_ref[...], high)
        for place in range(group):
            k = step * group + place
            for part in range(2):
                piece = lon[part * length : (part + 1) * length, place * BS : (place + 1) * BS]
                x_scr[pl.ds(part * own + k, length, stride=padded), :] = piece
    for k in range(2 * own, padded):
        x_scr[pl.ds(k, length, stride=padded), :] = jnp.zeros((length, BS), F32)
    for s in range(sources):
        grad_ref[s, 0] = x_scr[s * span : (s + 1) * span]
    for i, (left, right) in enumerate(((spec_scr, pre_scr), (hid_scr, two_scr))):
        square = dot_rows(left[...], right[...])
        sums_ref[0, 2 * i * BS : (2 * i + 1) * BS] = square[:BS, :BS] + square[BS:, BS:]
        sums_ref[0, (2 * i + 1) * BS : (2 * i + 2) * BS] = square[:BS, BS:] - square[BS:, :BS]
    total = gain_scr[...]
    sums_ref[0, 4 * BS : 4 * BS + 8] = jnp.concatenate(
        [
            total[2:3, :BS],
            total[2:3, BS:],
            total[1:2, :BS],
            total[1:2, BS:],
            total[0:1, :BS] + total[0:1, BS:],
            total[3:4, :BS] * shift_ref[0, 1:2, :BS],
            jnp.zeros((2, BS), F32),
        ],
        0,
    )


def lon_back_kernel(
    offset, carry_in, table_ref, grad_ref, in_ref, cot_ref, stat_ref, gain_ref, *refs
):
    if carry_in:
        before_ref, out_ref, sums_ref = refs
    else:
        out_ref, sums_ref = refs
    sources, blocks, rows, padded, _ = grad_ref.shape
    ones = jnp.ones((16, BS), BF16)
    for r in range(rows):
        mean, rstd = columns_of(stat_ref[r])
        pieces = [
            grad_ref[:, b, r].reshape(sources * padded, BS).astype(BF16) for b in range(blocks)
        ]
        mixed = dot(table_ref[...], jnp.concatenate(pieces, 1))
        grads = jnp.zeros((in_ref.shape[2], BS), F32)
        products = jnp.zeros((in_ref.shape[2], BS), F32)
        for b in range(blocks):
            lanes = slice((offset + b) * BS, (offset + b + 1) * BS)
            grad = mixed[:, b * BS : (b + 1) * BS] * gain_ref[:, lanes]
            values = in_ref[0, r, :, b * BS : (b + 1) * BS].astype(F32)
            cot = cot_ref[0, r, :, b * BS : (b + 1) * BS].astype(F32)
            out_ref[r, :, b * BS : (b + 1) * BS] = (cot + rstd * grad).astype(BF16)
            grads = grads + grad
            products = products + grad * ((values - mean) * rstd)
        both = [dot_cols(ones, values.astype(BF16))[0:1] for values in (grads, products)]
        sums = jnp.concatenate(both, 0)
        if carry_in:
            sums = sums + before_ref[r]
        sums_ref[r] = sums


def finish_kernel(chunks, channels, *refs):
    in_ref, stat_ref, sums_ref, more_ref = refs[:4]
    base_refs = refs[4 : 4 + len(chunks)]
    out_ref = refs[-1]
    for r in range(in_ref.shape[1]):
        mean, rstd = stat_ref[r, 0:1], stat_ref[r, 1:2]
        sums = (sums_ref[r] + more_ref[r]) / channels
        slope = rstd * rstd * sums[1:2]
        level = rstd * sums[0:1] - mean * slope
        level, slope = columns_of(jnp.concatenate([level, slope], 0))
        at = 0
        for base_ref, blocks in zip(base_refs, chunks):
            for b in range(blocks):
                lanes = slice(at * BS, (at + 1) * BS)
                values = in_ref[0, r, :, lanes].astype(F32)
                base = base_ref[r, :, b * BS : (b + 1) * BS].astype(F32)
                out_ref[0, r, :, lanes] = (base - level - slope * values).astype(BF16)
                at += 1


def xor_permute(piece, axis, bit):
    size = lax.axis_size(axis)
    return lax.ppermute(piece, axis, [(i, i ^ bit) for i in range(size)])


def pair_small(piece, axis):
    other = jnp.zeros_like(piece)
    bit = 1
    while bit < lax.axis_size(axis):
        piece = piece + other if bit > 1 else piece
        other = xor_permute(piece, axis, bit)
        bit *= 2
    return piece, other


def low_bits(axis):
    return max(lax.axis_size(axis).bit_length() - 2, 0)


def halve(piece, axis):
    index = lax.axis_index(axis)
    for i in range(low_bits(axis)):
        half = piece.shape[0] // 2
        low, high = piece[:half], piece[half:]
        upper = (index & (1 << i)) != 0
        piece = jnp.where(upper, high, low) + xor_permute(
            jnp.where(upper, low, high), axis, 1 << i
        )
    if lax.axis_size(axis) > 1:
        piece = piece + xor_permute(piece, axis, 1 << low_bits(axis))
    return piece


def double(piece, axis, bit):
    other = xor_permute(piece, axis, bit)
    upper = (lax.axis_index(axis) & bit) != 0
    return jnp.concatenate([jnp.where(upper, other, piece), jnp.where(upper, piece, other)], 0)


def divisor(count, limit):
    return max(n for n in range(1, limit + 1) if count % n == 0)


def params(mib=60):
    return pltpu.CompilerParams(vmem_limit_bytes=mib * 1024 * 1024)


def whole(shape):
    return pl.BlockSpec(shape, lambda *_: (0,) * len(shape))


def cost(flops, moved, transcendentals=0):
    return pl.CostEstimate(
        flops=int(flops), bytes_accessed=int(moved), transcendentals=int(transcendentals)
    )


def on_device(
    inputs, cotangent, ln_gain, ln_shift, first_weight, first_bias, second_weight, second_bias
):
    batch, rows, width, local = inputs.shape
    blocks = local // BS
    owners = lax.axis_size("row")
    height = rows * owners
    own = K // owners
    padded = -(-2 * own // 8) * 8
    tall = owners * padded
    group = 2 if own % 2 == 0 else 1
    total_chan = local * lax.axis_size("chan")
    chunks = (blocks - 1, 1) if blocks > 1 else (1,)
    starts = [sum(chunks[:i]) for i in range(len(chunks))]
    gain = ln_gain.reshape(1, local)

    lon = lon_table(width, owners, padded)
    lon_high, lon_low = high_low(lon)
    lon_both = np.concatenate([lon_high, lon_low], 0)
    cot_high, _ = high_low(lon * kept_scale(owners, padded))
    back = np.ascontiguousarray(lon.T).astype(np.float32).astype(jnp.bfloat16)
    fwd_high, fwd_low = high_low(lat_table(height))
    inv_high, inv_low = high_low(lat_table(height).T)

    def exchange(piece):
        return lax.all_to_all(piece, "row", split_axis=0, concat_axis=0, tiled=True)

    few = divisor(rows, 2)
    many = divisor(rows, 4)

    def row_spec(step):
        return pl.BlockSpec((1, step, width, local), lambda h: (0, h, 0, 0))

    def stat_spec(step):
        return pl.BlockSpec((step, 2, width), lambda h: (h, 0, 0))

    def grad_spec(step, count):
        return pl.BlockSpec((step, width, count * BS), lambda h: (h, 0, 0))

    def spectrum_spec(step, count):
        return pl.BlockSpec((owners, count, step, padded, BS), lambda h: (0, 0, h, 0, 0))

    def spectrum_shape(count):
        return jax.ShapeDtypeStruct((owners, count, rows, padded, BS), F32)

    lon_flops = 2 * rows * tall * width * local
    cot_lon = pl.pallas_call(
        cot_lon_kernel,
        grid=(rows // many,),
        in_specs=[whole((tall, width)), row_spec(many)],
        out_specs=spectrum_spec(many, blocks),
        out_shape=spectrum_shape(blocks),
        compiler_params=params(),
        cost_estimate=cost(lon_flops, rows * local * (2 * width + 4 * tall)),
        name="cot_lon",
    )(cot_high, cotangent)
    cot_lon, inputs = lax.optimization_barrier((cot_lon, inputs))
    cot_spec = exchange(cot_lon)

    values = inputs.astype(F32)
    mean = lax.psum(jnp.sum(values, -1), "chan") / total_chan
    centred = values - mean[..., None]
    variance = lax.psum(jnp.sum(centred * centred, -1), "chan") / total_chan
    stats = jnp.stack([mean[0], lax.rsqrt(variance + EPS)[0]], 1)

    input_lon = pl.pallas_call(
        input_lon_kernel,
        grid=(rows // few,),
        in_specs=[whole((2 * tall, width)), row_spec(few), stat_spec(few), whole((1, local))],
        out_specs=[spectrum_spec(few, count) for count in chunks],
        out_shape=[spectrum_shape(count) for count in chunks],
        compiler_params=params(),
        cost_estimate=cost(3 * lon_flops, rows * local * (2 * width + 4 * tall)),
        name="input_lon",
    )(lon_both, inputs, stats, gain)

    def square(weight):
        re, im = weight.reshape(2, blocks, BS, BS)
        return jnp.concatenate(
            [jnp.concatenate([re, im], 2), jnp.concatenate([-im, re], 2)], 1
        )

    w_one = square(first_weight)
    w_two = square(second_weight)
    w_one_t = w_one.swapaxes(1, 2)
    w_two_t = w_two.swapaxes(1, 2)
    bias = jnp.stack([first_bias, second_bias]).reshape(2, 2, blocks, BS)
    bias = bias.transpose(2, 0, 1, 3).reshape(blocks, 2, 2 * BS)
    is_origin = (lax.axis_index("row") == 0).astype(F32)
    shift = (ln_shift * (math.sqrt(height * width) * is_origin)).reshape(blocks, 1, BS)
    shift = jnp.concatenate([shift, jnp.zeros_like(shift)], 2)
    shift = jnp.concatenate([shift, jnp.full_like(shift, is_origin)], 1)

    weights = (w_one, w_one_t, w_two, w_two_t, bias, shift)
    first_piece, cot_spec, weights = lax.optimization_barrier((input_lon[0], cot_spec, weights))
    input_lon = [first_piece, *input_lon[1:]]

    span = rows * padded

    def mix(index, x_spec):
        count = chunks[index]
        start = starts[index]

        def at(shape):
            return pl.BlockSpec(shape, lambda b: (b + start,) + (0,) * (len(shape) - 1))

        tokens = own * height
        flops = 2 * count * tokens * 2 * BS * (3 * 2 * height * 3 + 6 * 2 * BS)
        return pl.pallas_call(
            functools.partial(mixer_kernel, own, group),
            grid=(count,),
            in_specs=[whole((2 * height, 2 * height))] * 4
            + [at((1, 2 * BS, 2 * BS))] * 4
            + [
                at((1, 2, 2 * BS)),
                at((1, 2, 2 * BS)),
                pl.BlockSpec((owners, 1, span, BS), lambda b: (0, b, 0, 0)),
                pl.BlockSpec((owners, 1, span, BS), lambda b: (0, b + start, 0, 0)),
            ],
            out_specs=[
                pl.BlockSpec((owners, 1, span, BS), lambda b: (0, b, 0, 0)),
                pl.BlockSpec((1, 4 * BS + 8, BS), lambda b: (b, 0, 0)),
            ],
            out_shape=[
                jax.ShapeDtypeStruct((owners, count, span, BS), F32),
                jax.ShapeDtypeStruct((count, 4 * BS + 8, BS), F32),
            ],
            scratch_shapes=[
                pltpu.VMEM((owners * span, BS), F32),
                pltpu.VMEM((owners * span, BS), F32),
                pltpu.VMEM((own // group, 2 * height, 2 * group * BS), BF16),
                pltpu.VMEM((own // group, 2 * height, 2 * group * BS), BF16),
                pltpu.VMEM((tokens, 2 * BS), BF16),
                pltpu.VMEM((tokens, 2 * BS), BF16),
                pltpu.VMEM((tokens, 2 * BS), BF16),
                pltpu.VMEM((tokens, 2 * BS), BF16),
                pltpu.VMEM((8, 2 * BS), F32),
            ],
            compiler_params=params(60 if index < len(chunks) - 1 else 44),
            cost_estimate=cost(flops, 3 * count * owners * span * BS * 4, 4 * tokens * BS * count),
            name=f"mixer_{index}",
        )(
            fwd_high,
            fwd_low,
            inv_high,
            inv_low,
            *weights,
            x_spec.reshape(owners, count, span, BS),
            cot_spec.reshape(owners, blocks, span, BS),
        )

    mixed = [mix(i, exchange(piece)) for i, piece in enumerate(input_lon)]
    param_rows = 4 * BS + 8
    unit = 8 * owners // math.gcd(8 * owners, blocks)
    tail = -(blocks * param_rows) % (unit * blocks)
    flat = jnp.concatenate([m[1].reshape(-1, BS) for m in mixed], 0)
    flat = jnp.pad(flat, ((0, tail), (0, 0)))
    param_part = halve(flat, "row")

    grads = []
    sums = None
    for index, count in enumerate(chunks):
        start = starts[index]
        piece = mixed[index][0].reshape(owners, count, rows, padded, BS)
        carry_in = sums is not None
        if index == len(chunks) - 1 and carry_in:
            piece, param_part = lax.optimization_barrier((piece, param_part))
            param_part, sums = lax.optimization_barrier((param_part, sums))
        piece = exchange(piece)
        in_spec = pl.BlockSpec(
            (1, many, width, count * BS), lambda h, at=start // count: (0, h, 0, at)
        )
        grad, sums = pl.pallas_call(
            functools.partial(lon_back_kernel, start, carry_in),
            grid=(rows // many,),
            in_specs=[
                whole((width, tall)),
                spectrum_spec(many, count),
                in_spec,
                in_spec,
                stat_spec(many),
                whole((1, local)),
            ]
            + [stat_spec(many)] * carry_in,
            out_specs=[grad_spec(many, count), stat_spec(many)],
            out_shape=[
                jax.ShapeDtypeStruct((rows, width, count * BS), BF16),
                jax.ShapeDtypeStruct((rows, 2, width), F32),
            ],
            compiler_params=params(59 if carry_in else 60),
            cost_estimate=cost(
                2 * rows * tall * width * count * BS, rows * count * BS * (6 * width + 4 * tall)
            ),
            name=f"lon_back_{index}",
        )(back, piece, inputs, cotangent, stats, gain, *([sums] * carry_in))
        grads.append(grad)

    param_sums = param_part
    for i in reversed(range(low_bits("row"))):
        if i == 0:
            param_sums, sums = lax.optimization_barrier((param_sums, sums))
        param_sums = double(param_sums, "row", 1 << i)
    param_sums = param_sums[: blocks * param_rows].reshape(blocks, param_rows, BS)

    spec_scale = 1.0 / math.sqrt(batch * height * K)
    dw = param_sums[:, : 4 * BS].reshape(blocks, 2, 2, BS, BS).transpose(1, 2, 0, 3, 4) * spec_scale
    db = param_sums[:, 4 * BS : 4 * BS + 4].reshape(blocks, 2, 2, BS).transpose(1, 2, 0, 3)
    db = db * spec_scale
    ln_scale = 1.0 / math.sqrt(batch * height * width)
    gain_grad = param_sums[:, 4 * BS + 4].reshape(local) / ln_gain * ln_scale
    outputs = (
        dw[0].reshape(2, local, BS),
        db[0].reshape(2, local),
        dw[1].reshape(2, local, BS),
        db[1].reshape(2, local),
        gain_grad,
        param_sums[:, 4 * BS + 5].reshape(local),
    )
    first, second = pair_small(sums, "chan")
    second, outputs = lax.optimization_barrier((second, outputs))

    input_grad = pl.pallas_call(
        functools.partial(finish_kernel, chunks, total_chan),
        grid=(rows // many,),
        in_specs=[row_spec(many), stat_spec(many), stat_spec(many), stat_spec(many)]
        + [grad_spec(many, count) for count in chunks],
        out_specs=row_spec(many),
        out_shape=jax.ShapeDtypeStruct(inputs.shape, BF16),
        compiler_params=params(),
        cost_estimate=cost(10 * rows * width * local, rows * width * local * 10),
        name="finish",
    )(inputs, stats, first, second, *grads)
    return (input_grad, *outputs)


def solution(mesh):
    placed = (
        P(None, "row", None, "chan"),
        P(None, "row", None, "chan"),
        P("chan"),
        P("chan"),
        P(None, "chan", None),
        P(None, "chan"),
        P(None, "chan", None),
        P(None, "chan"),
    )
    return jax.shard_map(
        on_device,
        mesh=mesh,
        in_specs=placed,
        out_specs=(
            P(None, "row", None, "chan"),
            P(None, "chan", None),
            P(None, "chan"),
            P(None, "chan", None),
            P(None, "chan"),
            P("chan"),
            P("chan"),
        ),
        check_vma=False,
    )
```

```python
import functools
import math

import jax
import jax.numpy as jnp
import numpy as np
from jax import lax
from jax.experimental import pallas as pl
from jax.experimental.pallas import tpu as pltpu
from jax.sharding import PartitionSpec as P

K = 192
BS = 128
EPS = 1e-05
LAMBDA = 0.01
ROOT_TWO_PI = math.sqrt(2.0 / math.pi)
BF16 = jnp.bfloat16
F32 = jnp.float32


def gelu_parts(values):
    inner = ROOT_TWO_PI * (values + 0.044715 * values * values * values)
    tangent = jnp.tanh(inner)
    output = 0.5 * values * (1.0 + tangent)
    slope = 0.5 * (1.0 + tangent) + 0.5 * values * (1.0 - tangent * tangent) * ROOT_TWO_PI * (
        1.0 + 3.0 * 0.044715 * values * values
    )
    return (output, slope)


def shrink_slope(values):
    tangent = jnp.tanh(values / LAMBDA)
    return tangent * tangent


def high_low(table):
    high = np.asarray(table, np.float32).astype(jnp.bfloat16)
    low = (np.asarray(table, np.float32) - high.astype(np.float32)).astype(jnp.bfloat16)
    return high, low


def lon_table(width, owners, padded):
    own = K // owners
    number = np.arange(K)[:, None]
    column = np.arange(width)[None, :]
    phase = (number * column % width) * (2.0 * math.pi / width)
    parts = np.stack([np.cos(phase), -np.sin(phase)]) / math.sqrt(width)
    parts = parts.reshape(2, owners, own, width).transpose(1, 0, 2, 3)
    table = np.zeros((owners, padded, width))
    table[:, : 2 * own] = parts.reshape(owners, 2 * own, width)
    return table.reshape(owners * padded, width)


def kept_scale(owners, padded):
    own = K // owners
    scale = np.full((2, K), 2.0)
    scale[:, 0] = 1.0
    out = np.ones((owners, padded))
    out[:, : 2 * own] = scale.reshape(2, owners, own).transpose(1, 0, 2).reshape(owners, 2 * own)
    return out.reshape(owners * padded, 1)


def lat_table(length):
    first = np.arange(length)
    phase = (first[:, None] * first[None, :] % length) * (2.0 * math.pi / length)
    cosine = np.cos(phase) / math.sqrt(length)
    sine = np.sin(phase) / math.sqrt(length)
    return np.block([[cosine, sine], [-sine, cosine]])


def dot(left, right):
    return jnp.dot(left, right, preferred_element_type=F32)


def dot_rows(left, right):
    return lax.dot_general(left, right, (((0,), (0,)), ((), ())), preferred_element_type=F32)


def dot_cols(left, right):
    return lax.dot_general(left, right, (((1,), (1,)), ((), ())), preferred_element_type=F32)


def split(values):
    high = values.astype(BF16)
    return high, (values - high.astype(F32)).astype(BF16)


def columns_of(stats):
    count = stats.shape[0]
    high, rest = split(stats)
    mid, low = split(stats - high.astype(F32))
    stacked = jnp.concatenate([high.astype(F32), mid.astype(F32), low.astype(F32)], 0)
    pad = -stacked.shape[0] % 16
    if pad:
        stacked = jnp.concatenate([stacked, jnp.zeros((pad, stacked.shape[1]), F32)], 0)
    rows = stacked.shape[0]
    row = lax.broadcasted_iota(jnp.int32, (rows, count * 128), 0)
    lane = lax.broadcasted_iota(jnp.int32, (rows, count * 128), 1)
    pick = (row % count == lane // 128) & (row < 3 * count)
    wide = dot_rows(stacked.astype(BF16), pick.astype(F32).astype(BF16))
    return [wide[:, i * 128 : (i + 1) * 128] for i in range(count)]


def cot_lon_kernel(table_ref, cot_ref, out_ref):
    owners, blocks, rows, padded, _ = out_ref.shape
    for r in range(rows):
        result = dot(table_ref[...], cot_ref[0, r])
        for b in range(blocks):
            out_ref[:, b, r] = result[:, b * BS : (b + 1) * BS].reshape(owners, padded, BS)


def input_lon_kernel(table_ref, in_ref, stat_ref, gain_ref, *out_refs):
    tall = table_ref.shape[0] // 2
    for r in range(in_ref.shape[1]):
        mean, rstd = columns_of(stat_ref[r])
        at = 0
        for out_ref in out_refs:
            owners, blocks, _, padded, _ = out_ref.shape
            pieces = []
            for b in range(at, at + blocks):
                lanes = slice(b * BS, (b + 1) * BS)
                values = in_ref[0, r, :, lanes].astype(F32)
                pieces.append((values - mean) * rstd * gain_ref[:, lanes])
            at += blocks
            high, low = split(jnp.concatenate(pieces, 1))
            both = dot(table_ref[...], high)
            result = both[:tall] + both[tall:] + dot(table_ref[:tall], low)
            for b in range(blocks):
                out_ref[:, b, r] = result[:, b * BS : (b + 1) * BS].reshape(owners, padded, BS)


def mixer_kernel(
    own,
    group,
    fwd_high_ref,
    fwd_low_ref,
    inv_high_ref,
    inv_low_ref,
    w_one_ref,
    w_one_t_ref,
    w_two_ref,
    w_two_t_ref,
    bias_ref,
    shift_ref,
    x_ref,
    c_ref,
    grad_ref,
    sums_ref,
    x_scr,
    c_scr,
    high_scr,
    low_scr,
    spec_scr,
    hid_scr,
    two_scr,
    pre_scr,
    gain_scr,
):
    sources, _, span, _ = x_ref.shape
    length = fwd_high_ref.shape[0] // 2
    padded = sources * span // length
    steps = own // group
    for s in range(sources):
        x_scr[s * span : (s + 1) * span] = x_ref[s, 0]
        c_scr[s * span : (s + 1) * span] = c_ref[s, 0]
    for k in range(own):
        step, place = divmod(k, group)
        for which, scr in enumerate((x_scr, c_scr)):
            lanes = slice((which * group + place) * BS, (which * group + place + 1) * BS)
            for part in range(2):
                values = scr[pl.ds(part * own + k, length, stride=padded), :]
                rows = slice(part * length, (part + 1) * length)
                high, low = split(values)
                high_scr[step, rows, lanes] = high
                low_scr[step, rows, lanes] = low
    gain_scr[...] = jnp.zeros_like(gain_scr)
    w_one = w_one_ref[0]
    w_two = w_two_ref[0]
    first = lax.broadcasted_iota(jnp.int32, (group * length, 1), 0) == 0

    def gather(full, which):
        rows = []
        for place in range(group):
            at = (which * group + place) * BS
            re = full[:length, at : at + BS]
            im = full[length:, at : at + BS]
            rows.append(jnp.concatenate([re, im], 1))
        return jnp.concatenate(rows, 0)

    def body(step, carry):
        high = high_scr[step]
        low = low_scr[step]
        full = dot(fwd_high_ref[...], high) + dot(fwd_high_ref[...], low)
        full = full + dot(fwd_low_ref[...], high)
        plain = gather(full, 0)
        cot = gather(full, 1)
        at = pl.ds(pl.multiple_of(step * (group * length), group * length), group * length)
        is_first = jnp.where(first & (step == 0), 1.0, 0.0)
        spec = (plain + is_first * shift_ref[0, 0:1]).astype(BF16)
        pre_one = dot(spec, w_one) + bias_ref[0, 0:1]
        act, slope = gelu_parts(pre_one)
        hid = act.astype(BF16)
        pre_two = dot(hid, w_two) + bias_ref[0, 1:2]
        grad_two = (cot * shrink_slope(pre_two)).astype(BF16)
        grad_pre = (dot(grad_two, w_two_t_ref[0]) * slope).astype(BF16)
        grad_spec = dot(grad_pre, w_one_t_ref[0])
        spec_scr[at] = spec
        hid_scr[at] = hid
        two_scr[at] = grad_two
        pre_scr[at] = grad_pre
        gain_scr[0:1] += jnp.sum(grad_spec * plain, 0, keepdims=True)
        gain_scr[1:2] += jnp.sum(grad_two.astype(F32), 0, keepdims=True)
        gain_scr[2:3] += jnp.sum(grad_pre.astype(F32), 0, keepdims=True)
        gain_scr[3:4] += jnp.sum(grad_spec * is_first, 0, keepdims=True)
        for place in range(group):
            piece = grad_spec[place * length : (place + 1) * length]
            stacked = jnp.concatenate([piece[:, :BS], piece[:, BS:]], 0)
            grad_high, grad_low = split(stacked)
            high_scr[step, :, place * BS : (place + 1) * BS] = grad_high
            low_scr[step, :, place * BS : (place + 1) * BS] = grad_low
        return carry

    lax.fori_loop(0, steps, body, 0)
    for step in range(steps):
        high = high_scr[step, :, : group * BS]
        low = low_scr[step, :, : group * BS]
        lon = dot(inv_high_ref[...], high) + dot(inv_high_ref[...], low)
        lon = lon + dot(inv_low_ref[...], high)
        for place in range(group):
            k = step * group + place
            for part in range(2):
                piece = lon[part * length : (part + 1) * length, place * BS : (place + 1) * BS]
                x_scr[pl.ds(part * own + k, length, stride=padded), :] = piece
    for k in range(2 * own, padded):
        x_scr[pl.ds(k, length, stride=padded), :] = jnp.zeros((length, BS), F32)
    for s in range(sources):
        grad_ref[s, 0] = x_scr[s * span : (s + 1) * span]
    for i, (left, right) in enumerate(((spec_scr, pre_scr), (hid_scr, two_scr))):
        square = dot_rows(left[...], right[...])
        sums_ref[0, 2 * i * BS : (2 * i + 1) * BS] = square[:BS, :BS] + square[BS:, BS:]
        sums_ref[0, (2 * i + 1) * BS : (2 * i + 2) * BS] = square[:BS, BS:] - square[BS:, :BS]
    total = gain_scr[...]
    sums_ref[0, 4 * BS : 4 * BS + 8] = jnp.concatenate(
        [
            total[2:3, :BS],
            total[2:3, BS:],
            total[1:2, :BS],
            total[1:2, BS:],
            total[0:1, :BS] + total[0:1, BS:],
            total[3:4, :BS] * shift_ref[0, 1:2, :BS],
            jnp.zeros((2, BS), F32),
        ],
        0,
    )


def lon_back_kernel(
    offset, carry_in, table_ref, grad_ref, in_ref, cot_ref, stat_ref, gain_ref, *refs
):
    if carry_in:
        before_ref, out_ref, sums_ref = refs
    else:
        out_ref, sums_ref = refs
    sources, blocks, rows, padded, _ = grad_ref.shape
    ones = jnp.ones((16, BS), BF16)
    for r in range(rows):
        mean, rstd = columns_of(stat_ref[r])
        pieces = [
            grad_ref[:, b, r].reshape(sources * padded, BS).astype(BF16) for b in range(blocks)
        ]
        mixed = dot(table_ref[...], jnp.concatenate(pieces, 1))
        grads = jnp.zeros((in_ref.shape[2], BS), F32)
        products = jnp.zeros((in_ref.shape[2], BS), F32)
        for b in range(blocks):
            lanes = slice((offset + b) * BS, (offset + b + 1) * BS)
            grad = mixed[:, b * BS : (b + 1) * BS] * gain_ref[:, lanes]
            values = in_ref[0, r, :, b * BS : (b + 1) * BS].astype(F32)
            cot = cot_ref[0, r, :, b * BS : (b + 1) * BS].astype(F32)
            out_ref[r, :, b * BS : (b + 1) * BS] = (cot + rstd * grad).astype(BF16)
            grads = grads + grad
            products = products + grad * ((values - mean) * rstd)
        both = [dot_cols(ones, values.astype(BF16))[0:1] for values in (grads, products)]
        sums = jnp.concatenate(both, 0)
        if carry_in:
            sums = sums + before_ref[r]
        sums_ref[r] = sums


def finish_kernel(chunks, channels, *refs):
    in_ref, stat_ref, sums_ref, more_ref = refs[:4]
    base_refs = refs[4 : 4 + len(chunks)]
    out_ref = refs[-1]
    for r in range(in_ref.shape[1]):
        mean, rstd = stat_ref[r, 0:1], stat_ref[r, 1:2]
        sums = (sums_ref[r] + more_ref[r]) / channels
        slope = rstd * rstd * sums[1:2]
        level = rstd * sums[0:1] - mean * slope
        level, slope = columns_of(jnp.concatenate([level, slope], 0))
        at = 0
        for base_ref, blocks in zip(base_refs, chunks):
            for b in range(blocks):
                lanes = slice(at * BS, (at + 1) * BS)
                values = in_ref[0, r, :, lanes].astype(F32)
                base = base_ref[r, :, b * BS : (b + 1) * BS].astype(F32)
                out_ref[0, r, :, lanes] = (base - level - slope * values).astype(BF16)
                at += 1


def xor_permute(piece, axis, bit):
    size = lax.axis_size(axis)
    return lax.ppermute(piece, axis, [(i, i ^ bit) for i in range(size)])


def pair_small(piece, axis):
    other = jnp.zeros_like(piece)
    bit = 1
    while bit < lax.axis_size(axis):
        piece = piece + other if bit > 1 else piece
        other = xor_permute(piece, axis, bit)
        bit *= 2
    return piece, other


def low_bits(axis):
    return max(lax.axis_size(axis).bit_length() - 2, 0)


def halve(piece, axis):
    index = lax.axis_index(axis)
    for i in range(low_bits(axis)):
        half = piece.shape[0] // 2
        low, high = piece[:half], piece[half:]
        upper = (index & (1 << i)) != 0
        piece = jnp.where(upper, high, low) + xor_permute(
            jnp.where(upper, low, high), axis, 1 << i
        )
    if lax.axis_size(axis) > 1:
        piece = piece + xor_permute(piece, axis, 1 << low_bits(axis))
    return piece


def double(piece, axis, bit):
    other = xor_permute(piece, axis, bit)
    upper = (lax.axis_index(axis) & bit) != 0
    return jnp.concatenate([jnp.where(upper, other, piece), jnp.where(upper, piece, other)], 0)


def divisor(count, limit):
    return max(n for n in range(1, limit + 1) if count % n == 0)


def params(mib=60):
    return pltpu.CompilerParams(vmem_limit_bytes=mib * 1024 * 1024)


def whole(shape):
    return pl.BlockSpec(shape, lambda *_: (0,) * len(shape))


def cost(flops, moved, transcendentals=0):
    return pl.CostEstimate(
        flops=int(flops), bytes_accessed=int(moved), transcendentals=int(transcendentals)
    )


def on_device(
    inputs, cotangent, ln_gain, ln_shift, first_weight, first_bias, second_weight, second_bias
):
    batch, rows, width, local = inputs.shape
    blocks = local // BS
    owners = lax.axis_size("row")
    height = rows * owners
    own = K // owners
    padded = -(-2 * own // 8) * 8
    tall = owners * padded
    group = 2 if own % 2 == 0 else 1
    total_chan = local * lax.axis_size("chan")
    chunks = (blocks - 1, 1) if blocks > 1 else (1,)
    starts = [sum(chunks[:i]) for i in range(len(chunks))]
    gain = ln_gain.reshape(1, local)

    lon = lon_table(width, owners, padded)
    lon_high, lon_low = high_low(lon)
    lon_both = np.concatenate([lon_high, lon_low], 0)
    cot_high, _ = high_low(lon * kept_scale(owners, padded))
    back = np.ascontiguousarray(lon.T).astype(np.float32).astype(jnp.bfloat16)
    fwd_high, fwd_low = high_low(lat_table(height))
    inv_high, inv_low = high_low(lat_table(height).T)

    def exchange(piece):
        return lax.all_to_all(piece, "row", split_axis=0, concat_axis=0, tiled=True)

    few = divisor(rows, 2)
    many = divisor(rows, 4)
    most = divisor(rows, 6)

    def row_spec(step):
        return pl.BlockSpec((1, step, width, local), lambda h: (0, h, 0, 0))

    def stat_spec(step):
        return pl.BlockSpec((step, 2, width), lambda h: (h, 0, 0))

    def grad_spec(step, count):
        return pl.BlockSpec((step, width, count * BS), lambda h: (h, 0, 0))

    def spectrum_spec(step, count):
        return pl.BlockSpec((owners, count, step, padded, BS), lambda h: (0, 0, h, 0, 0))

    def spectrum_shape(count):
        return jax.ShapeDtypeStruct((owners, count, rows, padded, BS), F32)

    lon_flops = 2 * rows * tall * width * local
    cot_lon = pl.pallas_call(
        cot_lon_kernel,
        grid=(rows // most,),
        in_specs=[whole((tall, width)), row_spec(most)],
        out_specs=spectrum_spec(most, blocks),
        out_shape=spectrum_shape(blocks),
        compiler_params=params(),
        cost_estimate=cost(lon_flops, rows * local * (2 * width + 4 * tall)),
        name="cot_lon",
    )(cot_high, cotangent)
    cot_lon, inputs = lax.optimization_barrier((cot_lon, inputs))
    cot_spec = exchange(cot_lon)

    values = inputs.astype(F32)
    mean = lax.psum(jnp.sum(values, -1), "chan") / total_chan
    centred = values - mean[..., None]
    variance = lax.psum(jnp.sum(centred * centred, -1), "chan") / total_chan
    stats = jnp.stack([mean[0], lax.rsqrt(variance + EPS)[0]], 1)

    input_lon = pl.pallas_call(
        input_lon_kernel,
        grid=(rows // few,),
        in_specs=[whole((2 * tall, width)), row_spec(few), stat_spec(few), whole((1, local))],
        out_specs=[spectrum_spec(few, count) for count in chunks],
        out_shape=[spectrum_shape(count) for count in chunks],
        compiler_params=params(),
        cost_estimate=cost(3 * lon_flops, rows * local * (2 * width + 4 * tall)),
        name="input_lon",
    )(lon_both, inputs, stats, gain)

    def square(weight):
        re, im = weight.reshape(2, blocks, BS, BS)
        return jnp.concatenate(
            [jnp.concatenate([re, im], 2), jnp.concatenate([-im, re], 2)], 1
        )

    w_one = square(first_weight)
    w_two = square(second_weight)
    w_one_t = w_one.swapaxes(1, 2)
    w_two_t = w_two.swapaxes(1, 2)
    bias = jnp.stack([first_bias, second_bias]).reshape(2, 2, blocks, BS)
    bias = bias.transpose(2, 0, 1, 3).reshape(blocks, 2, 2 * BS)
    is_origin = (lax.axis_index("row") == 0).astype(F32)
    shift = (ln_shift * (math.sqrt(height * width) * is_origin)).reshape(blocks, 1, BS)
    shift = jnp.concatenate([shift, jnp.zeros_like(shift)], 2)
    shift = jnp.concatenate([shift, jnp.full_like(shift, is_origin)], 1)

    weights = (w_one, w_one_t, w_two, w_two_t, bias, shift)
    first_piece, cot_spec, weights = lax.optimization_barrier((input_lon[0], cot_spec, weights))
    input_lon = [first_piece, *input_lon[1:]]

    span = rows * padded

    def mix(index, x_spec):
        count = chunks[index]
        start = starts[index]

        def at(shape):
            return pl.BlockSpec(shape, lambda b: (b + start,) + (0,) * (len(shape) - 1))

        tokens = own * height
        flops = 2 * count * tokens * 2 * BS * (3 * 2 * height * 3 + 6 * 2 * BS)
        return pl.pallas_call(
            functools.partial(mixer_kernel, own, group),
            grid=(count,),
            in_specs=[whole((2 * height, 2 * height))] * 4
            + [at((1, 2 * BS, 2 * BS))] * 4
            + [
                at((1, 2, 2 * BS)),
                at((1, 2, 2 * BS)),
                pl.BlockSpec((owners, 1, span, BS), lambda b: (0, b, 0, 0)),
                pl.BlockSpec((owners, 1, span, BS), lambda b: (0, b + start, 0, 0)),
            ],
            out_specs=[
                pl.BlockSpec((owners, 1, span, BS), lambda b: (0, b, 0, 0)),
                pl.BlockSpec((1, 4 * BS + 8, BS), lambda b: (b, 0, 0)),
            ],
            out_shape=[
                jax.ShapeDtypeStruct((owners, count, span, BS), F32),
                jax.ShapeDtypeStruct((count, 4 * BS + 8, BS), F32),
            ],
            scratch_shapes=[
                pltpu.VMEM((owners * span, BS), F32),
                pltpu.VMEM((owners * span, BS), F32),
                pltpu.VMEM((own // group, 2 * height, 2 * group * BS), BF16),
                pltpu.VMEM((own // group, 2 * height, 2 * group * BS), BF16),
                pltpu.VMEM((tokens, 2 * BS), BF16),
                pltpu.VMEM((tokens, 2 * BS), BF16),
                pltpu.VMEM((tokens, 2 * BS), BF16),
                pltpu.VMEM((tokens, 2 * BS), BF16),
                pltpu.VMEM((8, 2 * BS), F32),
            ],
            compiler_params=params(60 if index < len(chunks) - 1 else 44),
            cost_estimate=cost(flops, 3 * count * owners * span * BS * 4, 4 * tokens * BS * count),
            name=f"mixer_{index}",
        )(
            fwd_high,
            fwd_low,
            inv_high,
            inv_low,
            *weights,
            x_spec.reshape(owners, count, span, BS),
            cot_spec.reshape(owners, blocks, span, BS),
        )

    mixed = [mix(i, exchange(piece)) for i, piece in enumerate(input_lon)]
    param_rows = 4 * BS + 8
    unit = 8 * owners // math.gcd(8 * owners, blocks)
    tail = -(blocks * param_rows) % (unit * blocks)
    flat = jnp.concatenate([m[1].reshape(-1, BS) for m in mixed], 0)
    flat = jnp.pad(flat, ((0, tail), (0, 0)))
    param_part = halve(flat, "row")

    grads = []
    sums = None
    for index, count in enumerate(chunks):
        start = starts[index]
        piece = mixed[index][0].reshape(owners, count, rows, padded, BS)
        carry_in = sums is not None
        if index == len(chunks) - 1 and carry_in:
            piece, param_part = lax.optimization_barrier((piece, param_part))
            param_part, sums = lax.optimization_barrier((param_part, sums))
        piece = exchange(piece)
        in_spec = pl.BlockSpec(
            (1, many, width, count * BS), lambda h, at=start // count: (0, h, 0, at)
        )
        grad, sums = pl.pallas_call(
            functools.partial(lon_back_kernel, start, carry_in),
            grid=(rows // many,),
            in_specs=[
                whole((width, tall)),
                spectrum_spec(many, count),
                in_spec,
                in_spec,
                stat_spec(many),
                whole((1, local)),
            ]
            + [stat_spec(many)] * carry_in,
            out_specs=[grad_spec(many, count), stat_spec(many)],
            out_shape=[
                jax.ShapeDtypeStruct((rows, width, count * BS), BF16),
                jax.ShapeDtypeStruct((rows, 2, width), F32),
            ],
            compiler_params=params(44 if carry_in else 60),
            cost_estimate=cost(
                2 * rows * tall * width * count * BS, rows * count * BS * (6 * width + 4 * tall)
            ),
            name=f"lon_back_{index}",
        )(back, piece, inputs, cotangent, stats, gain, *([sums] * carry_in))
        grads.append(grad)

    param_sums = param_part
    for i in reversed(range(low_bits("row"))):
        if i == 0:
            param_sums, sums = lax.optimization_barrier((param_sums, sums))
        param_sums = double(param_sums, "row", 1 << i)
    param_sums = param_sums[: blocks * param_rows].reshape(blocks, param_rows, BS)

    spec_scale = 1.0 / math.sqrt(batch * height * K)
    dw = param_sums[:, : 4 * BS].reshape(blocks, 2, 2, BS, BS).transpose(1, 2, 0, 3, 4) * spec_scale
    db = param_sums[:, 4 * BS : 4 * BS + 4].reshape(blocks, 2, 2, BS).transpose(1, 2, 0, 3)
    db = db * spec_scale
    ln_scale = 1.0 / math.sqrt(batch * height * width)
    gain_grad = param_sums[:, 4 * BS + 4].reshape(local) / ln_gain * ln_scale
    outputs = (
        dw[0].reshape(2, local, BS),
        db[0].reshape(2, local),
        dw[1].reshape(2, local, BS),
        db[1].reshape(2, local),
        gain_grad,
        param_sums[:, 4 * BS + 5].reshape(local),
    )
    first, second = pair_small(sums, "chan")
    second, outputs = lax.optimization_barrier((second, outputs))

    input_grad = pl.pallas_call(
        functools.partial(finish_kernel, chunks, total_chan),
        grid=(rows // many,),
        in_specs=[row_spec(many), stat_spec(many), stat_spec(many), stat_spec(many)]
        + [grad_spec(many, count) for count in chunks],
        out_specs=row_spec(many),
        out_shape=jax.ShapeDtypeStruct(inputs.shape, BF16),
        compiler_params=params(),
        cost_estimate=cost(10 * rows * width * local, rows * width * local * 10),
        name="finish",
    )(inputs, stats, first, second, *grads)
    return (input_grad, *outputs)


def solution(mesh):
    placed = (
        P(None, "row", None, "chan"),
        P(None, "row", None, "chan"),
        P("chan"),
        P("chan"),
        P(None, "chan", None),
        P(None, "chan"),
        P(None, "chan", None),
        P(None, "chan"),
    )
    return jax.shard_map(
        on_device,
        mesh=mesh,
        in_specs=placed,
        out_specs=(
            P(None, "row", None, "chan"),
            P(None, "chan", None),
            P(None, "chan"),
            P(None, "chan", None),
            P(None, "chan"),
            P("chan"),
            P("chan"),
        ),
        check_vma=False,
    )
```
